128 devices in a mesh: wav: 8 (over x, core), slab: 16 (over y, z).
Axes of the slice: x: 4, y: 4, z: 4, core: 2. Of those that a mesh axis runs over, the one named last changes fastest.
Arguments:
- amplitude: float32 [512, 512], P('slab'), may hold values from 0.5 to 1
- seg_map: int32 [512, 512], P('slab'), may hold values from 0 to 797, as said below
- seg_table: int32 [798, 3], replicated, may hold values from -3000 to 3000
- focal_mask: float32 [1024, 1024], P('slab'), may hold values from 0.1 to 1
- trace_row: int32 [128, 128], P('slab', 'wav'), may hold values from 0 to 31
- trace_col: int32 [128, 128], P('slab', 'wav'), may hold values from 0 to 31
- block_count: int32 [128, 128], P('slab', 'wav'), may hold values from 1 to 16
- crosstalk: float32 [5, 5], replicated, may hold values from 0.01 to 0.1
Outputs:
- detector: float32 [4096, 4096], P('slab', 'wav')
The draws below stay inside these ranges and needn't reach their ends.
Inputs may be any that keep to these rules, and one draw needn't show every extreme that they name: seg_map is constant over aligned square blocks of 16 samples.
All inputs are finite; a program needn't handle non-finite values.
Results may differ from the reference program's by a relative error of at most 0.0001.
Values sent between devices are 32-bit elements; how exact they have to be, the bound alone decides.
No kernel may reach another device: no remote copies, remote signals or barrier semaphores. Data moves between devices by JAX's collectives and lax.ppermute only.
A program may use at most 128 MiB of HBM per device.

```python
import math
import jax
import jax.numpy as jnp
from jax import lax

NP = 512
NF = 1024
NL = 128
DPIX = 32
SEGMENTS = 798
WAV_ALL = 16


def draw_seg_map(key, part):
    key = jax.random.fold_in(key, 11)
    blocks = jax.random.randint(key, (32, 32), 0, SEGMENTS, dtype=jnp.int32)
    block_side = NP // 32
    return jnp.repeat(jnp.repeat(blocks, block_side, axis=0), block_side, axis=1)


def draw_block_count(key, part):
    key = jax.random.fold_in(key, 23)
    counts = jax.random.randint(key, (NL, NL), 1, WAV_ALL + 1, dtype=jnp.int32)
    return counts.at[0, 0].set(WAV_ALL).at[0, 1].set(1)


def with_ends(values, key, least, high):
    extent = values.shape
    spot = [jax.random.randint(jax.random.fold_in(key, axis), (), 0, extent[axis]) for axis in range(len(extent))]
    values = values.at[tuple(spot)].set(least)
    longest = extent.index(max(extent))
    spot[longest] = (spot[longest] + 1) % extent[longest]
    return values.at[tuple(spot)].set(high)


def level_of(rng, shape, pieces, least, high):
    loudness, own = 1.0, jax.random.fold_in(rng, 6)
    for dim, shards_of in pieces:
        draws = jnp.exp(jax.random.uniform(jax.random.fold_in(own, dim), (shards_of,), jnp.float32, least / len(pieces), high / len(pieces)))
        loudness = loudness * jnp.repeat(draws, shape[dim] // shards_of).reshape([-1 if axis == dim else 1 for axis in range(len(shape))])
    return loudness


def setup_inputs(seed: int = 0) -> dict:
    streams_of = jax.random.split(jax.random.key(seed), 9)
    amplitude = jnp.clip(0.5 + 0.5 * jax.random.uniform(streams_of[0], (NP, NP), jnp.float32) ** level_of(streams_of[0], (NP, NP), ((0, 16),), -0.2, 0.2), 0.5, 1.0)
    seg_map = draw_seg_map(jax.random.fold_in(streams_of[8], 71), 0)
    seg_table = with_ends(jax.random.randint(streams_of[2], (SEGMENTS, 3), -3000, 3001), jax.random.fold_in(streams_of[2], 1), -3000, 3000).astype(jnp.int32)
    focal_mask = jnp.clip(jnp.exp(math.log(1.0) - 2.3025851 * jax.random.uniform(streams_of[3], (NF, NF), jnp.float32) ** level_of(streams_of[3], (NF, NF), ((0, 16),), -0.2, 0.2)), 0.1, 1.0)
    trace_row = with_ends(jax.random.randint(streams_of[4], (NL, NL), 0, DPIX), jax.random.fold_in(streams_of[4], 1), 0, DPIX - 1).astype(jnp.int32)
    trace_col = with_ends(jax.random.randint(streams_of[5], (NL, NL), 0, DPIX), jax.random.fold_in(streams_of[5], 1), 0, DPIX - 1).astype(jnp.int32)
    block_count = draw_block_count(jax.random.fold_in(streams_of[8], 71), 0)
    crosstalk = jnp.clip(jax.random.uniform(streams_of[7], (5, 5), jnp.float32, 0.01, 0.1), 0.01, 0.1)
    return dict(amplitude=amplitude, seg_map=seg_map, seg_table=seg_table, focal_mask=focal_mask, trace_row=trace_row, trace_col=trace_col, block_count=block_count, crosstalk=crosstalk)


LAMBDA_START = 1000.0
LAMBDA_STEP = 1.0

def product(left, right):
    return jnp.dot(left, right, precision=lax.Precision.HIGHEST, preferred_element_type=jnp.float32)

def wavelength_of(index):
    return LAMBDA_START + LAMBDA_STEP * jnp.asarray(index).astype(jnp.float32)

def transform_table(out_index, in_index, wavelength, count_in, count_out):
    factor = (2 * out_index + 1 - count_out)[:, None] * (2 * in_index + 1 - count_in)[None, :]
    coefficient = 2.0 * jnp.pi * LAMBDA_START / 4.0 / (wavelength * count_out)
    angle = factor.astype(jnp.float32) * coefficient
    scaling = 1.0 / jnp.sqrt(jnp.asarray(count_in).astype(jnp.float32))
    return (scaling * jnp.cos(angle), -scaling * jnp.sin(angle))

def path_difference(seg_map, seg_table, row_index, col_index, count_in):
    piston = jnp.take(seg_table[:, 0], seg_map).astype(jnp.float32)
    tipping = jnp.take(seg_table[:, 1], seg_map).astype(jnp.float32)
    tilting = jnp.take(seg_table[:, 2], seg_map).astype(jnp.float32)
    across = (2 * col_index + 1 - count_in).astype(jnp.float32) / (2.0 * count_in)
    down = (2 * row_index + 1 - count_in).astype(jnp.float32) / (2.0 * count_in)
    return piston + tipping * across[None, :] + tilting * down[:, None]

def focal_transmission(mask, row_index, col_index, count_out):
    down = (2 * row_index + 1 - count_out).astype(jnp.float32) / 2.0
    across = (2 * col_index + 1 - count_out).astype(jnp.float32) / 2.0
    radius_sq = down[:, None] * down[:, None] + across[None, :] * across[None, :]
    width = count_out / 32.0
    return mask * (1.0 - jnp.exp(-radius_sq / (width * width)))

def pupil_field(amplitude, path, wavelength):
    phase = 2.0 * jnp.pi * path / wavelength
    return (amplitude * jnp.cos(phase), amplitude * jnp.sin(phase))

def lenslet_means(power, lens_pixels):
    rows_count = power.shape[0] // lens_pixels
    cols_count = power.shape[1] // lens_pixels
    return power.reshape(rows_count, lens_pixels, cols_count, lens_pixels).mean(axis=(1, 3))

def deposit(spectra, trace_row, trace_col, block_count, pixels):
    count_wave = spectra.shape[0]
    rows_count = trace_row.shape[0]
    cols_count = trace_row.shape[1]
    waves = jnp.arange(count_wave, dtype=jnp.int32)
    live = (waves[:, None, None] < block_count[None, :, :]).astype(jnp.float32)
    places = jnp.arange(pixels, dtype=jnp.int32)
    offset = places[None, None, None, :] - trace_col[None, :, :, None] - waves[:, None, None, None]
    along = jnp.exp(-jnp.abs(offset).astype(jnp.float32) / 2.0)
    spread = lax.optimization_barrier(jnp.sum((spectra * live)[:, :, :, None] * along, axis=0))
    across = jnp.exp(-jnp.abs(places[None, None, :] - trace_row[:, :, None]).astype(jnp.float32) / 4.0)
    stamp = across[:, :, :, None] * spread[:, :, None, :]
    return stamp.transpose(0, 2, 1, 3).reshape(rows_count * pixels, cols_count * pixels)

def apply_crosstalk(padded, kernel, rows_count, cols_count):
    result = padded[2:2 + rows_count, 2:2 + cols_count]
    for lag_row in range(5):
        for lag_col in range(5):
            result = result + kernel[lag_row, lag_col] * padded[lag_row:lag_row + rows_count, lag_col:lag_col + cols_count]
    return result

def reference(amplitude, seg_map, seg_table, focal_mask, trace_row, trace_col, block_count, crosstalk):
    pupil_index = jnp.arange(NP, dtype=jnp.int32)
    focal_index = jnp.arange(NF, dtype=jnp.int32)
    path = path_difference(seg_map, seg_table, pupil_index, pupil_index, NP)
    transmit = focal_transmission(focal_mask, focal_index, focal_index, NF)
    collected = []
    for member in range(WAV_ALL):
        wavelength = wavelength_of(member)
        field_re, field_im = pupil_field(amplitude, path, wavelength)
        table_re, table_im = transform_table(focal_index, pupil_index, wavelength, NP, NF)
        half_re = product(field_re, table_re.T) - product(field_im, table_im.T)
        half_im = product(field_re, table_im.T) + product(field_im, table_re.T)
        focal_re = product(table_re, half_re) - product(table_im, half_im)
        focal_im = product(table_re, half_im) + product(table_im, half_re)
        power = transmit * transmit * (focal_re * focal_re + focal_im * focal_im)
        collected.append(lenslet_means(power, NF // NL))
    spectra = jnp.stack(collected)
    raw = deposit(spectra, trace_row, trace_col, block_count, DPIX)
    padded = jnp.pad(raw, 2)
    return apply_crosstalk(padded, crosstalk, raw.shape[0], raw.shape[1])
```

```python
import functools

import jax
import jax.numpy as jnp
import numpy as np
from jax import lax
from jax.experimental import pallas as pl
from jax.experimental.pallas import tpu as pltpu
from jax.sharding import PartitionSpec as P

F32, BF16, I32 = jnp.float32, jnp.bfloat16, jnp.int32

NP, NF, NL, DPIX, SEGMENTS, WAVES = 512, 1024, 128, 32, 798, 16
NWAV, NSLAB = 8, 16
ROWS = NP // NSLAB
FROWS = NF // NSLAB
UROWS = FROWS + 16
GROUP = 128
MROWS = GROUP + 8
HALF, FHALF = NP // 2, NF // 2

SIN = (6.283185302511503, -41.34170040531721, 81.6051313857832, -76.70301535364747,
       42.02592698447418, -14.899846663536497, 3.2381375046186873)
COS = (0.9999999890590228, -19.73920449945383, 64.93911745989081, -85.45013953079767,
       60.167630950263465, -25.967599245923743, 6.52865815775625)


def scalars():
    wavelength = 1000.0 + np.arange(WAVES, dtype=np.float64)
    whole = 250.0 / wavelength
    short = np.round(whole * 2.0**14) / 2.0**14
    return np.stack([short, whole - short, whole / 1024.0, 1.0 / wavelength], 1).astype(np.float32).reshape(-1)


def iota(shape, dim):
    return lax.broadcasted_iota(I32, shape, dim)


def dot(a, b):
    return jnp.dot(a, b, preferred_element_type=F32)


def split2(x):
    high = x.astype(BF16)
    return high, (x - high.astype(F32)).astype(BF16)


def split3(x):
    high = x.astype(BF16)
    rest = x - high.astype(F32)
    middle = rest.astype(BF16)
    return high, middle, (rest - middle.astype(F32)).astype(BF16)


def sincos(turns):
    t = turns - jnp.round(turns)
    z = t * t
    s, c = SIN[-1], COS[-1]
    for a, b in zip(SIN[-2::-1], COS[-2::-1]):
        s, c = s * z + a, c * z + b
    return s * t, c


def reversal(n):
    return (iota((n, n), 0) + iota((n, n), 1) == n - 1).astype(BF16)


def prepare_kernel(info, amp, seg, tab, out):
    lower = info[2] >= 2
    rows, cols = iota((ROWS, ROWS), 0), iota((ROWS, ROWS), 1)
    order = (cols == jnp.where(lower, ROWS - 1 - rows, rows)).astype(BF16)
    rev = reversal(HALF)
    left = right = 0.0
    for part in split3(amp[...]):
        left = left + dot(order, part[:, :HALF])
        right = right + dot(order, dot(part[:, HALF:], rev).astype(BF16))
    out[0:ROWS, 0:HALF] = left
    out[0:ROWS, HALF:NP] = right
    lane = iota((NP, 128), 1)
    pick = ((iota((NP, 128), 0) == 16 * (lane & 31)) & (lane < 96)).astype(BF16)

    def ids(first):
        return sum(dot(part, pick) for part in split2(seg[first:first + 8, :].astype(F32)))[0:1]

    upper_ids, lower_ids = ids(0), ids(16)
    lane = iota((SEGMENTS, 128), 1)
    table = tab[...].astype(F32)
    wide = jnp.where(lane < 32, table[:, 0:1], jnp.where(lane < 64, table[:, 1:2], table[:, 2:3]))
    which = iota((SEGMENTS, 128), 0).astype(F32)
    out[ROWS:ROWS + 8, :] = jnp.zeros((8, NP), F32)
    for k in range(2):
        own = jnp.where(lower, lower_ids if k == 0 else upper_ids, upper_ids if k == 0 else lower_ids)
        out[ROWS + k:ROWS + k + 1, 0:128] = jnp.sum(jnp.where(which == own, wide, 0.0), axis=0, keepdims=True)


def merge_kernel(info, p0, p1, p2, p3, out):
    z = info[3]
    out[:, GROUP:MROWS, :] = jnp.zeros((4, 8, 128), F32)
    for k, piece in enumerate((p0, p1, p2, p3)):
        source = lax.rem(z - k + 4, 4)
        place = jnp.where(info[2] >= 2, 3 - source, source)
        for at in range(4):

            @pl.when(place == at)
            def _(at=at, piece=piece):
                for t in range(4):
                    lanes = slice(128 * t, 128 * t + 128)
                    for b in range(2):
                        out[t, pl.ds(2 * at + b, 16, stride=8), :] = piece[16 * b:16 * b + 16, lanes]
                out[0, GROUP + 2 * at:GROUP + 2 * at + 2, :] = piece[ROWS:ROWS + 2, 0:128]


def angle(m, n, finfo, w):
    product = m * n
    a, b = (product >> 10).astype(F32), (product & 1023).astype(F32)
    t = a * finfo[4 * w]
    t = t - jnp.round(t)
    return sincos(t + a * finfo[4 * w + 1] + b * finfo[4 * w + 2])


def table_kernel(info, finfo, mask, above, below, utab, vtab, weight, smat):
    s, sign, g0 = info[1], info[4].astype(F32), info[5]
    for m in range(2):
        w = 2 * info[0] + m
        for p in range(2):
            g = g0 if p == 0 else 1 - g0
            u = 64 * s - 8 + iota((UROWS, GROUP), 0)
            rho = iota((UROWS, GROUP), 1)
            i = 128 * g + 16 * (rho & 7) + (rho >> 3)
            sin, cos = angle(2 * u + 1 - NF, 2 * i + 1 - NP, finfo, w)
            for at, part in ((0, cos), (GROUP, sin * sign)):
                high, low = split2(part)
                utab[p, m, 0:UROWS, at:at + GROUP] = high
                utab[p, m, UROWS:2 * UROWS, at:at + GROUP] = low

        def chunk(c, carry, m=m, w=w):
            j0 = pl.multiple_of(16 * c, 16)
            j = j0 + iota((16, FHALF), 0)
            v = iota((16, FHALF), 1)
            sin, cos = angle(2 * v + 1 - NF, 2 * j + 1 - NP, finfo, w)
            for q, part in ((0, cos), (1, sin)):
                high, low = split2(part)
                vtab[m, q, 0, pl.ds(j0, 16), :] = high
                vtab[m, q, 1, pl.ds(j0, 16), :] = low
            return carry

        lax.fori_loop(0, HALF // 16, chunk, 0)
    u = 64 * s - 8 + iota((UROWS, FHALF), 0)
    v = iota((UROWS, FHALF), 1)
    down, across = (2 * u + 1 - NF).astype(F32) * 0.5, (2 * v + 1 - NF).astype(F32) * 0.5
    fade = 1.0 - jnp.exp((down * down + across * across) * (-1.0 / 1024.0))
    rev = reversal(256)
    full = jnp.concatenate([above[0:8, :], mask[...], below[0:8, :]], axis=0)
    t = full[:, :FHALF] * fade
    weight[:, :FHALF] = t * t * 2.0**-24
    for q in range(2):
        flipped = sum(dot(part, rev) for part in split3(full[:, NF - 256 * (q + 1):NF - 256 * q]))
        t = flipped * fade[:, 256 * q:256 * (q + 1)]
        weight[:, FHALF + 256 * q:FHALF + 256 * (q + 1)] = t * t * 2.0**-24
    row, lane = iota((FHALF, 256), 0), iota((FHALF, 256), 1)
    lens = jnp.where((lane & 31) < 18, 16 * (lane >> 5) - 1 + (lane & 31), -1)
    smat[0:FHALF, :] = (lens == row >> 3).astype(BF16)
    smat[FHALF:NF, :] = (lens == NL - 1 - (row >> 3)).astype(BF16)


def pair_fields(info, finfo, first, second, utab, p, whi, wlo):
    sign = info[4].astype(F32)
    g = info[5] if p == 0 else 1 - info[5]
    coef = jnp.concatenate([first[0, GROUP:MROWS, :], second[0, GROUP:MROWS, :]], axis=0)
    high, low = split2(coef)
    coef = jnp.concatenate([high, low], axis=0)
    row, lane = iota((128, HALF), 0), iota((128, HALF), 1)
    place = iota((16, HALF), 0)
    y = (32 * (8 * g + (place & 7)) + 1 - NP).astype(F32) * (1.0 / 1024.0)
    toward = jnp.where(place < 8, sign, -sign)
    x = (2 * iota((16, HALF), 1) + 1 - NP).astype(F32) * (1.0 / 1024.0)
    paths, steps = [], []
    for side in range(2):
        block = lane >> 4 if side == 0 else 31 - (lane >> 4)
        pqr = []
        for c in range(3):
            both = dot(coef, (row == 32 * c + block).astype(BF16))
            pqr.append(both[0:16] + both[16:32])
        slope = toward * pqr[2]
        paths.append(pqr[0] + (x if side == 0 else -x) * pqr[1] + slope * y)
        steps.append(slope * (1.0 / 512.0))
    fields = []
    for m in range(2):
        inverse = finfo[4 * (2 * info[0] + m) + 3]
        start = [sincos(path * inverse) for path in paths]
        turn = [sincos(step * inverse) for step in steps]
        for lt in range(2):
            at = slice(128 * lt, 128 * lt + 128)

            def four(values, n):
                return [values[side][n][8 * t:8 * t + 8, at] for t in range(2) for side in range(2)]

            step_im, step_re = four(turn, 0), four(turn, 1)

            def rows(r2, carry, lt=lt, step_im=step_im, step_re=step_re):
                re, im = carry
                found = [[] for _ in range(8)]
                for h in range(2):
                    r0 = pl.multiple_of(16 * r2 + 8 * h, 8)
                    qre, qim = [], []
                    for t, ref in enumerate((first, second)):
                        for side in range(2):
                            a = ref[2 * side + lt, pl.ds(r0, 8), :]
                            qre.append(a * re[2 * t + side])
                            qim.append(a * im[2 * t + side])
                    (fl, fr, sl, sr), (gl, gr, hl, hr) = qre, qim
                    a, b, c, d = fl + sl, sl - fl, fr + sr, sr - fr
                    e, f, k, n = gl + hl, gl - hl, gr + hr, gr - hr
                    for q, value in enumerate((a + c, e + k, e - k, c - a, f + n, b + d, b - d, n - f)):
                        found[q].append(value)
                    re, im = (
                        [x * p - y * q for x, y, p, q in zip(re, im, step_re, step_im)],
                        [x * q + y * p for x, y, p, q in zip(re, im, step_re, step_im)],
                    )
                for q, values in enumerate(found):
                    high, low = split2(jnp.concatenate(values, axis=0))
                    r0 = pl.multiple_of(16 * r2 + (GROUP if q >= 4 else 0), 16)
                    c0 = HALF * (q & 3) + 128 * lt
                    whi[pl.ds(r0, 16), c0:c0 + 128] = high
                    wlo[pl.ds(r0, 16), c0:c0 + 128] = low
                return re, im

            lax.fori_loop(0, 8, rows, (four(start, 1), four(start, 0)))
        table = utab[p, m]
        both = dot(table, whi[...])
        fields.append(both[:UROWS] + both[UROWS:] + dot(table[:UROWS], wlo[...]))
    return fields


def first_kernel(info, finfo, first, second, utab, out, whi, wlo):
    for m, field in enumerate(pair_fields(info, finfo, first, second, utab, 0, whi, wlo)):
        out[m] = field


def second_kernel(info, finfo, first, second, utab, before, vtab, weight, smat, trow, tcol, count, above, below, out, whi, wlo):
    fields = pair_fields(info, finfo, first, second, utab, 1, whi, wlo)
    out[...] = jnp.zeros(out.shape, F32)
    for m, field in enumerate(fields):
        field = field + before[m]
        terms = []
        for q in range(2):
            side = jnp.concatenate([field[:, 512 * q:512 * q + 256], field[:, 512 * q + 256:512 * q + 512]], axis=0)
            high, low = split2(side)
            both = dot(jnp.concatenate([high, low], axis=0), vtab[m, q, 0])
            terms.append(both[:2 * UROWS] + both[2 * UROWS:] + dot(high, vtab[m, q, 1]))
        lens = 0.0
        for q, value in enumerate((terms[0] + terms[1], terms[0] - terms[1])):
            re, im = value[:UROWS], value[UROWS:]
            power = (re * re + im * im) * weight[:, FHALF * q:FHALF * (q + 1)]
            summed = jnp.sum(power.reshape(UROWS // 8, 8, FHALF), axis=1)
            for part in split3(summed):
                lens = lens + dot(part, smat[FHALF * q:FHALF * (q + 1), :])
        for d in range(NWAV):
            out[d, 10 * m:10 * m + 10, 0:32] = lens[:, 32 * d:32 * d + 32]
    for c, table in enumerate((trow, tcol, count)):
        own = table[...].astype(F32)
        for d in range(NWAV):
            out[d, 0:8, 32 + 16 * c:48 + 16 * c] = own
    for d in range(NWAV):
        out[d, 8:9, 32:80] = above[8:9, 0:48]
        out[d, 9:10, 32:80] = below[8:9, 0:48]


TILES = 4 * 8 + 2


def order(a):
    return a - 1 if 0 < a < 9 else 8 + a // 9


def detector_kernel(info, kernel, arrived, out, spec, trace, sums, aq, bq, hp):
    w = info[0]
    lane = iota((24, 128), 1)
    prev, own, nxt = arrived[jnp.maximum(w - 1, 0)], arrived[w], arrived[jnp.minimum(w + 1, NWAV - 1)]
    spot = (iota((128, 640), 0) == iota((128, 640), 1) >> 5).astype(BF16)
    rows = arrived[...].reshape(NWAV * 24, 128)
    wide = sum(dot(part, spot) for part in split3(rows))
    for t in range(5):
        spec[t] = wide[:, 128 * t:128 * t + 128]
    tables = []
    for c in range(3):
        tables.append(
            jnp.where(
                lane == 0,
                pltpu.roll(prev, 128 - (47 + 16 * c), 1),
                jnp.where(
                    lane < 17,
                    pltpu.roll(own, 128 - (31 + 16 * c), 1),
                    jnp.where(lane == 17, pltpu.roll(nxt, 128 - (15 + 16 * c), 1), 0.0),
                ),
            )
        )
    trace[...] = dot(jnp.concatenate(tables, axis=0).astype(BF16), spot)
    place = (iota((8, 640), 1) & 31).astype(F32)
    wave = 2.0 * iota((8, 640), 0).astype(F32)
    sums[...] = jnp.zeros(sums.shape, F32)
    for a in range(10):
        at = order(a)
        offset = place - trace[24 + at:25 + at, :]
        count = trace[48 + at:49 + at, :]
        spread = 0.0
        for m in range(2):
            value = jnp.concatenate([spec[t, pl.ds(10 * m + a, NWAV, stride=24), :] for t in range(5)], axis=1)
            along = jnp.exp(-0.5 * jnp.abs(offset - (wave + m)))
            spread = spread + jnp.where(wave + m < count, value, 0.0) * along
        sums[at:at + 1, :] = jnp.sum(spread, axis=0, keepdims=True)
    row = trace[0:16, :] * 0.25
    total = sums[...]
    falling, rising = total * jnp.exp(row), total * jnp.exp(-row)
    for q in range(5):
        aq[q] = pltpu.roll(falling, 640 - (30 + q), 1)[:, 0:512]
        bq[q] = pltpu.roll(rising, 640 - (30 + q), 1)[:, 0:512]
    weights = [[kernel[p, q] + (1.0 if p == q == 2 else 0.0) for q in range(5)] for p in range(5)]
    depth = iota((8, 128), 0).astype(F32) * 0.25

    def cell(a, tiles):
        for lt in range(4):
            at = slice(128 * lt, 128 * lt + 128)
            if isinstance(a, int):
                fall, rise = ([ref[q, order(a):order(a) + 1, at] for q in range(5)] for ref in (aq, bq))
            else:
                fall, rise = ([pltpu.roll(ref[q, 0:8, at], 9 - a, 0)[0:1] for q in range(5)] for ref in (aq, bq))
            for rt in tiles:
                down, up = jnp.exp(-(depth + 2.0 * rt)), jnp.exp(depth + 2.0 * rt)
                raw = [jnp.minimum(down * f, up * r) for f, r in zip(fall, rise)]
                r0 = pl.multiple_of(8 * (4 * a + rt - 3), 8)
                for p in range(5):
                    h = raw[0] * weights[p][0]
                    for q in range(1, 5):
                        h = h + raw[q] * weights[p][q]
                    hp[p, pl.ds(r0, 8), at] = h

    cell(0, (3,))
    cell(9, (0,))

    def middle(a, carry):
        cell(a, range(4))
        return carry

    lax.fori_loop(1, 9, middle, 0)
    for r in range(0, 256, 8):
        out[r:r + 8, :] = sum(hp[p, r + 6 + p:r + 14 + p, :] for p in range(5))


def call(kernel, outs, in_smem, n_in, scratch=()):
    specs = [pl.BlockSpec(memory_space=pltpu.SMEM)] * in_smem
    specs += [pl.BlockSpec(memory_space=pltpu.VMEM)] * (n_in - in_smem)
    single = not isinstance(outs, (list, tuple))
    vmem = pl.BlockSpec(memory_space=pltpu.VMEM)
    return pl.pallas_call(
        kernel,
        out_shape=outs,
        in_specs=specs,
        out_specs=vmem if single else [vmem] * len(outs),
        scratch_shapes=list(scratch),
        compiler_params=pltpu.CompilerParams(vmem_limit_bytes=40 * 2**20),
        name=kernel.__name__,
    )


def shape(*dims, dtype=F32):
    return jax.ShapeDtypeStruct(dims, dtype)


def along_z(k):
    return [(4 * y + z, 4 * y + (z + k) % 4) for y in range(4) for z in range(4)]


def along_y(other):
    return [(4 * y + z, 4 * other[y] + z) for y in range(4) for z in range(4)]


def body(amplitude, seg_map, seg_table, focal_mask, trace_row, trace_col, block_count, crosstalk):
    w, s = lax.axis_index("wav").astype(I32), lax.axis_index("slab").astype(I32)
    y, z = s // 4, s % 4
    info = jnp.stack([w, s, y, z, jnp.where(y < 2, 1, -1), jnp.where((y == 0) | (y == 3), 0, 1), w, w]).astype(I32)
    finfo = jnp.asarray(scalars())

    piece = call(prepare_kernel, shape(ROWS + 8, NP), 1, 4)(info, amplitude, seg_map, seg_table)
    pieces = [piece] + [lax.ppermute(piece, "slab", along_z(k)) for k in (1, 3, 2)]
    pieces = [pieces[0], pieces[1], pieces[3], pieces[2]]
    own = call(merge_kernel, shape(4, MROWS, 128), 1, 5)(info, *pieces)
    partner = lax.ppermute(own, "slab", along_y((3, 2, 1, 0)))
    beside = lax.ppermute(own, "slab", along_y((1, 0, 3, 2)))
    last = lax.ppermute(own, "slab", along_y((2, 3, 0, 1)))

    def edge(row, rows):
        traces = jnp.concatenate([trace_row[row], trace_col[row], block_count[row]]).astype(F32)
        return jnp.concatenate([focal_mask[rows], jnp.pad(traces, (0, NF - 48))[None]], axis=0)

    above = lax.ppermute(edge(7, slice(56, 64)), "slab", [(i, i + 1) for i in range(NSLAB - 1)])
    below = lax.ppermute(edge(0, slice(0, 8)), "slab", [(i + 1, i) for i in range(NSLAB - 1)])

    utab, vtab, weight, smat = call(
        table_kernel,
        [
            shape(2, 2, 2 * UROWS, 256, dtype=BF16),
            shape(2, 2, 2, HALF, FHALF, dtype=BF16),
            shape(UROWS, NF),
            shape(NF, 256, dtype=BF16),
        ],
        2,
        5,
    )(info, finfo, focal_mask, above, below)
    scratch = [pltpu.VMEM((256, 1024), BF16), pltpu.VMEM((256, 1024), BF16)]
    before = call(first_kernel, shape(2, UROWS, 1024), 2, 5, scratch)(info, finfo, own, partner, utab)
    sent = call(second_kernel, shape(NWAV, 24, 128), 2, 14, scratch)(
        info, finfo, beside, last, utab, before, vtab, weight, smat, trace_row, trace_col, block_count, above, below
    )
    arrived = lax.all_to_all(sent, "wav", split_axis=0, concat_axis=0, tiled=True)
    return call(
        detector_kernel,
        shape(256, 512),
        2,
        3,
        [
            pltpu.VMEM((5, NWAV * 24, 128), F32),
            pltpu.VMEM((72, 640), F32),
            pltpu.VMEM((16, 640), F32),
            pltpu.VMEM((5, 16, 512), F32),
            pltpu.VMEM((5, 16, 512), F32),
            pltpu.VMEM((5, 8 * TILES, 512), F32),
        ],
    )(info, crosstalk, arrived)


def solution(mesh):
    return jax.shard_map(
        body,
        mesh=mesh,
        in_specs=(
            P("slab", None),
            P("slab", None),
            P(),
            P("slab", None),
            P("slab", "wav"),
            P("slab", "wav"),
            P("slab", "wav"),
            P(),
        ),
        out_specs=P("slab", "wav"),
        check_vma=False,
    )
```

```python
import functools

import jax
import jax.numpy as jnp
import numpy as np
from jax import lax
from jax.experimental import pallas as pl
from jax.experimental.pallas import tpu as pltpu
from jax.sharding import PartitionSpec as P

F32, BF16, I32 = jnp.float32, jnp.bfloat16, jnp.int32

NP, NF, NL, DPIX, SEGMENTS, WAVES = 512, 1024, 128, 32, 798, 16
NWAV, NSLAB = 8, 16
ROWS = NP // NSLAB
FROWS = NF // NSLAB
UROWS = FROWS + 16
GROUP = 128
PIECE, EDGE = 2 * (ROWS + 8), 72
MROWS = GROUP + 8
HALF, FHALF = NP // 2, NF // 2

SIN = (6.283185302511503, -41.34170040531721, 81.6051313857832, -76.70301535364747,
       42.02592698447418, -14.899846663536497, 3.2381375046186873)
COS = (0.9999999890590228, -19.73920449945383, 64.93911745989081, -85.45013953079767,
       60.167630950263465, -25.967599245923743, 6.52865815775625)


def place_of():
    w, s = lax.axis_index("wav").astype(I32), lax.axis_index("slab").astype(I32)
    y = s >> 2
    return w, s, y, s & 3, w >> 1, w & 1, jnp.where(y < 2, 1.0, -1.0), jnp.where((y == 0) | (y == 3), 0, 1)


def iota(shape, dim):
    return lax.broadcasted_iota(I32, shape, dim)


def dot(a, b):
    return jnp.dot(a, b, preferred_element_type=F32)


def split2(x):
    high = x.astype(BF16)
    return high, (x - high.astype(F32)).astype(BF16)


def split3(x):
    high = x.astype(BF16)
    rest = x - high.astype(F32)
    middle = rest.astype(BF16)
    return high, middle, (rest - middle.astype(F32)).astype(BF16)


def sincos(turns):
    t = turns - jnp.round(turns)
    z = t * t
    s, c = SIN[-1], COS[-1]
    for a, b in zip(SIN[-2::-1], COS[-2::-1]):
        s, c = s * z + a, c * z + b
    return s * t, c


def reversal(n):
    return (iota((n, n), 0) + iota((n, n), 1) == n - 1).astype(BF16)


def prepare_kernel(amp_in, seg_in, tab_in, mask, trow, tcol, count, out, up, down, trace, amp, seg, tab, tables, edges, sems):
    w, s, y, z, x, core, sign, pair = place_of()
    copies = [
        pltpu.make_async_copy(a, b, sems.at[k])
        for k, (a, b) in enumerate(
            (
                (tab_in, tab),
                (seg_in.at[0:8, :], seg.at[0:8, :]),
                (seg_in.at[16:24, :], seg.at[8:16, :]),
                (amp_in, amp),
                (trow, tables.at[0]),
                (tcol, tables.at[1]),
                (count, tables.at[2]),
                (mask.at[FROWS - 8:FROWS, :], edges.at[0]),
                (mask.at[0:8, :], edges.at[1]),
            )
        )
    ]
    for copy in copies:
        copy.start()
    lower = y >= 2
    rows, cols = iota((ROWS, ROWS), 0), iota((ROWS, ROWS), 1)
    turned = (cols == jnp.where(lower, ROWS - 1 - rows, rows)).astype(BF16)
    rev = reversal(128)
    lane = iota((NP, 128), 1)
    pick = ((iota((NP, 128), 0) == 16 * (lane & 31)) & (lane < 96)).astype(BF16)
    out[...] = jnp.zeros((PIECE, 128), F32)
    for ref in (up, down):
        ref[PIECE + 64:PIECE + EDGE, :] = jnp.zeros((8, 128), F32)
    trace[...] = jnp.zeros((8, 128), F32)
    for copy in copies:
        copy.wait()
    for c in range(3):
        table = tables[c].astype(F32)
        trace[:, 16 * c:16 * c + 16] = table
        up[PIECE + 64:PIECE + 65, 16 * c:16 * c + 16] = table[7:8]
        down[PIECE + 64:PIECE + 65, 16 * c:16 * c + 16] = table[0:1]
    ids = sum(dot(part, pick) for part in split2(seg[...].astype(F32)))
    upper_ids, lower_ids = ids[0:1], ids[8:9]
    ids = jnp.concatenate(
        [jnp.where(lower, lower_ids, upper_ids), jnp.where(lower, upper_ids, lower_ids)], axis=1
    )
    which = iota((SEGMENTS, 256), 0).astype(F32)
    found = sum(dot(part, (which == ids).astype(BF16)) for part in split2(tab[...].astype(F32)))
    found = jnp.sum(jnp.where(iota((3, 256), 0) == (iota((3, 256), 1) & 127) >> 5, found, 0.0), axis=0, keepdims=True)
    for k in range(2):
        out[ROWS + k:ROWS + k + 1, :] = found[:, 128 * k:128 * k + 128]
    first = core == 0
    left = jnp.where(first, amp[:, 0:128], amp[:, 128:256])
    right = jnp.where(first, amp[:, 384:512], amp[:, 256:384])
    out[0:ROWS, :] = sum(dot(turned, part) for part in split3(left))
    out[ROWS + 8:2 * ROWS + 8, :] = sum(dot(turned, dot(part, rev).astype(BF16)) for part in split3(right))
    for k, ref in enumerate((up, down)):
        ref[0:PIECE, :] = out[...]
        for q in range(8):
            ref[PIECE + 8 * q:PIECE + 8 * q + 8, :] = edges[k, :, 128 * q:128 * q + 128]


def merge_kernel(p0, p1, p2, p3, after, out, wrap):
    del after
    w, s, y, z, x, core, sign, pair = place_of()
    wrap[...] = jnp.where(z == 0, p1[PIECE:PIECE + EDGE, :], p3[PIECE:PIECE + EDGE, :])
    out[:, GROUP:MROWS, :] = jnp.zeros((2, 8, 128), F32)
    for k, piece in enumerate((p0, p1, p2, p3)):
        source = lax.rem(z - k + 4, 4)
        place = jnp.where(y >= 2, 3 - source, source)
        for at in range(4):

            @pl.when(place == at)
            def _(at=at, piece=piece):
                for t in range(2):
                    for b in range(2):
                        r0 = (ROWS + 8) * t + 16 * b
                        out[t, pl.ds(2 * at + b, 16, stride=8), :] = piece[r0:r0 + 16, :]
                out[0, GROUP + 2 * at:GROUP + 2 * at + 2, :] = piece[ROWS:ROWS + 2, :]


def wavelength(w):
    return jnp.full((1, 1), 1000 + w, I32).astype(F32)


def angle(m, n, w):
    lam = wavelength(w)
    short = jnp.round(250.0 / lam * 2.0**14) * 2.0**-14
    rest = (250.0 - short * lam) / lam
    product = m * n
    a, b = (product >> 10).astype(F32), (product & 1023).astype(F32)
    t = a * short
    t = t - jnp.round(t)
    return sincos(t + a * rest + b * (250.0 / 1024.0 / lam))


def table_kernel(after, utab, vtab, smat):
    del after
    w, s, y, z, x, core, sign, pair = place_of()
    for m in range(4):
        wave = 2 * (w if m < 2 else w ^ 1) + (m & 1)
        for p in range(2):
            g = pair if p == 0 else 1 - pair
            u = 64 * s - 8 + iota((UROWS, GROUP), 0)
            rho = iota((UROWS, GROUP), 1)
            i = 128 * g + 16 * (rho & 7) + (rho >> 3)
            sin, cos = angle(2 * u + 1 - NF, 2 * i + 1 - NP, wave)
            for at, part in ((0, cos), (GROUP, sin * sign)):
                high, low = split2(part)
                utab[p, m, 0:UROWS, at:at + GROUP] = high
                utab[p, m, UROWS:2 * UROWS, at:at + GROUP] = low

        if m >= 2:
            continue

        def chunk(c, carry, m=m, wave=wave):
            j0 = pl.multiple_of(16 * c, 16)
            j = ((j0 + 128 * core) & 255) + iota((16, FHALF), 0)
            v = iota((16, FHALF), 1)
            sin, cos = angle(2 * v + 1 - NF, 2 * j + 1 - NP, wave)
            for q, part in ((0, cos), (1, sin)):
                high, low = split2(part)
                vtab[m, q, 0, pl.ds(j0, 16), :] = high
                vtab[m, q, 1, pl.ds(j0, 16), :] = low
            return carry

        lax.fori_loop(0, HALF // 16, chunk, 0)
    row, lane = iota((FHALF, 256), 0), iota((FHALF, 256), 1)
    column = 2 * ((x + (lane >> 5)) & 3) + jnp.where(lane < 128, core, 1 - core)
    lens = jnp.where((lane & 31) < 18, 16 * column - 1 + (lane & 31), -1)
    smat[0:FHALF, :] = (lens == row >> 3).astype(BF16)
    smat[FHALF:NF, :] = (lens == NL - 1 - (row >> 3)).astype(BF16)


def weight_kernel(mask, p1, p3, edge, trace, after, weight, lenses):
    del after
    w, s, y, z, x, core, sign, pair = place_of()
    above = jnp.where(z == 0, edge[...], p1[PIECE:PIECE + EDGE, :])
    below = jnp.where(z == 3, edge[...], p3[PIECE:PIECE + EDGE, :])
    lenses[0:8, :] = trace[...]
    lenses[8:9, :] = above[64:65]
    lenses[9:10, :] = below[64:65]
    lenses[10:16, :] = jnp.zeros((6, 128), F32)
    u = 64 * s - 8 + iota((UROWS, FHALF), 0)
    v = iota((UROWS, FHALF), 1)
    down, across = (2 * u + 1 - NF).astype(F32) * 0.5, (2 * v + 1 - NF).astype(F32) * 0.5
    fade = 1.0 - jnp.exp((down * down + across * across) * (-1.0 / 1024.0))
    rev = reversal(256)
    above, below = (jnp.concatenate([ref[8 * q:8 * q + 8] for q in range(8)], axis=1) for ref in (above, below))
    full = jnp.concatenate([above, mask[...], below], axis=0)
    t = full[:, :FHALF] * fade
    weight[:, :FHALF] = t * t * 2.0**-24
    for q in range(2):
        flipped = sum(dot(part, rev) for part in split3(full[:, NF - 256 * (q + 1):NF - 256 * q]))
        t = flipped * fade[:, 256 * q:256 * (q + 1)]
        weight[:, FHALF + 256 * q:FHALF + 256 * (q + 1)] = t * t * 2.0**-24


def pair_fields(first, second, utab, p, whi, wlo):
    w, s, y, z, x, core, sign, pair = place_of()
    g = pair if p == 0 else 1 - pair
    coef = jnp.concatenate([first[0, GROUP:MROWS, :], second[0, GROUP:MROWS, :]], axis=0)
    high, low = split2(coef)
    coef = jnp.concatenate([high, low], axis=0)
    row, lane = iota((128, 128), 0), iota((128, 128), 1)
    place = iota((16, 128), 0)
    down = (32 * (8 * g + (place & 7)) + 1 - NP).astype(F32) * (1.0 / 1024.0)
    toward = jnp.where(place < 8, sign, -sign)
    across = (2 * (128 * core + iota((16, 128), 1)) + 1 - NP).astype(F32) * (1.0 / 1024.0)
    paths, steps = [], []
    for side in range(2):
        block = 8 * core + (lane >> 4)
        block = block if side == 0 else 31 - block
        pqr = []
        for c in range(3):
            both = dot(coef, (row == 32 * c + block).astype(BF16))
            pqr.append(both[0:16] + both[16:32])
        slope = toward * pqr[2]
        paths.append(pqr[0] + (across if side == 0 else -across) * pqr[1] + slope * down)
        steps.append(slope * (1.0 / 512.0))
    fields = []
    for m in range(4):
        inverse = 1.0 / wavelength(2 * (w if m < 2 else w ^ 1) + (m & 1))
        start = [sincos(path * inverse) for path in paths]
        turn = [sincos(step * inverse) for step in steps]

        def four(values, n):
            return [values[side][n][8 * t:8 * t + 8] for t in range(2) for side in range(2)]

        step_im, step_re = four(turn, 0), four(turn, 1)

        def rows(r2, carry, step_im=step_im, step_re=step_re):
            re, im = carry
            found = [[] for _ in range(8)]
            for h in range(2):
                r0 = pl.multiple_of(16 * r2 + 8 * h, 8)
                qre, qim = [], []
                for t, ref in enumerate((first, second)):
                    for side in range(2):
                        a = ref[side, pl.ds(r0, 8), :]
                        qre.append(a * re[2 * t + side])
                        qim.append(a * im[2 * t + side])
                (fl, fr, sl, sr), (gl, gr, hl, hr) = qre, qim
                a, b, c, d = fl + sl, sl - fl, fr + sr, sr - fr
                e, f, k, n = gl + hl, gl - hl, gr + hr, gr - hr
                for q, value in enumerate((a + c, e + k, e - k, c - a, f + n, b + d, b - d, n - f)):
                    found[q].append(value)
                re, im = (
                    [x * p - y * q for x, y, p, q in zip(re, im, step_re, step_im)],
                    [x * q + y * p for x, y, p, q in zip(re, im, step_re, step_im)],
                )
            for q, values in enumerate(found):
                high, low = split2(jnp.concatenate(values, axis=0))
                r0 = pl.multiple_of(16 * r2 + (GROUP if q >= 4 else 0), 16)
                c0 = 128 * (q & 3)
                whi[pl.ds(r0, 16), c0:c0 + 128] = high
                wlo[pl.ds(r0, 16), c0:c0 + 128] = low
            return re, im

        lax.fori_loop(0, 8, rows, (four(start, 1), four(start, 0)))
        table = utab[p, m]
        both = dot(table, whi[...])
        fields.append(both[:UROWS] + both[UROWS:] + dot(table[:UROWS], wlo[...]))
    return fields


def first_kernel(first, second, utab, out, whi, wlo):
    for m, field in enumerate(pair_fields(first, second, utab, 0, whi, wlo)):
        out[m] = field


def second_kernel(first, second, utab, before, after, keep, give, whi, wlo):
    del after
    for m, field in enumerate(pair_fields(first, second, utab, 1, whi, wlo)):
        (keep if m < 2 else give)[m & 1] = field + before[m]


def lens_kernel(keep, got, vtab, weight, smat, lenses, mine, other):
    mine[...] = jnp.zeros(mine.shape, F32)
    other[...] = jnp.zeros(other.shape, F32)
    outs = [ref.at[k] for ref in (mine, other) for k in range(4)]
    for m in range(2):
        parts = [
            jnp.concatenate([ref[m, :, 128 * q:128 * q + 128] for ref in (keep, got)], axis=1) for q in range(4)
        ]
        terms = []
        for q in range(2):
            side = jnp.concatenate(parts[2 * q:2 * q + 2], axis=0)
            high, low = split2(side)
            both = dot(jnp.concatenate([high, low], axis=0), vtab[m, q, 0])
            terms.append(both[:2 * UROWS] + both[2 * UROWS:] + dot(high, vtab[m, q, 1]))
        lens = 0.0
        for q, value in enumerate((terms[0] + terms[1], terms[0] - terms[1])):
            re, im = value[:UROWS], value[UROWS:]
            power = (re * re + im * im) * weight[:, FHALF * q:FHALF * (q + 1)]
            summed = jnp.sum(power.reshape(UROWS // 8, 8, FHALF), axis=1)
            for part in split3(summed):
                lens = lens + dot(part, smat[FHALF * q:FHALF * (q + 1), :])
        for d in range(NWAV):
            outs[d][10 * m:10 * m + 10, 0:32] = lens[:, 32 * d:32 * d + 32]
    tables = lenses[0:10, 0:48]
    for out in outs:
        out[0:10, 32:80] = tables


def pack_kernel(mine, got, *outs):
    for k, out in enumerate(outs):
        out[0] = mine[k]
        out[1] = got[k]


TILES = 4 * 8 + 2


def order(a):
    return a - 1 if 0 < a < 9 else 8 + a // 9


def detector_kernel(kernel, a0, a1, a2, a3, out, arrived, spec, trace, sums, aq, bq, hp):
    w, s, y, z, x, core, sign, pair = place_of()
    for k, ref in enumerate((a0, a1, a2, a3)):
        source = 2 * ((x - k + 4) & 3)
        arrived[source + core] = ref[0]
        arrived[source + 1 - core] = ref[1]
    lane = iota((24, 128), 1)
    prev, own, nxt = arrived[jnp.maximum(w - 1, 0)], arrived[w], arrived[jnp.minimum(w + 1, NWAV - 1)]
    spot = (iota((128, 640), 0) == iota((128, 640), 1) >> 5).astype(BF16)
    rows = arrived[...].reshape(NWAV * 24, 128)
    wide = sum(dot(part, spot) for part in split3(rows))
    for t in range(5):
        spec[t] = wide[:, 128 * t:128 * t + 128]
    tables = []
    for c in range(3):
        tables.append(
            jnp.where(
                lane == 0,
                pltpu.roll(prev, 128 - (47 + 16 * c), 1),
                jnp.where(
                    lane < 17,
                    pltpu.roll(own, 128 - (31 + 16 * c), 1),
                    jnp.where(lane == 17, pltpu.roll(nxt, 128 - (15 + 16 * c), 1), 0.0),
                ),
            )
        )
    trace[...] = dot(jnp.concatenate(tables, axis=0).astype(BF16), spot)
    place = (iota((8, 640), 1) & 31).astype(F32)
    wave = 2.0 * iota((8, 640), 0).astype(F32)
    sums[...] = jnp.zeros(sums.shape, F32)
    for a in range(10):
        at = order(a)
        offset = place - trace[24 + at:25 + at, :]
        count = trace[48 + at:49 + at, :]
        spread = 0.0
        for m in range(2):
            value = jnp.concatenate([spec[t, pl.ds(10 * m + a, NWAV, stride=24), :] for t in range(5)], axis=1)
            along = jnp.exp(-0.5 * jnp.abs(offset - (wave + m)))
            spread = spread + jnp.where(wave + m < count, value, 0.0) * along
        sums[at:at + 1, :] = jnp.sum(spread, axis=0, keepdims=True)
    row = trace[0:16, :] * 0.25
    total = sums[...]
    falling, rising = total * jnp.exp(row), total * jnp.exp(-row)
    for q in range(5):
        aq[q] = pltpu.roll(falling, 640 - (30 + q), 1)[:, 0:512]
        bq[q] = pltpu.roll(rising, 640 - (30 + q), 1)[:, 0:512]
    weights = [[kernel[p, q] + (1.0 if p == q == 2 else 0.0) for q in range(5)] for p in range(5)]
    depth = iota((8, 128), 0).astype(F32) * 0.25

    def cell(a, tiles):
        for lt in range(4):
            at = slice(128 * lt, 128 * lt + 128)
            if isinstance(a, int):
                fall, rise = ([ref[q, order(a):order(a) + 1, at] for q in range(5)] for ref in (aq, bq))
            else:
                fall, rise = ([pltpu.roll(ref[q, 0:8, at], 9 - a, 0)[0:1] for q in range(5)] for ref in (aq, bq))
            for rt in tiles:
                down, up = jnp.exp(-(depth + 2.0 * rt)), jnp.exp(depth + 2.0 * rt)
                raw = [jnp.minimum(down * f, up * r) for f, r in zip(fall, rise)]
                r0 = pl.multiple_of(8 * (4 * a + rt - 3), 8)
                for p in range(5):
                    h = raw[0] * weights[p][0]
                    for q in range(1, 5):
                        h = h + raw[q] * weights[p][q]
                    hp[p, pl.ds(r0, 8), at] = h

    cell(0, (3,))
    cell(9, (0,))

    def middle(a, carry):
        cell(a, range(4))
        return carry

    lax.fori_loop(1, 9, middle, 0)
    for r in range(0, 256, 8):
        out[r:r + 8, :] = sum(hp[p, r + 6 + p:r + 14 + p, :] for p in range(5))


def call(kernel, outs, in_smem, n_in, scratch=(), tail=(), limit=40):
    specs = [pl.BlockSpec(memory_space=pltpu.SMEM)] * in_smem
    specs += [pl.BlockSpec(memory_space=pltpu.VMEM)] * (n_in - in_smem)
    specs[n_in - len(tail):] = tail
    single = not isinstance(outs, (list, tuple))
    vmem = pl.BlockSpec(memory_space=pltpu.VMEM)
    return pl.pallas_call(
        kernel,
        out_shape=outs,
        in_specs=specs,
        out_specs=vmem if single else [vmem] * len(outs),
        scratch_shapes=list(scratch),
        compiler_params=pltpu.CompilerParams(vmem_limit_bytes=limit * 2**20),
        name=kernel.__name__,
    )


def shape(*dims, dtype=F32):
    return jax.ShapeDtypeStruct(dims, dtype)


def along_z(k):
    return [(4 * y + z, 4 * y + (z + k) % 4) for y in range(4) for z in range(4)]


def along_y(other):
    return [(4 * y + z, 4 * other[y] + z) for y in range(4) for z in range(4)]


def body(amplitude, seg_map, seg_table, focal_mask, trace_row, trace_col, block_count, crosstalk):
    anywhere = [pl.BlockSpec(memory_space=pl.ANY)]
    piece, up, down, trace = call(
        prepare_kernel,
        [shape(PIECE, 128), shape(PIECE + EDGE, 128), shape(PIECE + EDGE, 128), shape(8, 128)],
        0,
        7,
        [
            pltpu.VMEM((ROWS, NP), F32),
            pltpu.VMEM((16, NP), I32),
            pltpu.VMEM((3, SEGMENTS), I32),
            pltpu.VMEM((3, 8, 16), I32),
            pltpu.VMEM((2, 8, NF), F32),
            pltpu.SemaphoreType.DMA((9,)),
        ],
        tail=anywhere * 7,
        limit=54,
    )(amplitude, seg_map, seg_table.T, focal_mask, trace_row, trace_col, block_count)
    utab, vtab, smat = call(
        table_kernel,
        [
            shape(2, 4, 2 * UROWS, 256, dtype=BF16),
            shape(2, 2, 2, HALF, FHALF, dtype=BF16),
            shape(NF, 256, dtype=BF16),
        ],
        0,
        1,
        tail=anywhere,
    )(piece)
    p1 = lax.ppermute(up, "slab", along_z(1))
    p3 = lax.ppermute(down, "slab", along_z(3))
    p2 = lax.ppermute(piece, "slab", along_z(2))
    own, wrap = call(merge_kernel, [shape(2, MROWS, 128), shape(EDGE, 128)], 0, 5, tail=anywhere)(
        piece, p1, p2, p3, smat
    )
    partner = lax.ppermute(own, "slab", along_y((3, 2, 1, 0)))
    beside = lax.ppermute(own, "slab", along_y((1, 0, 3, 2)))
    last = lax.ppermute(own, "slab", along_y((2, 3, 0, 1)))
    edge = lax.ppermute(
        wrap, "slab", [(4 * y, 4 * y + 4) for y in range(3)] + [(4 * y + 7, 4 * y + 3) for y in range(3)]
    )
    scratch = [pltpu.VMEM((256, 512), BF16)] * 2
    before = call(first_kernel, shape(4, UROWS, 512), 0, 3, scratch)(own, partner, utab)
    keep, give = call(second_kernel, [shape(2, UROWS, 512)] * 2, 0, 5, scratch, tail=anywhere)(
        beside, last, utab, before, edge
    )
    weight, lenses = call(weight_kernel, [shape(UROWS, NF), shape(16, 128)], 0, 6, tail=anywhere)(
        focal_mask, p1, p3, edge, trace, give
    )
    sibling = [(i, i ^ 1) for i in range(NWAV)]
    crossed = lax.ppermute(give, "wav", sibling)
    mine, other = call(lens_kernel, [shape(4, 24, 128)] * 2, 0, 6)(
        keep, crossed, vtab, weight, smat, lenses
    )
    got = lax.ppermute(other, "wav", sibling)
    sent = call(pack_kernel, [shape(2, 24, 128)] * 4, 0, 2)(mine, got)
    arrived = [sent[0]] + [
        lax.ppermute(sent[k], "wav", [(i, (i + 2 * k) % NWAV) for i in range(NWAV)]) for k in (1, 2, 3)
    ]
    return call(
        detector_kernel,
        shape(256, 512),
        1,
        5,
        [
            pltpu.VMEM((NWAV, 24, 128), F32),
            pltpu.VMEM((5, NWAV * 24, 128), F32),
            pltpu.VMEM((72, 640), F32),
            pltpu.VMEM((16, 640), F32),
            pltpu.VMEM((5, 16, 512), F32),
            pltpu.VMEM((5, 16, 512), F32),
            pltpu.VMEM((5, 8 * TILES, 512), F32),
        ],
    )(crosstalk, *arrived)


def solution(mesh):
    return jax.shard_map(
        body,
        mesh=mesh,
        in_specs=(
            P("slab", None),
            P("slab", None),
            P(),
            P("slab", None),
            P("slab", "wav"),
            P("slab", "wav"),
            P("slab", "wav"),
            P(),
        ),
        out_specs=P("slab", "wav"),
        check_vma=False,
    )
```

```python
import functools
import math

import jax
import jax.numpy as jnp
import numpy as np
from jax import lax
from jax.experimental import pallas as pl
from jax.experimental.pallas import tpu as pltpu
from jax.sharding import PartitionSpec as P

F32, BF16, I32 = jnp.float32, jnp.bfloat16, jnp.int32

NP, NF, NL, DPIX, SEGMENTS, WAVES = 512, 1024, 128, 32, 798, 16
NWAV, NSLAB = 8, 16
ROWS = NP // NSLAB
FROWS = NF // NSLAB
UROWS = FROWS + 16
GROUP = 128
PIECE, EDGE = 2 * (ROWS + 8), 72
MROWS = GROUP + 8
HALF, FHALF = NP // 2, NF // 2

SIN = (6.283184916495428, -41.34158923268831, 81.59994332977429, -76.61447253115396, 41.34288235413569, -12.471243534350362)
COS = (0.9999999890590228, -19.73920449945383, 64.93911745989081, -85.45013953079767,
       60.167630950263465, -25.967599245923743, 6.52865815775625)


def place_of():
    w, s = lax.axis_index("wav").astype(I32), lax.axis_index("slab").astype(I32)
    y = s >> 2
    return w, s, y, s & 3, w >> 1, w & 1, jnp.where(y < 2, 1.0, -1.0), jnp.where((y == 0) | (y == 3), 0, 1)


def iota(shape, dim):
    return lax.broadcasted_iota(I32, shape, dim)


def dot(a, b):
    return jnp.dot(a, b, preferred_element_type=F32)


def split2(x):
    high = x.astype(BF16)
    return high, (x - high.astype(F32)).astype(BF16)


def split3(x):
    high = x.astype(BF16)
    rest = x - high.astype(F32)
    middle = rest.astype(BF16)
    return high, middle, (rest - middle.astype(F32)).astype(BF16)


def sincos(turns):
    t = turns - jnp.round(turns)
    z = t * t
    s, c = SIN[-1], COS[-1]
    for a in SIN[-2::-1]:
        s = s * z + a
    for b in COS[-2::-1]:
        c = c * z + b
    return s * t, c


def focal_row(s, shape):
    a = iota(shape, 0)
    return FROWS * s + jnp.where(a < FROWS, a, jnp.where(a < FROWS + 8, a - FROWS - 8, a - 8))


def reversal(n):
    return (iota((n, n), 0) + iota((n, n), 1) == n - 1).astype(BF16)


def prepare_kernel(amp_in, seg_in, tab_in, mask, trow, tcol, count, out, up, down, trace, amp, seg, tab, tables, edges, sems):
    w, s, y, z, x, core, sign, pair = place_of()
    copies = [
        pltpu.make_async_copy(a, b, sems.at[k])
        for k, (a, b) in enumerate(
            (
                (tab_in, tab),
                (seg_in.at[0:8, :], seg.at[0:8, :]),
                (seg_in.at[16:24, :], seg.at[8:16, :]),
                (amp_in, amp),
                (trow, tables.at[0]),
                (tcol, tables.at[1]),
                (count, tables.at[2]),
                (mask.at[FROWS - 8:FROWS, :], edges.at[0]),
                (mask.at[0:8, :], edges.at[1]),
            )
        )
    ]
    for copy in copies:
        copy.start()
    lower = y >= 2
    rows, cols = iota((ROWS, ROWS), 0), iota((ROWS, ROWS), 1)
    turned = (cols == jnp.where(lower, ROWS - 1 - rows, rows)).astype(BF16)
    rev = reversal(128)
    lane = iota((NP, 128), 1)
    pick = ((iota((NP, 128), 0) == 16 * (lane & 31)) & (lane < 96)).astype(BF16)
    out[...] = jnp.zeros((PIECE, 128), F32)
    for ref in (up, down):
        ref[PIECE + 64:PIECE + EDGE, :] = jnp.zeros((8, 128), F32)
    trace[...] = jnp.zeros((8, 128), F32)
    for copy in copies:
        copy.wait()
    for c in range(3):
        table = tables[c].astype(F32)
        trace[:, 16 * c:16 * c + 16] = table
        up[PIECE + 64:PIECE + 65, 16 * c:16 * c + 16] = table[7:8]
        down[PIECE + 64:PIECE + 65, 16 * c:16 * c + 16] = table[0:1]
    ids = sum(dot(part, pick) for part in split2(seg[...].astype(F32)))
    upper_ids, lower_ids = ids[0:1], ids[8:9]
    ids = jnp.concatenate(
        [jnp.where(lower, lower_ids, upper_ids), jnp.where(lower, upper_ids, lower_ids)], axis=1
    )
    which = iota((SEGMENTS, 256), 0).astype(F32)
    found = sum(dot(part, (which == ids).astype(BF16)) for part in split2(tab[...].astype(F32)))
    found = jnp.sum(jnp.where(iota((3, 256), 0) == (iota((3, 256), 1) & 127) >> 5, found, 0.0), axis=0, keepdims=True)
    for k in range(2):
        out[ROWS + k:ROWS + k + 1, :] = found[:, 128 * k:128 * k + 128]
    first = core == 0
    left = jnp.where(first, amp[:, 0:128], amp[:, 128:256])
    right = jnp.where(first, amp[:, 384:512], amp[:, 256:384])
    out[0:ROWS, :] = sum(dot(turned, part) for part in split3(left))
    out[ROWS + 8:2 * ROWS + 8, :] = sum(dot(turned, dot(part, rev).astype(BF16)) for part in split3(right))
    for k, ref in enumerate((up, down)):
        ref[0:PIECE, :] = out[...]
        for q in range(8):
            ref[PIECE + 8 * q:PIECE + 8 * q + 8, :] = edges[k, :, 128 * q:128 * q + 128]


def merge_kernel(p0, p1, p2, p3, after, out, wrap):
    del after
    w, s, y, z, x, core, sign, pair = place_of()
    wrap[...] = jnp.where(z == 0, p1[PIECE:PIECE + EDGE, :], p3[PIECE:PIECE + EDGE, :])
    out[:, GROUP:MROWS, :] = jnp.zeros((2, 8, 128), F32)
    for k, piece in enumerate((p0, p1, p2, p3)):
        source = lax.rem(z - k + 4, 4)
        place = jnp.where(y >= 2, 3 - source, source)
        for at in range(4):

            @pl.when(place == at)
            def _(at=at, piece=piece):
                for t in range(2):
                    for b in range(2):
                        r0 = (ROWS + 8) * t + 16 * b
                        out[t, pl.ds(2 * at + b, 16, stride=8), :] = piece[r0:r0 + 16, :]
                out[0, GROUP + 2 * at:GROUP + 2 * at + 2, :] = piece[ROWS:ROWS + 2, :]


def wavelength(w):
    return jnp.full((1, 1), 1000 + w, I32).astype(F32)


def slope(n, w):
    lam = wavelength(w)
    short = jnp.round(250.0 / lam * 2.0**14) * 2.0**-14
    rest = (250.0 - short * lam) / lam
    whole = n * (short * 2.0**-10)
    high = jnp.round(whole * 2.0**13) * 2.0**-13
    return high, (whole - high) + n * (rest * 2.0**-10)


def angle(m, step):
    t = m * step[0]
    t = t - jnp.round(t)
    return sincos(t + m * step[1])


def odd(index, count):
    return (2 * index + 1 - count).astype(F32)


def focal_table_kernel(after, utab):
    del after
    w, s, y, z, x, core, sign, pair = place_of()
    m = odd(focal_row(s, (UROWS, GROUP)), NF)
    rho = iota((1, GROUP), 1)
    for k in range(4):
        wave = 2 * (w if k < 2 else w ^ 1) + (k & 1)
        for p in range(2):
            g = pair if p == 0 else 1 - pair
            sin, cos = angle(m, slope(odd(128 * g + 16 * (rho & 7) + (rho >> 3), NP), wave))
            for at, part in ((0, cos), (GROUP, sin * sign)):
                high, low = split2(part)
                utab[p, k, 0:UROWS, at:at + GROUP] = high
                utab[p, k, UROWS:2 * UROWS, at:at + GROUP] = low


def lens_table_kernel(after, vtab, smat):
    del after
    w, s, y, z, x, core, sign, pair = place_of()
    m = odd(iota((16, 128), 1), NF)
    for k in range(2):

        def chunk(c, carry, k=k):
            j0 = pl.multiple_of(16 * c, 16)
            step = slope(odd(((j0 + 128 * core) & 255) + iota((16, 128), 0), NP), 2 * w + k)
            sin, cos = angle(m, step)
            turn_im, turn_re = angle(jnp.full((16, 128), 256.0, F32), step)
            for t in range(4):
                for q, part in ((0, cos), (1, sin)):
                    high, low = split2(part)
                    vtab[k, q, 0, pl.ds(j0, 16), 128 * t:128 * t + 128] = high
                    vtab[k, q, 1, pl.ds(j0, 16), 128 * t:128 * t + 128] = low
                cos, sin = cos * turn_re - sin * turn_im, cos * turn_im + sin * turn_re
            return carry

        lax.fori_loop(0, HALF // 16, chunk, 0)
    row, lane = iota((FHALF, 256), 0), iota((FHALF, 256), 1)
    column = 2 * ((lane >> 5) & 3) + jnp.where(lane < 128, core, 1 - core)
    lens = jnp.where((lane & 31) < 18, 16 * column - 1 + (lane & 31), -1)
    smat[0:FHALF, :] = (lens == row >> 3).astype(BF16)
    smat[FHALF:NF, :] = (lens == NL - 1 - (row >> 3)).astype(BF16)


def weight_kernel(mask, p1, p3, edge, trace, after, weight, lenses):
    del after
    w, s, y, z, x, core, sign, pair = place_of()
    above = jnp.where(z == 0, edge[...], p1[PIECE:PIECE + EDGE, :])
    below = jnp.where(z == 3, edge[...], p3[PIECE:PIECE + EDGE, :])
    lenses[0:8, :] = trace[...]
    lenses[8:9, :] = above[64:65]
    lenses[9:10, :] = below[64:65]
    lenses[10:16, :] = jnp.zeros((6, 128), F32)
    u = focal_row(s, (UROWS, FHALF))
    v = iota((UROWS, FHALF), 1)
    down, across = (2 * u + 1 - NF).astype(F32) * 0.5, (2 * v + 1 - NF).astype(F32) * 0.5
    fade = 1.0 - jnp.exp((down * down + across * across) * (-1.0 / 1024.0))
    rev = reversal(256)
    above, below = (jnp.concatenate([ref[8 * q:8 * q + 8] for q in range(8)], axis=1) for ref in (above, below))
    full = jnp.concatenate([mask[...], above, below], axis=0)
    t = full[:, :FHALF] * fade
    weight[:, :FHALF] = t * t * 2.0**-24
    for q in range(2):
        flipped = sum(dot(part, rev) for part in split3(full[:, NF - 256 * (q + 1):NF - 256 * q]))
        t = flipped * fade[:, 256 * q:256 * (q + 1)]
        weight[:, FHALF + 256 * q:FHALF + 256 * (q + 1)] = t * t * 2.0**-24


def pair_fields(first, second, utab, p, whi, wlo):
    w, s, y, z, x, core, sign, pair = place_of()
    g = pair if p == 0 else 1 - pair
    coef = jnp.concatenate([first[0, GROUP:MROWS, :], second[0, GROUP:MROWS, :]], axis=0)
    high, low = split2(coef)
    coef = jnp.concatenate([high, low], axis=0)
    row, lane = iota((128, 128), 0), iota((128, 128), 1)
    place = iota((16, 128), 0)
    down = (32 * (8 * g + (place & 7)) + 1 - NP).astype(F32) * (1.0 / 1024.0)
    toward = jnp.where(place < 8, sign, -sign)
    across = (2 * (128 * core + iota((16, 128), 1)) + 1 - NP).astype(F32) * (1.0 / 1024.0)
    paths, steps = [], []
    for side in range(2):
        block = 8 * core + (lane >> 4)
        block = block if side == 0 else 31 - block
        pqr = []
        for c in range(3):
            both = dot(coef, (row == 32 * c + block).astype(BF16))
            pqr.append(both[0:16] + both[16:32])
        slope = toward * pqr[2]
        paths.append(pqr[0] + (across if side == 0 else -across) * pqr[1] + slope * down)
        steps.append(slope * (1.0 / 512.0))
    fields = []
    for m in range(4):
        inverse = 1.0 / wavelength(2 * (w if m < 2 else w ^ 1) + (m & 1))
        start = [sincos(path * inverse) for path in paths]
        turn = [sincos(step * inverse) for step in steps]

        def four(values, n):
            return [values[side][n][8 * t:8 * t + 8] for t in range(2) for side in range(2)]

        step_im, step_re = four(turn, 0), four(turn, 1)

        def rows(r2, carry, m=m, step_im=step_im, step_re=step_re):
            re, im = carry
            found = [[] for _ in range(8)]
            for h in range(2):
                r0 = pl.multiple_of(16 * r2 + 8 * h, 8)
                qre, qim = [], []
                for t, ref in enumerate((first, second)):
                    for side in range(2):
                        a = ref[side, pl.ds(r0, 8), :]
                        qre.append(a * re[2 * t + side])
                        qim.append(a * im[2 * t + side])
                for side in range(2):
                    found[2 * side].append(qre[side] + qre[2 + side])
                    found[2 * side + 1].append(qim[side] + qim[2 + side])
                    found[4 + 2 * side].append(qim[side] - qim[2 + side])
                    found[5 + 2 * side].append(qre[2 + side] - qre[side])
                re, im = (
                    [x * p - y * q for x, y, p, q in zip(re, im, step_re, step_im)],
                    [x * q + y * p for x, y, p, q in zip(re, im, step_re, step_im)],
                )
            for q, values in enumerate(found):
                high, low = split2(jnp.concatenate(values, axis=0))
                r0 = pl.multiple_of(16 * r2 + (GROUP if q >= 4 else 0), 16)
                c0 = 128 * (q & 3)
                whi[m, pl.ds(r0, 16), c0:c0 + 128] = high
                wlo[m, pl.ds(r0, 16), c0:c0 + 128] = low
            return re, im

        lax.fori_loop(0, 8, rows, (four(start, 1), four(start, 0)), unroll=True)
        table = utab[p, m]
        both = dot(table, whi[m])
        fields.append(both[:UROWS] + both[UROWS:] + dot(table[:UROWS], wlo[m]))
    return fields


def first_kernel(first, second, utab, after, out, whi, wlo):
    del after
    for m, field in enumerate(pair_fields(first, second, utab, 0, whi, wlo)):
        out[m] = field


def second_kernel(first, second, utab, before, after, keep, give, whi, wlo):
    del after
    for m, field in enumerate(pair_fields(first, second, utab, 1, whi, wlo)):
        (keep if m < 2 else give)[m & 1] = field + before[m]


def lens_kernel(keep, got, vtab, weight, smat, lenses, mine, other):
    for m in range(2):
        lre, lim, rre, rim = (
            jnp.concatenate([ref[m, :, 128 * q:128 * q + 128] for ref in (keep, got)], axis=1) for q in range(4)
        )
        parts = [lre + rre, lim + rim, lim - rim, rre - lre]
        terms = []
        for q in range(2):
            side = jnp.concatenate(parts[2 * q:2 * q + 2], axis=0)
            high, low = split2(side)
            both = dot(jnp.concatenate([high, low], axis=0), vtab[m, q, 0])
            terms.append(both[:2 * UROWS] + both[2 * UROWS:] + dot(high, vtab[m, q, 1]))
        lens = 0.0
        for q, value in enumerate((terms[0] + terms[1], terms[0] - terms[1])):
            re, im = value[:UROWS], value[UROWS:]
            power = (re * re + im * im) * weight[:, FHALF * q:FHALF * (q + 1)]
            summed = jnp.sum(power.reshape(UROWS // 8, 8, FHALF), axis=1)
            for part in split2(summed):
                lens = lens + dot(part, smat[FHALF * q:FHALF * (q + 1), :])
        for k, out in enumerate((mine, other)):
            out[16 * m:16 * m + 10, :] = lens[:, 128 * k:128 * k + 128]
            out[16 * m + 10:16 * m + 16, :] = jnp.zeros((6, 128), F32)
    row, lane = iota((128, 128), 0), iota((128, 128), 1) & 31
    spot = ((lane >= 18) & (lane < 21) & (row == 16 * (lane - 18) + 15)) | ((lane >= 21) & (lane < 24) & (row == 16 * (lane - 21)))
    sides = dot(lenses[...].astype(BF16), spot.astype(BF16))
    for out in (mine, other):
        out[0:16, :] += sides


def pack_kernel(mine, got, after, *outs, shifts):
    w, s, y, z, x, core, sign, pair = place_of()
    lane = iota((16, 128), 1) >> 5
    for out, k in zip(outs, shifts):
        at = (x + k) & 3
        packed = 0.0
        for c in range(2):
            rows = jnp.where(core == c, mine[...], got[...])
            for m in range(2):
                moved = pltpu.roll(rows[16 * m:16 * m + 16], (32 * (2 * c + m - at)) & 127, 1)
                packed = jnp.where(lane == 2 * c + m, moved, packed)
        out[...] = packed


def order(a):
    return a - 1 if 0 < a < 9 else 8 + a // 9


def detector_kernel(kernel, a0, a1, a2, a3, lenses, out, arrived, base, across, image, sems):
    w, s, y, z, x, core, sign, pair = place_of()
    for k, ref in enumerate((a0, a1, a2, a3)):
        for c in range(4):
            arrived[4 * ((x - k + 4) & 3) + c] = ref[...] if c == 0 else pltpu.roll(ref[...], 128 - 32 * c, 1)
    spot = (iota((128, 640), 0) == (iota((128, 640), 1) >> 5)) & (iota((128, 640), 1) < 18 * DPIX)
    spot = spot.astype(BF16)
    left, own, right = arrived[jnp.maximum(2 * w - 2, 0)], lenses[...], arrived[jnp.minimum(2 * w + 2, WAVES - 1)]
    lane = iota((16, 128), 1)
    tables = []
    for c in range(3):
        tables.append(
            jnp.where(
                lane == 0,
                pltpu.roll(left, 128 - 18 - c, 1),
                jnp.where(lane == 17, pltpu.roll(right, 128 - 4 - c, 1), pltpu.roll(own, 129 - 16 * c if c else 1, 1)),
            )
        )
    wide = dot(jnp.concatenate(tables, axis=0).astype(BF16), spot)
    row, column, count = wide[0:16] * 0.25, wide[16:32], wide[32:48]
    values = sum(dot(part, spot) for part in split2(arrived[...].reshape(WAVES * 16, 128)))
    offset = 0.5 * ((iota((16, 640), 1) & 31).astype(F32) - column)
    falling, rising = jnp.exp(-offset), jnp.exp(offset)
    spread = 0.0
    for wave in range(WAVES):
        value = values[16 * wave:16 * wave + 16]
        along = jnp.minimum(falling * math.exp(0.5 * wave), rising * math.exp(-0.5 * wave))
        spread = spread + jnp.where(count > wave, value, 0.0) * along
    within = iota((16, 512), 1) & 31
    moved = [pltpu.roll(spread, 640 - (30 + q), 1)[:, 0:512] for q in range(5)]
    inside = [(within + q - 2 >= 0) & (within + q - 2 < DPIX) for q in range(5)]
    own = [jnp.where(i, v, 0.0) for i, v in zip(inside, moved)]
    beside = [jnp.where(i, 0.0, v) for i, v in zip(inside, moved)]
    for p in range(5):
        weights = [kernel[p:p + 1, q:q + 1] + (1.0 if p == q == 2 else 0.0) for q in range(5)]
        base[p] = sum(v * k for v, k in zip(own, weights))
        base[5 + p] = sum(v * k for q, (v, k) in enumerate(zip(beside, weights)) if q != 2)
    near = row[:, DPIX:DPIX + 512]
    far = jnp.where(within < 2, pltpu.roll(row, 640 - 30, 1)[:, 0:512], pltpu.roll(row, 640 - 34, 1)[:, 0:512])
    for k, value in enumerate((near, -near, far, -far)):
        across[k] = jnp.exp(value)
    sub = iota((8, 128), 0)
    depth = sub.astype(F32) * 0.25
    downs = [jnp.exp(-(depth + 2.0 * t)) for t in range(4)]
    ups = [jnp.exp(depth + 2.0 * t) for t in range(4)]
    copies = []
    for lt in range(4):
        at = slice(128 * lt, 128 * lt + 128)
        state = None
        for a in range(10):
            r = order(a)
            scale = [base[p, r:r + 1, at] for p in range(10)]
            fall, rise, fall_far, rise_far = (across[k, r:r + 1, at] for k in range(4))
            for t in (3,) if a == 0 else (0,) if a == 9 else range(4):
                one = jnp.minimum(downs[t] * fall, ups[t] * rise)
                two = jnp.minimum(downs[t] * fall_far, ups[t] * rise_far)
                h = [one * scale[p] + two * scale[5 + p] for p in range(5)]
                if state is not None:
                    part, h0, h1, h3, h4 = state
                    done = part + pltpu.roll(jnp.where(sub == 0, h[3], h3), 7, 0)
                    done = done + pltpu.roll(jnp.where(sub < 2, h[4], h4), 6, 0)
                    image[lt, 8 * (4 * a + t - 4):8 * (4 * a + t - 4) + 8, :] = done
                    part = h[2] + pltpu.roll(jnp.where(sub >= 6, h0, h[0]), 2, 0)
                    part = part + pltpu.roll(jnp.where(sub == 7, h1, h[1]), 1, 0)
                else:
                    part = h[2]
                state = part, h[0], h[1], h[3], h[4]
        copies.append(pltpu.make_async_copy(image.at[lt, 8:264, :], out.at[:, at], sems.at[lt]))
        copies[-1].start()
    for copy in copies:
        copy.wait()


def call(kernel, outs, in_smem, n_in, scratch=(), tail=(), limit=40, outside=False):
    specs = [pl.BlockSpec(memory_space=pltpu.SMEM)] * in_smem
    specs += [pl.BlockSpec(memory_space=pltpu.VMEM)] * (n_in - in_smem)
    specs[n_in - len(tail):] = tail
    single = not isinstance(outs, (list, tuple))
    vmem = pl.BlockSpec(memory_space=pltpu.VMEM)
    return pl.pallas_call(
        kernel,
        out_shape=outs,
        in_specs=specs,
        out_specs=pl.BlockSpec(memory_space=pl.ANY) if outside else vmem if single else [vmem] * len(outs),
        scratch_shapes=list(scratch),
        compiler_params=pltpu.CompilerParams(vmem_limit_bytes=limit * 2**20),
        name=getattr(kernel, "func", kernel).__name__,
    )


def shape(*dims, dtype=F32):
    return jax.ShapeDtypeStruct(dims, dtype)


def along_z(k):
    return [(4 * y + z, 4 * y + (z + k) % 4) for y in range(4) for z in range(4)]


def along_y(other):
    return [(4 * y + z, 4 * other[y] + z) for y in range(4) for z in range(4)]


def body(amplitude, seg_map, seg_table, focal_mask, trace_row, trace_col, block_count, crosstalk):
    anywhere = [pl.BlockSpec(memory_space=pl.ANY)]
    piece, up, down, trace = call(
        prepare_kernel,
        [shape(PIECE, 128), shape(PIECE + EDGE, 128), shape(PIECE + EDGE, 128), shape(8, 128)],
        0,
        7,
        [
            pltpu.VMEM((ROWS, NP), F32),
            pltpu.VMEM((16, NP), I32),
            pltpu.VMEM((3, SEGMENTS), I32),
            pltpu.VMEM((3, 8, 16), I32),
            pltpu.VMEM((2, 8, NF), F32),
            pltpu.SemaphoreType.DMA((9,)),
        ],
        tail=anywhere * 7,
        limit=54,
    )(amplitude, seg_map, seg_table.T, focal_mask, trace_row, trace_col, block_count)
    utab = call(focal_table_kernel, shape(2, 4, 2 * UROWS, 256, dtype=BF16), 0, 1, tail=anywhere)(piece)
    p1 = lax.ppermute(up, "slab", along_z(1))
    p3 = lax.ppermute(down, "slab", along_z(3))
    p2 = lax.ppermute(piece, "slab", along_z(2))
    own, wrap = call(merge_kernel, [shape(2, MROWS, 128), shape(EDGE, 128)], 0, 5, tail=anywhere)(
        piece, p1, p2, p3, utab
    )
    vtab, smat = call(
        lens_table_kernel, [shape(2, 2, 2, HALF, FHALF, dtype=BF16), shape(NF, 256, dtype=BF16)], 0, 1, tail=anywhere
    )(own)
    partner = lax.ppermute(own, "slab", along_y((3, 2, 1, 0)))
    beside = lax.ppermute(own, "slab", along_y((1, 0, 3, 2)))
    last = lax.ppermute(own, "slab", along_y((2, 3, 0, 1)))
    edge = lax.ppermute(
        wrap, "slab", [(4 * y, 4 * y + 4) for y in range(3)] + [(4 * y + 7, 4 * y + 3) for y in range(3)]
    )
    scratch = [pltpu.VMEM((4, 256, 512), BF16)] * 2
    before = call(first_kernel, shape(4, UROWS, 512), 0, 4, scratch, tail=anywhere)(own, partner, utab, smat)
    keep, give = call(second_kernel, [shape(2, UROWS, 512)] * 2, 0, 5, scratch, tail=anywhere)(
        beside, last, utab, before, edge
    )
    weight, lenses = call(weight_kernel, [shape(UROWS, NF), shape(16, 128)], 0, 6, tail=anywhere)(
        focal_mask, p1, p3, edge, trace, give
    )
    sibling = [(i, i ^ 1) for i in range(NWAV)]
    crossed = lax.ppermute(give, "wav", sibling)
    mine, other = call(lens_kernel, [shape(32, 128)] * 2, 0, 6)(
        keep, crossed, vtab, weight, smat, lenses
    )
    got = lax.ppermute(other, "wav", sibling)
    def along_x(sent, k):
        return lax.ppermute(sent, "wav", [(i, (i + 2 * k) % NWAV) for i in range(NWAV)])

    (opposite,) = call(functools.partial(pack_kernel, shifts=(2,)), [shape(16, 128)], 0, 3, tail=anywhere)(mine, got, lenses)
    a2 = along_x(opposite, 2)
    kept, forth, back = call(functools.partial(pack_kernel, shifts=(0, 1, 3)), [shape(16, 128)] * 3, 0, 3, tail=anywhere)(
        mine, got, opposite
    )
    a1, a3 = along_x(forth, 1), along_x(back, 3)
    return call(
        detector_kernel,
        shape(256, 512),
        0,
        6,
        [
            pltpu.VMEM((WAVES, 16, 128), F32),
            pltpu.VMEM((10, 16, 512), F32),
            pltpu.VMEM((4, 16, 512), F32),
            pltpu.VMEM((4, 264, 128), F32),
            pltpu.SemaphoreType.DMA((4,)),
        ],
        outside=True,
    )(crosstalk, kept, a1, a2, a3, lenses)


def solution(mesh):
    return jax.shard_map(
        body,
        mesh=mesh,
        in_specs=(
            P("slab", None),
            P("slab", None),
            P(),
            P("slab", None),
            P("slab", "wav"),
            P("slab", "wav"),
            P("slab", "wav"),
            P(),
        ),
        out_specs=P("slab", "wav"),
        check_vma=False,
    )
```

```python
import functools
import math

import jax
import jax.numpy as jnp
import numpy as np
from jax import lax
from jax.experimental import pallas as pl
from jax.experimental.pallas import tpu as pltpu
from jax.sharding import PartitionSpec as P

F32, BF16, I32 = jnp.float32, jnp.bfloat16, jnp.int32

NP, NF, NL, DPIX, SEGMENTS, WAVES = 512, 1024, 128, 32, 798, 16
NWAV, NSLAB = 8, 16
ROWS = NP // NSLAB
FROWS = NF // NSLAB
UROWS = FROWS + 16
GROUP = 128
PIECE, EDGE = 2 * (ROWS + 8), 72
MROWS = GROUP + 8
HALF, FHALF = NP // 2, NF // 2

SIN = (6.283184916495428, -41.34158923268831, 81.59994332977429, -76.61447253115396, 41.34288235413569, -12.471243534350362)
COS = (0.9999999890590228, -19.73920449945383, 64.93911745989081, -85.45013953079767,
       60.167630950263465, -25.967599245923743, 6.52865815775625)


def place_of():
    w, s = lax.axis_index("wav").astype(I32), lax.axis_index("slab").astype(I32)
    y = s >> 2
    return w, s, y, s & 3, w >> 1, w & 1, jnp.where(y < 2, 1.0, -1.0), jnp.where((y == 0) | (y == 3), 0, 1)


def iota(shape, dim):
    return lax.broadcasted_iota(I32, shape, dim)


def dot(a, b):
    return jnp.dot(a, b, preferred_element_type=F32)


def split2(x):
    high = x.astype(BF16)
    return high, (x - high.astype(F32)).astype(BF16)


def split3(x):
    high = x.astype(BF16)
    rest = x - high.astype(F32)
    middle = rest.astype(BF16)
    return high, middle, (rest - middle.astype(F32)).astype(BF16)


def sincos(turns):
    t = turns - jnp.round(turns)
    z = t * t
    s, c = SIN[-1], COS[-1]
    for a in SIN[-2::-1]:
        s = s * z + a
    for b in COS[-2::-1]:
        c = c * z + b
    return s * t, c


def focal_row(s, shape):
    a = iota(shape, 0)
    r = (a - FROWS) >> 1
    own = 8 * (a & 7) + (a >> 3)
    return FROWS * s + jnp.where(a < FROWS, own, jnp.where((a & 1) == 0, r - 8, FROWS + r))


def reversal(n):
    return (iota((n, n), 0) + iota((n, n), 1) == n - 1).astype(BF16)


def prepare_kernel(amp_in, seg_in, tab_in, mask, trow, tcol, count, out, up, down, trace, amp, seg, tab, tables, edges, sems):
    w, s, y, z, x, core, sign, pair = place_of()
    copies = [
        pltpu.make_async_copy(a, b, sems.at[k])
        for k, (a, b) in enumerate(
            (
                (tab_in, tab),
                (seg_in.at[0:8, :], seg.at[0:8, :]),
                (seg_in.at[16:24, :], seg.at[8:16, :]),
                (amp_in, amp),
                (trow, tables.at[0]),
                (tcol, tables.at[1]),
                (count, tables.at[2]),
                (mask.at[FROWS - 8:FROWS, :], edges.at[0]),
                (mask.at[0:8, :], edges.at[1]),
            )
        )
    ]
    for copy in copies:
        copy.start()
    lower = y >= 2
    rows, cols = iota((ROWS, ROWS), 0), iota((ROWS, ROWS), 1)
    turned = (cols == jnp.where(lower, ROWS - 1 - rows, rows)).astype(BF16)
    rev = reversal(128)
    lane = iota((NP, 128), 1)
    pick = ((iota((NP, 128), 0) == 16 * (lane & 31)) & (lane < 96)).astype(BF16)
    out[...] = jnp.zeros((PIECE, 128), F32)
    for ref in (up, down):
        ref[PIECE + 64:PIECE + EDGE, :] = jnp.zeros((8, 128), F32)
    trace[...] = jnp.zeros((8, 128), F32)
    for copy in copies:
        copy.wait()
    for c in range(3):
        table = tables[c].astype(F32)
        trace[:, 16 * c:16 * c + 16] = table
        up[PIECE + 64:PIECE + 65, 16 * c:16 * c + 16] = table[7:8]
        down[PIECE + 64:PIECE + 65, 16 * c:16 * c + 16] = table[0:1]
    ids = dot(jnp.concatenate(split2(seg[...].astype(F32)), axis=0), pick)
    ids = ids[0:16] + ids[16:32]
    upper_ids, lower_ids = ids[0:1], ids[8:9]
    ids = jnp.concatenate(
        [jnp.where(lower, lower_ids, upper_ids), jnp.where(lower, upper_ids, lower_ids)], axis=1
    )
    which = iota((SEGMENTS, 256), 0).astype(F32)
    table = jnp.concatenate([tab[...].astype(F32), jnp.zeros((5, SEGMENTS), F32)], axis=0)
    found = dot(jnp.concatenate(split2(table), axis=0), (which == ids).astype(BF16))
    found = found[0:3] + found[8:11]
    found = jnp.sum(jnp.where(iota((3, 256), 0) == (iota((3, 256), 1) & 127) >> 5, found, 0.0), axis=0, keepdims=True)
    for k in range(2):
        out[ROWS + k:ROWS + k + 1, :] = found[:, 128 * k:128 * k + 128]
    first = core == 0
    left = jnp.where(first, amp[:, 0:128], amp[:, 128:256])
    right = jnp.where(first, amp[:, 384:512], amp[:, 256:384])
    right = dot(jnp.concatenate(split3(right), axis=0), rev).astype(BF16)
    parts = list(split3(left)) + [right[ROWS * k:ROWS * k + ROWS] for k in range(3)]
    found = dot(turned, jnp.concatenate(parts, axis=1))
    for k in range(2):
        out[(ROWS + 8) * k:(ROWS + 8) * k + ROWS, :] = sum(found[:, 128 * q:128 * q + 128] for q in range(3 * k, 3 * k + 3))
    for k, ref in enumerate((up, down)):
        ref[0:PIECE, :] = out[...]
        for q in range(8):
            ref[PIECE + 8 * q:PIECE + 8 * q + 8, :] = edges[k, :, 128 * q:128 * q + 128]


def place_pieces(out, pieces):
    w, s, y, z, x, core, sign, pair = place_of()
    for k, piece in pieces:
        source = lax.rem(z - k + 4, 4)
        place = jnp.where(y >= 2, 3 - source, source)
        for at in range(4):

            @pl.when(place == at)
            def _(at=at, piece=piece):
                for t in range(2):
                    for b in range(2):
                        r0 = (ROWS + 8) * t + 16 * b
                        out[pl.ds(MROWS * t + 2 * at + b, 16, stride=8), :] = piece[r0:r0 + 16, :]
                out[GROUP + 2 * at:GROUP + 2 * at + 2, :] = piece[ROWS:ROWS + 2, :]


def opposite_kernel(p0, p2, after, out):
    del after
    out[GROUP:MROWS, :] = jnp.zeros((8, 128), F32)
    out[MROWS + GROUP:2 * MROWS, :] = jnp.zeros((8, 128), F32)
    place_pieces(out, ((0, p0), (2, p2)))


def merge_kernel(begun, p1, p3, out, more):
    del begun
    w, s, y, z, x, core, sign, pair = place_of()
    place_pieces(out, ((1, p1), (3, p3)))
    more[0:2 * MROWS, :] = out[...]
    more[2 * MROWS:2 * MROWS + EDGE, :] = jnp.where(z == 0, p1[PIECE:PIECE + EDGE, :], p3[PIECE:PIECE + EDGE, :])


def wavelength(w):
    return jnp.full((1, 1), 1000 + w, I32).astype(F32)


def slope(n, w):
    lam = wavelength(w)
    short = jnp.round(250.0 / lam * 2.0**14) * 2.0**-14
    rest = (250.0 - short * lam) / lam
    whole = n * (short * 2.0**-10)
    high = jnp.round(whole * 2.0**13) * 2.0**-13
    return high, (whole - high) + n * (rest * 2.0**-10)


def angle(m, step):
    t = m * step[0]
    t = t - jnp.round(t)
    return sincos(t + m * step[1])


def odd(index, count):
    return (2 * index + 1 - count).astype(F32)


def table_kernel(after, utab, vtab, spot):
    del after
    w, s, y, z, x, core, sign, pair = place_of()
    row, lane = iota((128, 768), 0), iota((128, 768), 1)
    block = 8 * core + ((lane & 127) >> 4)
    spot[...] = (row == 32 * (lane >> 8) + jnp.where((lane & 128) == 0, block, 31 - block)).astype(BF16)
    m = odd(focal_row(s, (UROWS, GROUP)), NF)
    rho = iota((1, GROUP), 1)
    for k in range(4):
        wave = 2 * (w if k < 2 else w ^ 1) + (k & 1)
        for p in range(2):
            g = pair if p == 0 else 1 - pair
            sin, cos = angle(m, slope(odd(128 * g + 16 * (rho & 7) + (rho >> 3), NP), wave))
            sin = sin * sign
            for r0, at, part in ((0, 0, cos), (0, GROUP, sin), (UROWS, 0, -sin), (UROWS, GROUP, cos)):
                high, low = split2(part)
                utab[p, k, r0:r0 + UROWS, at:at + GROUP] = high
                utab[p, k, r0 + 2 * UROWS:r0 + 3 * UROWS, at:at + GROUP] = low
    m = odd(iota((16, 128), 1), NF)
    for k in range(2):

        def chunk(c, carry, k=k):
            j0 = pl.multiple_of(16 * c, 16)
            step = slope(odd(((j0 + 128 * core) & 255) + iota((16, 128), 0), NP), 2 * w + k)
            sin, cos = angle(m, step)
            turn_im, turn_re = angle(jnp.full((16, 128), 256.0, F32), step)
            for t in range(4):
                for q, part in ((0, cos), (1, sin)):
                    high, low = split2(part)
                    vtab[k, q, 0, pl.ds(j0, 16), 128 * t:128 * t + 128] = high
                    vtab[k, q, 1, pl.ds(j0, 16), 128 * t:128 * t + 128] = low
                cos, sin = cos * turn_re - sin * turn_im, cos * turn_im + sin * turn_re
            return carry

        lax.fori_loop(0, HALF // 16, chunk, 0)


def weight_kernel(mask, p1, p3, partner, beside, trace, after, weight, lenses, smat, full):
    del after
    w, s, y, z, x, core, sign, pair = place_of()
    rows = slice(2 * MROWS, 2 * MROWS + EDGE)
    across = jnp.where(jnp.where(z == 0, y == 2, y == 1), partner[rows, :], beside[rows, :])
    across = jnp.where(jnp.where(z == 0, y == 0, y == 3), 0.0, across)
    above = jnp.where(z == 0, across, p1[PIECE:PIECE + EDGE, :])
    below = jnp.where(z == 3, across, p3[PIECE:PIECE + EDGE, :])
    lenses[0:8, :] = trace[...]
    lenses[8:9, :] = above[64:65]
    lenses[9:10, :] = below[64:65]
    lenses[10:16, :] = jnp.zeros((6, 128), F32)
    u = focal_row(s, (UROWS, FHALF))
    v = iota((UROWS, FHALF), 1)
    down, across = (2 * u + 1 - NF).astype(F32) * 0.5, (2 * v + 1 - NF).astype(F32) * 0.5
    fade = 1.0 - jnp.exp((down * down + across * across) * (-1.0 / 1024.0))
    rev = reversal(256)
    for q in range(8):
        for a in range(8):
            full[q, pl.ds(a, 8, stride=8), :] = mask[8 * a:8 * a + 8, 128 * q:128 * q + 128]
        full[q, pl.ds(FROWS, 8, stride=2), :] = above[8 * q:8 * q + 8]
        full[q, pl.ds(FROWS + 1, 8, stride=2), :] = below[8 * q:8 * q + 8]
    t = jnp.concatenate([full[q] for q in range(4)], axis=1) * fade
    weight[:, :FHALF] = t * t * 2.0**-24
    for q in range(2):
        flipped = sum(dot(part, rev) for part in split3(jnp.concatenate([full[6 - 2 * q], full[7 - 2 * q]], axis=1)))
        t = flipped * fade[:, 256 * q:256 * (q + 1)]
        weight[:, FHALF + 256 * q:FHALF + 256 * (q + 1)] = t * t * 2.0**-24
    row, lane = iota((FHALF, 256), 0), iota((FHALF, 256), 1)
    column = 2 * ((lane >> 5) & 3) + jnp.where(lane < 128, core, 1 - core)
    lens = jnp.where((lane & 31) < 18, 16 * column - 1 + (lane & 31), -1)
    smat[0:FHALF, :] = (lens == row >> 3).astype(BF16)
    smat[FHALF:NF, :] = (lens == NL - 1 - (row >> 3)).astype(BF16)


def group_kernel(ref, utab, spot, *refs, p, flipped):
    before = refs[0] if flipped or p else None
    outs, (whi, wlo) = refs[before is not None:-2], refs[-2:]
    w, s, y, z, x, core, sign, pair = place_of()
    g = pair if p == 0 else 1 - pair
    turned = -1.0 if flipped else 1.0
    coef = jnp.concatenate(split2(ref[GROUP:MROWS, :]), axis=0)
    both = dot(coef, spot[...])
    coef = both[0:8] + both[8:16]
    down = odd(16 * (8 * g + iota((8, 128), 0)), NP) * (1.0 / 1024.0)
    across = odd(128 * core + iota((8, 128), 1), NP) * (1.0 / 1024.0)
    paths, steps = [], []
    for side in range(2):
        piston, tip, tilt = (coef[:, 256 * c + 128 * side:256 * c + 128 * side + 128] for c in range(3))
        tilt = (sign * turned) * tilt
        paths.append(piston + (across if side == 0 else -across) * tip + tilt * down)
        steps.append(tilt * (1.0 / 512.0))
    for m in range(4):
        inverse = 1.0 / wavelength(2 * (w if m < 2 else w ^ 1) + (m & 1))
        im, re = zip(*(sincos(path * (turned * inverse)) for path in paths))
        step_im, step_re = zip(*(sincos(step * (turned * inverse)) for step in steps))
        for r2 in range(8):
            found = [[] for _ in range(4)]
            for h in range(2):
                r0 = 16 * r2 + 8 * h
                for side in range(2):
                    a = ref[MROWS * side + r0:MROWS * side + r0 + 8, :]
                    found[side].append(a * re[side])
                    found[2 + side].append(a * im[side])
                re, im = (
                    [a * p - b * q for a, b, p, q in zip(re, im, step_re, step_im)],
                    [a * q + b * p for a, b, p, q in zip(re, im, step_re, step_im)],
                )
            for k, values in enumerate(found):
                high, low = split2(jnp.concatenate(values, axis=0))
                r0, c0 = GROUP * (k >> 1) + 16 * r2, 128 * (k & 1)
                whi[m, r0:r0 + 16, c0:c0 + 128] = high
                wlo[m, r0:r0 + 16, c0:c0 + 128] = low
    for m in range(4):
        table = utab[p, m]
        both = dot(table, whi[m])
        field = both[:2 * UROWS] + both[2 * UROWS:] + dot(table[:2 * UROWS], wlo[m])
        out = outs[0].at[m] if len(outs) == 1 else outs[m >> 1].at[m & 1]
        if before is None:
            out[...] = field
        elif flipped:
            out[0:UROWS] = before[m, 0:UROWS] + field[:UROWS]
            out[UROWS:2 * UROWS] = before[m, UROWS:2 * UROWS] - field[UROWS:]
        else:
            out[...] = before[m] + field


def lens_kernel(keep, got, vtab, weight, smat, lenses, mine, other):
    parts = []
    for m in range(2):
        left, right = (
            jnp.concatenate([ref[m, :, 128 * q:128 * q + 128] for ref in (keep, got)], axis=1) for q in range(2)
        )
        odd_part = left - right
        sides = left + right, jnp.concatenate([odd_part[UROWS:], -odd_part[:UROWS]], axis=0)
        terms = []
        for q, side in enumerate(sides):
            high, low = split2(side)
            both = dot(jnp.concatenate([high, low], axis=0), vtab[m, q, 0])
            terms.append(both[:2 * UROWS] + both[2 * UROWS:] + dot(high, vtab[m, q, 1]))
        summed = []
        for q, value in enumerate((terms[0] + terms[1], terms[0] - terms[1])):
            re, im = value[:UROWS], value[UROWS:]
            power = (re * re + im * im) * weight[:, FHALF * q:FHALF * (q + 1)]
            edges = power[FROWS:FROWS + 8] + power[FROWS + 8:]
            edges = edges + pltpu.roll(edges, 4, 0)
            edges = edges + pltpu.roll(edges, 2, 0)
            summed.append(jnp.concatenate([sum(power[8 * r:8 * r + 8] for r in range(8)), edges], axis=0))
        parts.extend(split2(jnp.concatenate(summed, axis=1)))
    lens = dot(jnp.concatenate(parts, axis=0), smat[...])
    for m in range(2):
        for k, out in enumerate((mine, other)):
            at = slice(128 * k, 128 * k + 128)
            out[16 * m:16 * m + 16, :] = lens[32 * m:32 * m + 16, at] + lens[32 * m + 16:32 * m + 32, at]
    row, lane = iota((128, 128), 0), iota((128, 128), 1) & 31
    spot = ((lane >= 18) & (lane < 21) & (row == 16 * (lane - 18) + 15)) | ((lane >= 21) & (lane < 24) & (row == 16 * (lane - 21)))
    sides = dot(lenses[...].astype(BF16), spot.astype(BF16))
    for out in (mine, other):
        out[0:16, :] += sides


def pack_kernel(mine, got, after, *outs, shifts):
    w, s, y, z, x, core, sign, pair = place_of()
    lane = iota((16, 128), 1) >> 5
    for out, k in zip(outs, shifts):
        at = (x + k) & 3
        packed = 0.0
        for c in range(2):
            rows = jnp.where(core == c, mine[...], got[...])
            for m in range(2):
                moved = pltpu.roll(rows[16 * m:16 * m + 16], (32 * (2 * c + m - at)) & 127, 1)
                packed = jnp.where(lane == 2 * c + m, moved, packed)
        out[...] = packed


def unpack_kernel(a0, a2, out):
    for k, ref in enumerate((a0, a2)):
        for c in range(4):
            out[4 * k + c] = ref[...] if c == 0 else pltpu.roll(ref[...], 128 - 32 * c, 1)


def order(a):
    return a - 1 if 0 < a < 9 else 8 + a // 9


def detector_kernel(kernel, begun, a1, a3, lenses, out, arrived, base, across, image, sems):
    w, s, y, z, x, core, sign, pair = place_of()
    for k, ref in ((1, a1), (3, a3)):
        for c in range(4):
            arrived[4 * ((x - k + 4) & 3) + c] = ref[...] if c == 0 else pltpu.roll(ref[...], 128 - 32 * c, 1)
    for k in (0, 2):
        for c in range(4):
            arrived[4 * ((x - k + 4) & 3) + c] = begun[2 * k + c]
    spot = (iota((128, 640), 0) == (iota((128, 640), 1) >> 5)) & (iota((128, 640), 1) < 18 * DPIX)
    spot = spot.astype(BF16)
    left, own, right = arrived[jnp.maximum(2 * w - 2, 0)], lenses[...], arrived[jnp.minimum(2 * w + 2, WAVES - 1)]
    lane = iota((16, 128), 1)
    tables = []
    for c in range(3):
        tables.append(
            jnp.where(
                lane == 0,
                pltpu.roll(left, 128 - 18 - c, 1),
                jnp.where(lane == 17, pltpu.roll(right, 128 - 4 - c, 1), pltpu.roll(own, 129 - 16 * c if c else 1, 1)),
            )
        )
    parts = list(split2(arrived[...].reshape(WAVES * 16, 128)))
    wide = dot(jnp.concatenate(parts + [jnp.concatenate(tables, axis=0).astype(BF16)], axis=0), spot)
    values, tables = wide[:16 * WAVES] + wide[16 * WAVES:32 * WAVES], wide[32 * WAVES:]
    row, column, count = tables[0:16] * 0.25, tables[16:32], tables[32:48]
    offset = 0.5 * ((iota((16, 640), 1) & 31).astype(F32) - column)
    falling, rising = jnp.exp(-offset), jnp.exp(offset)
    spread = 0.0
    for wave in range(WAVES):
        value = values[16 * wave:16 * wave + 16]
        along = jnp.minimum(falling * math.exp(0.5 * wave), rising * math.exp(-0.5 * wave))
        spread = spread + jnp.where(count > wave, value, 0.0) * along
    within = iota((16, 512), 1) & 31
    moved = [pltpu.roll(spread, 640 - (30 + q), 1)[:, 0:512] for q in range(5)]
    inside = [(within + q - 2 >= 0) & (within + q - 2 < DPIX) for q in range(5)]
    own = [jnp.where(i, v, 0.0) for i, v in zip(inside, moved)]
    beside = [jnp.where(i, 0.0, v) for i, v in zip(inside, moved)]
    for p in range(5):
        weights = [kernel[p:p + 1, q:q + 1] + (1.0 if p == q == 2 else 0.0) for q in range(5)]
        base[p] = sum(v * k for v, k in zip(own, weights))
        base[5 + p] = sum(v * k for q, (v, k) in enumerate(zip(beside, weights)) if q != 2)
    near = row[:, DPIX:DPIX + 512]
    far = jnp.where(within < 2, pltpu.roll(row, 640 - 30, 1)[:, 0:512], pltpu.roll(row, 640 - 34, 1)[:, 0:512])
    for k, value in enumerate((near, -near, far, -far)):
        across[k] = jnp.exp(value)
    sub = iota((8, 128), 0)
    depth = sub.astype(F32) * 0.25
    downs = [jnp.exp(-(depth + 2.0 * t)) for t in range(4)]
    ups = [jnp.exp(depth + 2.0 * t) for t in range(4)]
    copies = []
    for lt in range(4):
        at = slice(128 * lt, 128 * lt + 128)
        state = None
        for a in range(10):
            r = order(a)
            scale = [base[p, r:r + 1, at] for p in range(10)]
            fall, rise, fall_far, rise_far = (across[k, r:r + 1, at] for k in range(4))
            for t in (3,) if a == 0 else (0,) if a == 9 else range(4):
                one = jnp.minimum(downs[t] * fall, ups[t] * rise)
                two = jnp.minimum(downs[t] * fall_far, ups[t] * rise_far)
                h = [one * scale[p] + two * scale[5 + p] for p in range(5)]
                if state is not None:
                    part, h0, h1, h3, h4 = state
                    done = part + pltpu.roll(jnp.where(sub == 0, h[3], h3), 7, 0)
                    done = done + pltpu.roll(jnp.where(sub < 2, h[4], h4), 6, 0)
                    image[lt, 8 * (4 * a + t - 4):8 * (4 * a + t - 4) + 8, :] = done
                    part = h[2] + pltpu.roll(jnp.where(sub >= 6, h0, h[0]), 2, 0)
                    part = part + pltpu.roll(jnp.where(sub == 7, h1, h[1]), 1, 0)
                else:
                    part = h[2]
                state = part, h[0], h[1], h[3], h[4]
        copies.append(pltpu.make_async_copy(image.at[lt, 8:264, :], out.at[:, at], sems.at[lt]))
        copies[-1].start()
    for copy in copies:
        copy.wait()


def call(kernel, outs, in_smem, n_in, scratch=(), tail=(), limit=40, outside=False, aliases=None):
    specs = [pl.BlockSpec(memory_space=pltpu.SMEM)] * in_smem
    specs += [pl.BlockSpec(memory_space=pltpu.VMEM)] * (n_in - in_smem)
    specs[n_in - len(tail):] = tail
    single = not isinstance(outs, (list, tuple))
    vmem = pl.BlockSpec(memory_space=pltpu.VMEM)
    return pl.pallas_call(
        kernel,
        out_shape=outs,
        in_specs=specs,
        out_specs=pl.BlockSpec(memory_space=pl.ANY) if outside else vmem if single else [vmem] * len(outs),
        scratch_shapes=list(scratch),
        input_output_aliases=aliases or {},
        compiler_params=pltpu.CompilerParams(vmem_limit_bytes=limit * 2**20),
        name=getattr(kernel, "func", kernel).__name__,
    )


def shape(*dims, dtype=F32):
    return jax.ShapeDtypeStruct(dims, dtype)


def along_z(k):
    return [(4 * y + z, 4 * y + (z + k) % 4) for y in range(4) for z in range(4)]


def along_y(other):
    return [(4 * y + z, 4 * other[y] + z) for y in range(4) for z in range(4)]


def body(amplitude, seg_map, seg_table, focal_mask, trace_row, trace_col, block_count, crosstalk):
    anywhere = [pl.BlockSpec(memory_space=pl.ANY)]
    piece, up, down, trace = call(
        prepare_kernel,
        [shape(PIECE, 128), shape(PIECE + EDGE, 128), shape(PIECE + EDGE, 128), shape(8, 128)],
        0,
        7,
        [
            pltpu.VMEM((ROWS, NP), F32),
            pltpu.VMEM((16, NP), I32),
            pltpu.VMEM((3, SEGMENTS), I32),
            pltpu.VMEM((3, 8, 16), I32),
            pltpu.VMEM((2, 8, NF), F32),
            pltpu.SemaphoreType.DMA((9,)),
        ],
        tail=anywhere * 7,
        limit=54,
    )(amplitude, seg_map, seg_table.T, focal_mask, trace_row, trace_col, block_count)
    utab, vtab, spot = call(
        table_kernel,
        [shape(2, 4, 4 * UROWS, 256, dtype=BF16), shape(2, 2, 2, HALF, FHALF, dtype=BF16), shape(128, 768, dtype=BF16)],
        0,
        1,
        tail=anywhere,
    )(piece)
    p1 = lax.ppermute(up, "slab", along_z(1))
    p3 = lax.ppermute(down, "slab", along_z(3))
    p2 = lax.ppermute(piece, "slab", along_z(2))
    begun = call(opposite_kernel, shape(2 * MROWS, 128), 0, 3, tail=anywhere)(piece, p2, utab)
    own, more = call(
        merge_kernel, [shape(2 * MROWS, 128), shape(2 * MROWS + EDGE, 128)], 0, 3, aliases={0: 0}
    )(begun, p1, p3)
    partner = lax.ppermute(more, "slab", along_y((3, 2, 1, 0)))
    beside = lax.ppermute(more, "slab", along_y((1, 0, 3, 2)))
    last = lax.ppermute(own, "slab", along_y((2, 3, 0, 1)))
    scratch = [pltpu.VMEM((4, 256, 256), BF16)] * 2

    def add(group, p, flipped, *before, outs=shape(4, 2 * UROWS, 256), **options):
        kernel = functools.partial(group_kernel, p=p, flipped=flipped)
        return call(kernel, outs, 0, 3 + len(before), scratch, **options)(group, utab, spot, *before)

    field = add(own, 0, False)
    field = add(partner, 0, True, field)
    field = add(beside, 1, False, field)
    keep, give = add(last, 1, True, field, outs=[shape(2, 2 * UROWS, 256)] * 2)
    weight, lenses, smat = call(
        weight_kernel,
        [shape(UROWS, NF), shape(16, 128), shape(NF, 256, dtype=BF16)],
        0,
        7,
        [pltpu.VMEM((8, UROWS, 128), F32)],
        tail=anywhere,
    )(focal_mask, p1, p3, partner, beside, trace, give)
    sibling = [(i, i ^ 1) for i in range(NWAV)]
    crossed = lax.ppermute(give, "wav", sibling)
    mine, other = call(lens_kernel, [shape(32, 128)] * 2, 0, 6)(
        keep, crossed, vtab, weight, smat, lenses
    )
    got = lax.ppermute(other, "wav", sibling)
    def along_x(sent, k):
        return lax.ppermute(sent, "wav", [(i, (i + 2 * k) % NWAV) for i in range(NWAV)])

    (opposite,) = call(functools.partial(pack_kernel, shifts=(2,)), [shape(16, 128)], 0, 3, tail=anywhere)(mine, got, lenses)
    a2 = along_x(opposite, 2)
    kept, forth, back = call(functools.partial(pack_kernel, shifts=(0, 1, 3)), [shape(16, 128)] * 3, 0, 3, tail=anywhere)(
        mine, got, opposite
    )
    a1, a3 = along_x(forth, 1), along_x(back, 3)
    begun = call(unpack_kernel, shape(8, 16, 128), 0, 2)(kept, a2)
    return call(
        detector_kernel,
        shape(256, 512),
        0,
        5,
        [
            pltpu.VMEM((WAVES, 16, 128), F32),
            pltpu.VMEM((10, 16, 512), F32),
            pltpu.VMEM((4, 16, 512), F32),
            pltpu.VMEM((4, 264, 128), F32),
            pltpu.SemaphoreType.DMA((4,)),
        ],
        outside=True,
    )(crosstalk, begun, a1, a3, lenses)


def solution(mesh):
    return jax.shard_map(
        body,
        mesh=mesh,
        in_specs=(
            P("slab", None),
            P("slab", None),
            P(),
            P("slab", None),
            P("slab", "wav"),
            P("slab", "wav"),
            P("slab", "wav"),
            P(),
        ),
        out_specs=P("slab", "wav"),
        check_vma=False,
    )
```

```python
import functools
import math

import jax
import jax.numpy as jnp
import numpy as np
from jax import lax
from jax.experimental import pallas as pl
from jax.experimental.pallas import tpu as pltpu
from jax.sharding import PartitionSpec as P

F32, BF16, I32 = jnp.float32, jnp.bfloat16, jnp.int32

NP, NF, NL, DPIX, SEGMENTS, WAVES = 512, 1024, 128, 32, 798, 16
NWAV, NSLAB = 8, 16
ROWS = NP // NSLAB
FROWS = NF // NSLAB
UROWS = FROWS + 16
GROUP = 128
PIECE, EDGE = 2 * (ROWS + 8), 40
MROWS = GROUP + 8
HALF, FHALF = NP // 2, NF // 2

SIN = (6.283184916495428, -41.34158923268831, 81.59994332977429, -76.61447253115396, 41.34288235413569, -12.471243534350362)
COS = (0.9999999890590228, -19.73920449945383, 64.93911745989081, -85.45013953079767,
       60.167630950263465, -25.967599245923743, 6.52865815775625)


def place_of():
    w, s = lax.axis_index("wav").astype(I32), lax.axis_index("slab").astype(I32)
    y = s >> 2
    return w, s, y, s & 3, w >> 1, w & 1, jnp.where(y < 2, 1.0, -1.0), jnp.where((y == 0) | (y == 3), 0, 1)


def iota(shape, dim):
    return lax.broadcasted_iota(I32, shape, dim)


def dot(a, b):
    return jnp.dot(a, b, preferred_element_type=F32)


def split2(x):
    high = x.astype(BF16)
    return high, (x - high.astype(F32)).astype(BF16)


def split3(x):
    high = x.astype(BF16)
    rest = x - high.astype(F32)
    middle = rest.astype(BF16)
    return high, middle, (rest - middle.astype(F32)).astype(BF16)


def sincos(turns):
    t = turns - jnp.round(turns)
    z = t * t
    s, c = SIN[-1], COS[-1]
    for a in SIN[-2::-1]:
        s = s * z + a
    for b in COS[-2::-1]:
        c = c * z + b
    return s * t, c


def focal_row(s, shape):
    a = iota(shape, 0)
    r = (a - FROWS) >> 1
    own = 8 * (a & 7) + (a >> 3)
    return FROWS * s + jnp.where(a < FROWS, own, jnp.where((a & 1) == 0, r - 8, FROWS + r))


def reversal(n):
    return (iota((n, n), 0) + iota((n, n), 1) == n - 1).astype(BF16)


def prepare_kernel(amp_in, seg_in, tab_in, mask, trow, tcol, count, out, up, down, trace, amp, seg, tab, tables, edges, sems):
    w, s, y, z, x, core, sign, pair = place_of()
    half = pl.ds(pl.multiple_of(FHALF * core, FHALF), FHALF)
    copies = [
        pltpu.make_async_copy(a, b, sems.at[k])
        for k, (a, b) in enumerate(
            (
                (tab_in, tab),
                (seg_in.at[0:8, :], seg.at[0:8, :]),
                (seg_in.at[16:24, :], seg.at[8:16, :]),
                (amp_in, amp),
                (trow, tables.at[0]),
                (tcol, tables.at[1]),
                (count, tables.at[2]),
                (mask.at[FROWS - 8:FROWS, half], edges.at[0]),
                (mask.at[0:8, half], edges.at[1]),
            )
        )
    ]
    for copy in copies:
        copy.start()
    lower = y >= 2
    rows, cols = iota((ROWS, ROWS), 0), iota((ROWS, ROWS), 1)
    turned = (cols == jnp.where(lower, ROWS - 1 - rows, rows)).astype(BF16)
    rev = reversal(128)
    lane = iota((NP, 128), 1)
    pick = ((iota((NP, 128), 0) == 16 * (lane & 31)) & (lane < 96)).astype(BF16)
    out[...] = jnp.zeros((PIECE, 128), F32)
    for ref in (up, down):
        ref[PIECE + 32:PIECE + EDGE, :] = jnp.zeros((8, 128), F32)
    trace[...] = jnp.zeros((8, 128), F32)
    for copy in copies:
        copy.wait()
    for c in range(3):
        table = tables[c].astype(F32)
        trace[:, 16 * c:16 * c + 16] = table
        up[PIECE + 32:PIECE + 33, 16 * c:16 * c + 16] = table[7:8]
        down[PIECE + 32:PIECE + 33, 16 * c:16 * c + 16] = table[0:1]
    ids = dot(jnp.concatenate(split2(seg[...].astype(F32)), axis=0), pick)
    ids = ids[0:16] + ids[16:32]
    upper_ids, lower_ids = ids[0:1], ids[8:9]
    ids = jnp.concatenate(
        [jnp.where(lower, lower_ids, upper_ids), jnp.where(lower, upper_ids, lower_ids)], axis=1
    )
    which = iota((SEGMENTS, 256), 0).astype(F32)
    table = jnp.concatenate([tab[...].astype(F32), jnp.zeros((5, SEGMENTS), F32)], axis=0)
    found = dot(jnp.concatenate(split2(table), axis=0), (which == ids).astype(BF16))
    found = found[0:3] + found[8:11]
    found = jnp.sum(jnp.where(iota((3, 256), 0) == (iota((3, 256), 1) & 127) >> 5, found, 0.0), axis=0, keepdims=True)
    for k in range(2):
        out[ROWS + k:ROWS + k + 1, :] = found[:, 128 * k:128 * k + 128]
    first = core == 0
    left = jnp.where(first, amp[:, 0:128], amp[:, 128:256])
    right = jnp.where(first, amp[:, 384:512], amp[:, 256:384])
    right = dot(jnp.concatenate(split3(right), axis=0), rev).astype(BF16)
    parts = list(split3(left)) + [right[ROWS * k:ROWS * k + ROWS] for k in range(3)]
    found = dot(turned, jnp.concatenate(parts, axis=1))
    for k in range(2):
        out[(ROWS + 8) * k:(ROWS + 8) * k + ROWS, :] = sum(found[:, 128 * q:128 * q + 128] for q in range(3 * k, 3 * k + 3))
    for k, ref in enumerate((up, down)):
        ref[0:PIECE, :] = out[...]
        for q in range(4):
            ref[PIECE + 8 * q:PIECE + 8 * q + 8, :] = edges[k, :, 128 * q:128 * q + 128]


def place_pieces(out, pieces):
    w, s, y, z, x, core, sign, pair = place_of()
    for k, piece in pieces:
        source = lax.rem(z - k + 4, 4)
        place = jnp.where(y >= 2, 3 - source, source)
        for at in range(4):

            @pl.when(place == at)
            def _(at=at, piece=piece):
                for t in range(2):
                    for b in range(2):
                        r0 = (ROWS + 8) * t + 16 * b
                        out[pl.ds(MROWS * t + 2 * at + b, 16, stride=8), :] = piece[r0:r0 + 16, :]
                out[GROUP + 2 * at:GROUP + 2 * at + 2, :] = piece[ROWS:ROWS + 2, :]


def opposite_kernel(p0, p2, after, out):
    del after
    out[GROUP:MROWS, :] = jnp.zeros((8, 128), F32)
    out[MROWS + GROUP:2 * MROWS, :] = jnp.zeros((8, 128), F32)
    place_pieces(out, ((0, p0), (2, p2)))


def merge_kernel(begun, p1, p3, out, more):
    del begun
    w, s, y, z, x, core, sign, pair = place_of()
    place_pieces(out, ((1, p1), (3, p3)))
    more[0:2 * MROWS, :] = out[...]
    wrap = jnp.where(z == 0, p1[PIECE:PIECE + EDGE, :], p3[PIECE:PIECE + EDGE, :])
    more[2 * MROWS:2 * MROWS + 32, :] = wrap[0:32]
    more[MROWS + GROUP:2 * MROWS, :] = wrap[32:EDGE]


def wavelength(w):
    return jnp.full((1, 1), 1000 + w, I32).astype(F32)


def slope(n, w):
    lam = wavelength(w)
    short = jnp.round(250.0 / lam * 2.0**14) * 2.0**-14
    rest = (250.0 - short * lam) / lam
    whole = n * (short * 2.0**-10)
    high = jnp.round(whole * 2.0**13) * 2.0**-13
    return high, (whole - high) + n * (rest * 2.0**-10)


def angle(m, step):
    t = m * step[0]
    t = t - jnp.round(t)
    return sincos(t + m * step[1])


def odd(index, count):
    return (2 * index + 1 - count).astype(F32)


def table_kernel(after, utab, vtab, spot):
    del after
    w, s, y, z, x, core, sign, pair = place_of()
    row, lane = iota((128, 768), 0), iota((128, 768), 1)
    block = 8 * core + ((lane & 127) >> 4)
    spot[...] = (row == 32 * (lane >> 8) + jnp.where((lane & 128) == 0, block, 31 - block)).astype(BF16)
    m = odd(focal_row(s, (UROWS, GROUP)), NF)
    rho = iota((1, GROUP), 1)
    for k in range(4):
        wave = 2 * (w if k < 2 else w ^ 1) + (k & 1)
        for p in range(2):
            g = pair if p == 0 else 1 - pair
            sin, cos = angle(m, slope(odd(128 * g + 16 * (rho & 7) + (rho >> 3), NP), wave))
            sin = sin * sign
            for r0, at, part in ((0, 0, cos), (0, GROUP, sin), (UROWS, 0, -sin), (UROWS, GROUP, cos)):
                high, low = split2(part)
                utab[p, k, r0:r0 + UROWS, at:at + GROUP] = high
                utab[p, k, r0 + 2 * UROWS:r0 + 3 * UROWS, at:at + GROUP] = low
    m = odd(iota((16, 128), 1), NF)
    for k in range(2):

        def chunk(c, carry, k=k):
            j0 = pl.multiple_of(16 * c, 16)
            step = slope(odd(((j0 + 128 * core) & 255) + iota((16, 128), 0), NP), 2 * w + k)
            sin, cos = angle(m, step)
            turn_im, turn_re = angle(jnp.full((16, 128), 256.0, F32), step)
            for t in range(4):
                for q, part in ((0, cos), (1, sin)):
                    high, low = split2(part)
                    vtab[k, q, 0, pl.ds(j0, 16), 128 * t:128 * t + 128] = high
                    vtab[k, q, 1, pl.ds(j0, 16), 128 * t:128 * t + 128] = low
                cos, sin = cos * turn_re - sin * turn_im, cos * turn_im + sin * turn_re
            return carry

        lax.fori_loop(0, HALF // 16, chunk, 0)


def flipped_columns(x):
    rev = reversal(256)
    n = x.shape[1] // 256
    parts = [jnp.concatenate(split3(x[:, 256 * q:256 * q + 256]), axis=0) for q in range(n)]
    rows, found = x.shape[0], [dot(part, rev) for part in reversed(parts)]
    return jnp.concatenate([f[:rows] + f[rows:2 * rows] + f[2 * rows:] for f in found], axis=1)


def weight_kernel(mask, p1, p3, partner, beside, trace, weight, border, lenses, smat, full, edges):
    w, s, y, z, x, core, sign, pair = place_of()
    rows, row = slice(2 * MROWS, 2 * MROWS + 32), slice(MROWS + GROUP, 2 * MROWS)
    inner, outer = jnp.where(z == 0, y == 2, y == 1), jnp.where(z == 0, y == 0, y == 3)
    crossing = [jnp.where(outer, 0.0, jnp.where(inner, partner[r, :], beside[r, :])) for r in (rows, row)]
    own_rows = slice(PIECE, PIECE + 32), slice(PIECE + 32, PIECE + EDGE)
    above = [jnp.where(z == 0, c, p1[r, :]) for c, r in zip(crossing, own_rows)]
    below = [jnp.where(z == 3, c, p3[r, :]) for c, r in zip(crossing, own_rows)]
    lenses[0:8, :] = trace[...]
    lenses[8:9, :] = above[1][0:1]
    lenses[9:10, :] = below[1][0:1]
    lenses[10:16, :] = jnp.zeros((6, 128), F32)
    v = iota((UROWS, FHALF), 1)
    down, across = odd(focal_row(s, (UROWS, FHALF)), NF) * 0.5, odd(v, NF) * 0.5
    fade = 1.0 - jnp.exp((down * down + across * across) * (-1.0 / 1024.0))
    for q in range(8):
        for a in range(8):
            full[q, pl.ds(a, 8, stride=8), :] = mask[8 * a:8 * a + 8, 128 * q:128 * q + 128]
    for q in range(4):
        edges[q, pl.ds(0, 8, stride=2), :] = above[0][8 * q:8 * q + 8]
        edges[q, pl.ds(1, 8, stride=2), :] = below[0][8 * q:8 * q + 8]
    half = jnp.concatenate([edges[q] for q in range(4)], axis=1)
    half = jnp.where(core == 0, half, flipped_columns(half))
    t = half * fade[FROWS:]
    border[...] = t * t * 2.0**-24
    left, right = (jnp.concatenate([full[4 * k + q] for q in range(4)], axis=1) for k in range(2))
    for k, part in enumerate((left, flipped_columns(right))):
        t = part * fade[:FROWS]
        weight[:, FHALF * k:FHALF * (k + 1)] = t * t * 2.0**-24
    row, lane = iota((FHALF, 256), 0), iota((FHALF, 256), 1)
    column = 2 * ((lane >> 5) & 3) + jnp.where(lane < 128, core, 1 - core)
    lens = jnp.where((lane & 31) < 18, 16 * column - 1 + (lane & 31), -1)
    smat[0:FHALF, :] = (lens == row >> 3).astype(BF16)
    smat[FHALF:NF, :] = (lens == NL - 1 - (row >> 3)).astype(BF16)


def group_kernel(ref, utab, spot, *refs, p, flipped, waves=range(4)):
    before = refs[0] if flipped or p else None
    outs, (whi, wlo) = refs[before is not None:-2], refs[-2:]
    if len(waves) == 4:
        outs = [outs[0].at[m] for m in range(4)]
    else:
        *rest, out = outs
        outs = {m: out.at[2 * UROWS * (m & 1):2 * UROWS * ((m & 1) + 1), :] for m in waves}
        if 2 in waves:
            for k in range(2):
                out[4 * UROWS + 16 * k:4 * UROWS + 16 * k + 16, :] = rest[0][:, 256 * k:256 * k + 256]
    w, s, y, z, x, core, sign, pair = place_of()
    g = pair if p == 0 else 1 - pair
    turned = -1.0 if flipped else 1.0
    coef = jnp.concatenate(split2(ref[GROUP:MROWS, :]), axis=0)
    both = dot(coef, spot[...])
    coef = both[0:8] + both[8:16]
    down = odd(16 * (8 * g + iota((8, 128), 0)), NP) * (1.0 / 1024.0)
    across = odd(128 * core + iota((8, 128), 1), NP) * (1.0 / 1024.0)
    paths, steps = [], []
    for side in range(2):
        piston, tip, tilt = (coef[:, 256 * c + 128 * side:256 * c + 128 * side + 128] for c in range(3))
        tilt = (sign * turned) * tilt
        paths.append(piston + (across if side == 0 else -across) * tip + tilt * down)
        steps.append(tilt * (1.0 / 512.0))
    for m in waves:
        inverse = 1.0 / wavelength(2 * (w if m < 2 else w ^ 1) + (m & 1))
        im, re = zip(*(sincos(path * (turned * inverse)) for path in paths))
        step_im, step_re = zip(*(sincos(step * (turned * inverse)) for step in steps))
        for r2 in range(8):
            found = [[] for _ in range(4)]
            for h in range(2):
                r0 = 16 * r2 + 8 * h
                for side in range(2):
                    a = ref[MROWS * side + r0:MROWS * side + r0 + 8, :]
                    found[side].append(a * re[side])
                    found[2 + side].append(a * im[side])
                re, im = (
                    [a * p - b * q for a, b, p, q in zip(re, im, step_re, step_im)],
                    [a * q + b * p for a, b, p, q in zip(re, im, step_re, step_im)],
                )
            for k, values in enumerate(found):
                high, low = split2(jnp.concatenate(values, axis=0))
                r0, c0 = GROUP * (k >> 1) + 16 * r2, 128 * (k & 1)
                whi[m, r0:r0 + 16, c0:c0 + 128] = high
                wlo[m, r0:r0 + 16, c0:c0 + 128] = low
    for m in waves:
        table = utab[p, m]
        both = dot(table, whi[m])
        field = both[:2 * UROWS] + both[2 * UROWS:] + dot(table[:2 * UROWS], wlo[m])
        out = outs[m]
        if before is None:
            out[...] = field
        elif flipped:
            out[0:UROWS] = before[m, 0:UROWS] + field[:UROWS]
            out[UROWS:2 * UROWS] = before[m, UROWS:2 * UROWS] - field[UROWS:]
        else:
            out[...] = before[m] + field


def lens_kernel(keep, got, vtab, weight, border, smat, lenses, mine, other):
    parts = []
    w, s, y, z, x, core, sign, pair = place_of()
    theirs = jnp.concatenate([got[4 * UROWS + 16 * k:4 * UROWS + 16 * k + 16, :] for k in range(2)], axis=1)
    first = core == 0
    borders = jnp.where(first, border[...], theirs), jnp.where(first, theirs, border[...])
    for m in range(2):
        rows = slice(2 * UROWS * m, 2 * UROWS * (m + 1))
        left, right = (
            jnp.concatenate([ref[rows, 128 * q:128 * q + 128] for ref in (keep, got)], axis=1) for q in range(2)
        )
        odd_part = left - right
        sides = left + right, jnp.concatenate([odd_part[UROWS:], -odd_part[:UROWS]], axis=0)
        terms = []
        for q, side in enumerate(sides):
            high, low = split2(side)
            both = dot(jnp.concatenate([high, low], axis=0), vtab[m, q, 0])
            terms.append(both[:2 * UROWS] + both[2 * UROWS:] + dot(high, vtab[m, q, 1]))
        summed = []
        for q, value in enumerate((terms[0] + terms[1], terms[0] - terms[1])):
            re, im = value[:UROWS], value[UROWS:]
            power = re * re + im * im
            edges = power[FROWS:] * borders[q]
            power = power[:FROWS] * weight[:, FHALF * q:FHALF * (q + 1)]
            edges = edges[:8] + edges[8:]
            edges = edges + pltpu.roll(edges, 4, 0)
            edges = edges + pltpu.roll(edges, 2, 0)
            summed.append(jnp.concatenate([sum(power[8 * r:8 * r + 8] for r in range(8)), edges], axis=0))
        parts.extend(split2(jnp.concatenate(summed, axis=1)))
    lens = dot(jnp.concatenate(parts, axis=0), smat[...])
    for m in range(2):
        for k, out in enumerate((mine, other)):
            at = slice(128 * k, 128 * k + 128)
            out[16 * m:16 * m + 16, :] = lens[32 * m:32 * m + 16, at] + lens[32 * m + 16:32 * m + 32, at]
    row, lane = iota((128, 128), 0), iota((128, 128), 1) & 31
    spot = ((lane >= 18) & (lane < 21) & (row == 16 * (lane - 18) + 15)) | ((lane >= 21) & (lane < 24) & (row == 16 * (lane - 21)))
    sides = dot(lenses[...].astype(BF16), spot.astype(BF16))
    for out in (mine, other):
        out[0:16, :] += sides


def pack_kernel(mine, got, after, *outs, shifts):
    w, s, y, z, x, core, sign, pair = place_of()
    lane = iota((16, 128), 1) >> 5
    for out, k in zip(outs, shifts):
        at = (x + k) & 3
        packed = 0.0
        for c in range(2):
            rows = jnp.where(core == c, mine[...], got[...])
            for m in range(2):
                moved = pltpu.roll(rows[16 * m:16 * m + 16], (32 * (2 * c + m - at)) & 127, 1)
                packed = jnp.where(lane == 2 * c + m, moved, packed)
        out[...] = packed


def unpack_kernel(a0, a2, out):
    for k, ref in enumerate((a0, a2)):
        for c in range(4):
            out[4 * k + c] = ref[...] if c == 0 else pltpu.roll(ref[...], 128 - 32 * c, 1)


def order(a):
    return a - 1 if 0 < a < 9 else 8 + a // 9


def detector_kernel(kernel, begun, a1, a3, lenses, out, arrived, base, across, image, sems):
    w, s, y, z, x, core, sign, pair = place_of()
    for k, ref in ((1, a1), (3, a3)):
        for c in range(4):
            arrived[4 * ((x - k + 4) & 3) + c] = ref[...] if c == 0 else pltpu.roll(ref[...], 128 - 32 * c, 1)
    for k in (0, 2):
        for c in range(4):
            arrived[4 * ((x - k + 4) & 3) + c] = begun[2 * k + c]
    spot = (iota((128, 640), 0) == (iota((128, 640), 1) >> 5)) & (iota((128, 640), 1) < 18 * DPIX)
    spot = spot.astype(BF16)
    left, own, right = arrived[jnp.maximum(2 * w - 2, 0)], lenses[...], arrived[jnp.minimum(2 * w + 2, WAVES - 1)]
    lane = iota((16, 128), 1)
    tables = []
    for c in range(3):
        tables.append(
            jnp.where(
                lane == 0,
                pltpu.roll(left, 128 - 18 - c, 1),
                jnp.where(lane == 17, pltpu.roll(right, 128 - 4 - c, 1), pltpu.roll(own, 129 - 16 * c if c else 1, 1)),
            )
        )
    parts = list(split2(arrived[...].reshape(WAVES * 16, 128)))
    wide = dot(jnp.concatenate(parts + [jnp.concatenate(tables, axis=0).astype(BF16)], axis=0), spot)
    values, tables = wide[:16 * WAVES] + wide[16 * WAVES:32 * WAVES], wide[32 * WAVES:]
    row, column, count = tables[0:16] * 0.25, tables[16:32], tables[32:48]
    offset = 0.5 * ((iota((16, 640), 1) & 31).astype(F32) - column)
    falling, rising = jnp.exp(-offset), jnp.exp(offset)
    spread = 0.0
    for wave in range(WAVES):
        value = values[16 * wave:16 * wave + 16]
        along = jnp.minimum(falling * math.exp(0.5 * wave), rising * math.exp(-0.5 * wave))
        spread = spread + jnp.where(count > wave, value, 0.0) * along
    within = iota((16, 512), 1) & 31
    moved = [pltpu.roll(spread, 640 - (30 + q), 1)[:, 0:512] for q in range(5)]
    inside = [(within + q - 2 >= 0) & (within + q - 2 < DPIX) for q in range(5)]
    own = [jnp.where(i, v, 0.0) for i, v in zip(inside, moved)]
    beside = [jnp.where(i, 0.0, v) for i, v in zip(inside, moved)]
    for p in range(5):
        weights = [kernel[p:p + 1, q:q + 1] + (1.0 if p == q == 2 else 0.0) for q in range(5)]
        base[p] = sum(v * k for v, k in zip(own, weights))
        base[5 + p] = sum(v * k for q, (v, k) in enumerate(zip(beside, weights)) if q != 2)
    near = row[:, DPIX:DPIX + 512]
    far = jnp.where(within < 2, pltpu.roll(row, 640 - 30, 1)[:, 0:512], pltpu.roll(row, 640 - 34, 1)[:, 0:512])
    for k, value in enumerate((near, -near, far, -far)):
        across[k] = jnp.exp(value)
    sub = iota((8, 128), 0)
    depth = sub.astype(F32) * 0.25
    downs = [jnp.exp(-(depth + 2.0 * t)) for t in range(4)]
    ups = [jnp.exp(depth + 2.0 * t) for t in range(4)]
    copies = []
    for lt in range(4):
        at = slice(128 * lt, 128 * lt + 128)
        state = None
        for a in range(10):
            r = order(a)
            scale = [base[p, r:r + 1, at] for p in range(10)]
            fall, rise, fall_far, rise_far = (across[k, r:r + 1, at] for k in range(4))
            for t in (3,) if a == 0 else (0,) if a == 9 else range(4):
                one = jnp.minimum(downs[t] * fall, ups[t] * rise)
                two = jnp.minimum(downs[t] * fall_far, ups[t] * rise_far)
                h = [one * scale[p] + two * scale[5 + p] for p in range(5)]
                if state is not None:
                    part, h0, h1, h3, h4 = state
                    done = part + pltpu.roll(jnp.where(sub == 0, h[3], h3), 7, 0)
                    done = done + pltpu.roll(jnp.where(sub < 2, h[4], h4), 6, 0)
                    image[lt, 8 * (4 * a + t - 4):8 * (4 * a + t - 4) + 8, :] = done
                    part = h[2] + pltpu.roll(jnp.where(sub >= 6, h0, h[0]), 2, 0)
                    part = part + pltpu.roll(jnp.where(sub == 7, h1, h[1]), 1, 0)
                else:
                    part = h[2]
                state = part, h[0], h[1], h[3], h[4]
        copies.append(pltpu.make_async_copy(image.at[lt, 8:264, :], out.at[:, at], sems.at[lt]))
        copies[-1].start()
    for copy in copies:
        copy.wait()


def call(kernel, outs, in_smem, n_in, scratch=(), tail=(), limit=40, outside=False, aliases=None):
    specs = [pl.BlockSpec(memory_space=pltpu.SMEM)] * in_smem
    specs += [pl.BlockSpec(memory_space=pltpu.VMEM)] * (n_in - in_smem)
    specs[n_in - len(tail):] = tail
    single = not isinstance(outs, (list, tuple))
    vmem = pl.BlockSpec(memory_space=pltpu.VMEM)
    return pl.pallas_call(
        kernel,
        out_shape=outs,
        in_specs=specs,
        out_specs=pl.BlockSpec(memory_space=pl.ANY) if outside else vmem if single else [vmem] * len(outs),
        scratch_shapes=list(scratch),
        input_output_aliases=aliases or {},
        compiler_params=pltpu.CompilerParams(vmem_limit_bytes=limit * 2**20),
        name=getattr(kernel, "func", kernel).__name__,
    )


def shape(*dims, dtype=F32):
    return jax.ShapeDtypeStruct(dims, dtype)


def along_z(k):
    return [(4 * y + z, 4 * y + (z + k) % 4) for y in range(4) for z in range(4)]


def along_y(other):
    return [(4 * y + z, 4 * other[y] + z) for y in range(4) for z in range(4)]


def body(amplitude, seg_map, seg_table, focal_mask, trace_row, trace_col, block_count, crosstalk):
    anywhere = [pl.BlockSpec(memory_space=pl.ANY)]
    piece, up, down, trace = call(
        prepare_kernel,
        [shape(PIECE, 128), shape(PIECE + EDGE, 128), shape(PIECE + EDGE, 128), shape(8, 128)],
        0,
        7,
        [
            pltpu.VMEM((ROWS, NP), F32),
            pltpu.VMEM((16, NP), I32),
            pltpu.VMEM((3, SEGMENTS), I32),
            pltpu.VMEM((3, 8, 16), I32),
            pltpu.VMEM((2, 8, FHALF), F32),
            pltpu.SemaphoreType.DMA((9,)),
        ],
        tail=[pl.BlockSpec(memory_space=pltpu.HBM)] * 7,
    )(*(pltpu.with_memory_space_constraint(v, pltpu.HBM) for v in (amplitude, seg_map, seg_table.T, focal_mask, trace_row, trace_col, block_count)))
    utab, vtab, spot = call(
        table_kernel,
        [shape(2, 4, 4 * UROWS, 256, dtype=BF16), shape(2, 2, 2, HALF, FHALF, dtype=BF16), shape(128, 768, dtype=BF16)],
        0,
        1,
        tail=anywhere,
    )(piece)
    p1 = lax.ppermute(up, "slab", along_z(1))
    p3 = lax.ppermute(down, "slab", along_z(3))
    p2 = lax.ppermute(piece, "slab", along_z(2))
    begun = call(opposite_kernel, shape(2 * MROWS, 128), 0, 3, tail=anywhere)(piece, p2, utab)
    own, more = call(
        merge_kernel, [shape(2 * MROWS, 128), shape(2 * MROWS + 32, 128)], 0, 3, aliases={0: 0}
    )(begun, p1, p3)
    partner = lax.ppermute(more, "slab", along_y((3, 2, 1, 0)))
    beside = lax.ppermute(more, "slab", along_y((1, 0, 3, 2)))
    last = lax.ppermute(own, "slab", along_y((2, 3, 0, 1)))
    scratch = [pltpu.VMEM((4, 256, 256), BF16)] * 2

    def add(group, p, flipped, *before, outs=shape(4, 2 * UROWS, 256), tail=(), **options):
        kernel = functools.partial(group_kernel, p=p, flipped=flipped, **options)
        return call(kernel, outs, 0, 3 + len(before), scratch, tail=tail)(group, utab, spot, *before)

    field = add(own, 0, False)
    field = add(partner, 0, True, field)
    field = add(beside, 1, False, field)
    weight, border, lenses, smat = call(
        weight_kernel,
        [shape(FROWS, NF), shape(16, FHALF), shape(16, 128), shape(NF, 256, dtype=BF16)],
        0,
        6,
        [pltpu.VMEM((8, FROWS, 128), F32), pltpu.VMEM((4, 16, 128), F32)],
    )(focal_mask, p1, p3, partner, beside, trace)
    give = add(last, 1, True, field, border, outs=shape(4 * UROWS + 32, 256), waves=(2, 3))
    keep = add(last, 1, True, field, give, outs=shape(4 * UROWS, 256), waves=(0, 1), tail=anywhere)
    sibling = [(i, i ^ 1) for i in range(NWAV)]
    crossed = lax.ppermute(give, "wav", sibling)
    mine, other = call(lens_kernel, [shape(32, 128)] * 2, 0, 7)(
        keep, crossed, vtab, weight, border, smat, lenses
    )
    got = lax.ppermute(other, "wav", sibling)
    def along_x(sent, k):
        return lax.ppermute(sent, "wav", [(i, (i + 2 * k) % NWAV) for i in range(NWAV)])

    (opposite,) = call(functools.partial(pack_kernel, shifts=(2,)), [shape(16, 128)], 0, 3, tail=anywhere)(mine, got, lenses)
    a2 = along_x(opposite, 2)
    kept, forth, back = call(functools.partial(pack_kernel, shifts=(0, 1, 3)), [shape(16, 128)] * 3, 0, 3, tail=anywhere)(
        mine, got, opposite
    )
    a1, a3 = along_x(forth, 1), along_x(back, 3)
    begun = call(unpack_kernel, shape(8, 16, 128), 0, 2)(kept, a2)
    return call(
        detector_kernel,
        shape(256, 512),
        0,
        5,
        [
            pltpu.VMEM((WAVES, 16, 128), F32),
            pltpu.VMEM((10, 16, 512), F32),
            pltpu.VMEM((4, 16, 512), F32),
            pltpu.VMEM((4, 264, 128), F32),
            pltpu.SemaphoreType.DMA((4,)),
        ],
        outside=True,
    )(crosstalk, begun, a1, a3, lenses)


def solution(mesh):
    return jax.shard_map(
        body,
        mesh=mesh,
        in_specs=(
            P("slab", None),
            P("slab", None),
            P(),
            P("slab", None),
            P("slab", "wav"),
            P("slab", "wav"),
            P("slab", "wav"),
            P(),
        ),
        out_specs=P("slab", "wav"),
        check_vma=False,
    )
```

```python
import functools
import math

import jax
import jax.numpy as jnp
import numpy as np
from jax import lax
from jax.experimental import pallas as pl
from jax.experimental.pallas import tpu as pltpu
from jax.sharding import PartitionSpec as P

F32, BF16, I32 = jnp.float32, jnp.bfloat16, jnp.int32

NP, NF, NL, DPIX, SEGMENTS, WAVES = 512, 1024, 128, 32, 798, 16
NWAV, NSLAB = 8, 16
ROWS = NP // NSLAB
FROWS = NF // NSLAB
UROWS = FROWS + 16
GROUP = 128
PIECE, EDGE = 2 * (ROWS + 8), 40
MROWS = GROUP + 8
HALF, FHALF = NP // 2, NF // 2

SIN = (6.283184916495428, -41.34158923268831, 81.59994332977429, -76.61447253115396, 41.34288235413569, -12.471243534350362)
COS = (0.9999999890590228, -19.73920449945383, 64.93911745989081, -85.45013953079767,
       60.167630950263465, -25.967599245923743, 6.52865815775625)


def place_of():
    w, s = lax.axis_index("wav").astype(I32), lax.axis_index("slab").astype(I32)
    y = s >> 2
    return w, s, y, s & 3, w >> 1, w & 1, jnp.where(y < 2, 1.0, -1.0), jnp.where((y == 0) | (y == 3), 0, 1)


def iota(shape, dim):
    return lax.broadcasted_iota(I32, shape, dim)


def dot(a, b):
    return jnp.dot(a, b, preferred_element_type=F32)


def split2(x):
    high = x.astype(BF16)
    return high, (x - high.astype(F32)).astype(BF16)


def split3(x):
    high = x.astype(BF16)
    rest = x - high.astype(F32)
    middle = rest.astype(BF16)
    return high, middle, (rest - middle.astype(F32)).astype(BF16)


def sincos(turns):
    t = turns - jnp.round(turns)
    z = t * t
    s, c = SIN[-1], COS[-1]
    for a in SIN[-2::-1]:
        s = s * z + a
    for b in COS[-2::-1]:
        c = c * z + b
    return s * t, c


def focal_row(s, shape):
    a = iota(shape, 0)
    r = (a - FROWS) >> 1
    own = 8 * (a & 7) + (a >> 3)
    return FROWS * s + jnp.where(a < FROWS, own, jnp.where((a & 1) == 0, r - 8, FROWS + r))


def reversal(n):
    return (iota((n, n), 0) + iota((n, n), 1) == n - 1).astype(BF16)


def prepare_kernel(amp_in, seg_in, tab_in, mask, trow, tcol, count, out, up, down, trace, amp, seg, tab, tables, edges, sems):
    w, s, y, z, x, core, sign, pair = place_of()
    half = pl.ds(pl.multiple_of(FHALF * core, FHALF), FHALF)
    copies = [
        pltpu.make_async_copy(a, b, sems.at[k])
        for k, (a, b) in enumerate(
            (
                (tab_in, tab),
                (seg_in.at[0:8, :], seg.at[0:8, :]),
                (seg_in.at[16:24, :], seg.at[8:16, :]),
                (amp_in, amp),
                (trow, tables.at[0]),
                (tcol, tables.at[1]),
                (count, tables.at[2]),
                (mask.at[FROWS - 8:FROWS, half], edges.at[0]),
                (mask.at[0:8, half], edges.at[1]),
            )
        )
    ]
    for copy in copies:
        copy.start()
    lower = y >= 2
    rows, cols = iota((ROWS, ROWS), 0), iota((ROWS, ROWS), 1)
    turned = (cols == jnp.where(lower, ROWS - 1 - rows, rows)).astype(BF16)
    rev = reversal(128)
    lane = iota((NP, 128), 1)
    pick = ((iota((NP, 128), 0) == 16 * (lane & 31)) & (lane < 96)).astype(BF16)
    out[...] = jnp.zeros((PIECE, 128), F32)
    for ref in (up, down):
        ref[PIECE + 32:PIECE + EDGE, :] = jnp.zeros((8, 128), F32)
    trace[...] = jnp.zeros((8, 128), F32)
    for copy in copies:
        copy.wait()
    for c in range(3):
        table = tables[c].astype(F32)
        trace[:, 16 * c:16 * c + 16] = table
        up[PIECE + 32:PIECE + 33, 16 * c:16 * c + 16] = table[7:8]
        down[PIECE + 32:PIECE + 33, 16 * c:16 * c + 16] = table[0:1]
    ids = dot(jnp.concatenate(split2(seg[...].astype(F32)), axis=0), pick)
    ids = ids[0:16] + ids[16:32]
    upper_ids, lower_ids = ids[0:1], ids[8:9]
    ids = jnp.concatenate(
        [jnp.where(lower, lower_ids, upper_ids), jnp.where(lower, upper_ids, lower_ids)], axis=1
    )
    which = iota((SEGMENTS, 256), 0).astype(F32)
    table = jnp.concatenate([tab[...].astype(F32), jnp.zeros((5, SEGMENTS), F32)], axis=0)
    found = dot(jnp.concatenate(split2(table), axis=0), (which == ids).astype(BF16))
    found = found[0:3] + found[8:11]
    found = jnp.sum(jnp.where(iota((3, 256), 0) == (iota((3, 256), 1) & 127) >> 5, found, 0.0), axis=0, keepdims=True)
    for k in range(2):
        out[ROWS + k:ROWS + k + 1, :] = found[:, 128 * k:128 * k + 128]
    first = core == 0
    left = jnp.where(first, amp[:, 0:128], amp[:, 128:256])
    right = jnp.where(first, amp[:, 384:512], amp[:, 256:384])
    right = dot(jnp.concatenate(split3(right), axis=0), rev).astype(BF16)
    parts = list(split3(left)) + [right[ROWS * k:ROWS * k + ROWS] for k in range(3)]
    found = dot(turned, jnp.concatenate(parts, axis=1))
    for k in range(2):
        out[(ROWS + 8) * k:(ROWS + 8) * k + ROWS, :] = sum(found[:, 128 * q:128 * q + 128] for q in range(3 * k, 3 * k + 3))
    for k, ref in enumerate((up, down)):
        ref[0:PIECE, :] = out[...]
        for q in range(4):
            ref[PIECE + 8 * q:PIECE + 8 * q + 8, :] = edges[k, :, 128 * q:128 * q + 128]


def place_pieces(out, pieces):
    w, s, y, z, x, core, sign, pair = place_of()
    for k, piece in pieces:
        source = lax.rem(z - k + 4, 4)
        place = jnp.where(y >= 2, 3 - source, source)
        for at in range(4):

            @pl.when(place == at)
            def _(at=at, piece=piece):
                for t in range(2):
                    for b in range(2):
                        r0 = (ROWS + 8) * t + 16 * b
                        out[pl.ds(MROWS * t + 2 * at + b, 16, stride=8), :] = piece[r0:r0 + 16, :]
                out[GROUP + 2 * at:GROUP + 2 * at + 2, :] = piece[ROWS:ROWS + 2, :]


def opposite_kernel(p0, p2, after, out):
    del after
    out[GROUP:MROWS, :] = jnp.zeros((8, 128), F32)
    out[MROWS + GROUP:2 * MROWS, :] = jnp.zeros((8, 128), F32)
    place_pieces(out, ((0, p0), (2, p2)))


def merge_kernel(begun, p1, p3, out, more):
    del begun
    w, s, y, z, x, core, sign, pair = place_of()
    place_pieces(out, ((1, p1), (3, p3)))
    more[0:2 * MROWS, :] = out[...]
    wrap = jnp.where(z == 0, p1[PIECE:PIECE + EDGE, :], p3[PIECE:PIECE + EDGE, :])
    more[2 * MROWS:2 * MROWS + 32, :] = wrap[0:32]
    more[MROWS + GROUP:2 * MROWS, :] = wrap[32:EDGE]


def wavelength(w):
    return jnp.full((1, 1), 1000 + w, I32).astype(F32)


def slope(n, w):
    lam = wavelength(w)
    short = jnp.round(250.0 / lam * 2.0**14) * 2.0**-14
    rest = (250.0 - short * lam) / lam
    whole = n * (short * 2.0**-10)
    high = jnp.round(whole * 2.0**13) * 2.0**-13
    return high, (whole - high) + n * (rest * 2.0**-10)


def angle(m, step):
    t = m * step[0]
    t = t - jnp.round(t)
    return sincos(t + m * step[1])


def odd(index, count):
    return (2 * index + 1 - count).astype(F32)


def table_kernel(after, utab, vtab, spot):
    del after
    w, s, y, z, x, core, sign, pair = place_of()
    row, lane = iota((128, 768), 0), iota((128, 768), 1)
    block = 8 * core + ((lane & 127) >> 4)
    spot[...] = (row == 32 * (lane >> 8) + jnp.where((lane & 128) == 0, block, 31 - block)).astype(BF16)
    m = odd(focal_row(s, (UROWS, GROUP)), NF)
    rho = iota((1, GROUP), 1)
    for k in range(4):
        wave = 2 * (w if k < 2 else w ^ 1) + (k & 1)
        for p in range(2):
            g = pair if p == 0 else 1 - pair
            sin, cos = angle(m, slope(odd(128 * g + 16 * (rho & 7) + (rho >> 3), NP), wave))
            sin = sin * sign
            for r0, at, part in ((0, 0, cos), (0, GROUP, sin), (UROWS, 0, -sin), (UROWS, GROUP, cos)):
                high, low = split2(part)
                utab[p, k, r0:r0 + UROWS, at:at + GROUP] = high
                utab[p, k, r0 + 2 * UROWS:r0 + 3 * UROWS, at:at + GROUP] = low
    m = odd(iota((16, 128), 1), NF)
    for k in range(2):

        def chunk(c, carry, k=k):
            j0 = pl.multiple_of(16 * c, 16)
            step = slope(odd(((j0 + 128 * core) & 255) + iota((16, 128), 0), NP), 2 * w + k)
            sin, cos = angle(m, step)
            turn_im, turn_re = angle(jnp.full((16, 128), 256.0, F32), step)
            for t in range(4):
                for q, part in ((0, cos), (1, sin)):
                    high, low = split2(part)
                    vtab[k, q, 0, pl.ds(j0, 16), 128 * t:128 * t + 128] = high
                    vtab[k, q, 1, pl.ds(j0, 16), 128 * t:128 * t + 128] = low
                cos, sin = cos * turn_re - sin * turn_im, cos * turn_im + sin * turn_re
            return carry

        lax.fori_loop(0, HALF // 16, chunk, 0)


def flipped_columns(x):
    rev = reversal(256)
    n = x.shape[1] // 256
    parts = [jnp.concatenate(split3(x[:, 256 * q:256 * q + 256]), axis=0) for q in range(n)]
    rows, found = x.shape[0], [dot(part, rev) for part in reversed(parts)]
    return jnp.concatenate([f[:rows] + f[rows:2 * rows] + f[2 * rows:] for f in found], axis=1)


def weight_kernel(mask, p1, p3, partner, beside, trace, weight, border, lenses, smat, full, edges):
    w, s, y, z, x, core, sign, pair = place_of()
    rows, row = slice(2 * MROWS, 2 * MROWS + 32), slice(MROWS + GROUP, 2 * MROWS)
    inner, outer = jnp.where(z == 0, y == 2, y == 1), jnp.where(z == 0, y == 0, y == 3)
    crossing = [jnp.where(outer, 0.0, jnp.where(inner, partner[r, :], beside[r, :])) for r in (rows, row)]
    own_rows = slice(PIECE, PIECE + 32), slice(PIECE + 32, PIECE + EDGE)
    above = [jnp.where(z == 0, c, p1[r, :]) for c, r in zip(crossing, own_rows)]
    below = [jnp.where(z == 3, c, p3[r, :]) for c, r in zip(crossing, own_rows)]
    lenses[0:8, :] = trace[...]
    lenses[8:9, :] = above[1][0:1]
    lenses[9:10, :] = below[1][0:1]
    lenses[10:16, :] = jnp.zeros((6, 128), F32)
    v = iota((UROWS, FHALF), 1)
    down, across = odd(focal_row(s, (UROWS, FHALF)), NF) * 0.5, odd(v, NF) * 0.5
    fade = 1.0 - jnp.exp((down * down + across * across) * (-1.0 / 1024.0))
    for q in range(8):
        for a in range(8):
            full[q, pl.ds(a, 8, stride=8), :] = mask[8 * a:8 * a + 8, 128 * q:128 * q + 128]
    for q in range(4):
        edges[q, pl.ds(0, 8, stride=2), :] = above[0][8 * q:8 * q + 8]
        edges[q, pl.ds(1, 8, stride=2), :] = below[0][8 * q:8 * q + 8]
    half = jnp.concatenate([edges[q, 0:16, :] for q in range(4)], axis=1)
    half = jnp.where(core == 0, half, flipped_columns(half))
    t = half * fade[FROWS:]
    border[...] = t * t * 2.0**-24
    left, right = (jnp.concatenate([full[4 * k + q, 0:FROWS, :] for q in range(4)], axis=1) for k in range(2))
    for k, part in enumerate((left, flipped_columns(right))):
        t = part * fade[:FROWS]
        weight[:, FHALF * k:FHALF * (k + 1)] = t * t * 2.0**-24
    row, lane = iota((FHALF, 256), 0), iota((FHALF, 256), 1)
    column = 2 * ((lane >> 5) & 3) + jnp.where(lane < 128, core, 1 - core)
    lens = jnp.where((lane & 31) < 18, 16 * column - 1 + (lane & 31), -1)
    smat[0:FHALF, :] = (lens == row >> 3).astype(BF16)
    smat[FHALF:NF, :] = (lens == NL - 1 - (row >> 3)).astype(BF16)


def group_kernel(ref, utab, spot, *refs, p, flipped, waves=range(4)):
    before = refs[0] if flipped or p else None
    outs, (whi, wlo) = refs[before is not None:-2], refs[-2:]
    if len(waves) == 4:
        outs = [outs[0].at[m] for m in range(4)]
    else:
        *rest, out = outs
        outs = {m: out.at[2 * UROWS * (m & 1):2 * UROWS * ((m & 1) + 1), :] for m in waves}
        if 2 in waves:
            for k in range(2):
                out[4 * UROWS + 16 * k:4 * UROWS + 16 * k + 16, :] = rest[0][:, 256 * k:256 * k + 256]
    w, s, y, z, x, core, sign, pair = place_of()
    g = pair if p == 0 else 1 - pair
    turned = -1.0 if flipped else 1.0
    coef = jnp.concatenate(split2(ref[GROUP:MROWS, :]), axis=0)
    both = dot(coef, spot[...])
    coef = both[0:8] + both[8:16]
    down = odd(16 * (8 * g + iota((8, 128), 0)), NP) * (1.0 / 1024.0)
    across = odd(128 * core + iota((8, 128), 1), NP) * (1.0 / 1024.0)
    paths, steps = [], []
    for side in range(2):
        piston, tip, tilt = (coef[:, 256 * c + 128 * side:256 * c + 128 * side + 128] for c in range(3))
        tilt = (sign * turned) * tilt
        paths.append(piston + (across if side == 0 else -across) * tip + tilt * down)
        steps.append(tilt * (1.0 / 512.0))
    for m in waves:
        inverse = 1.0 / wavelength(2 * (w if m < 2 else w ^ 1) + (m & 1))
        im, re = zip(*(sincos(path * (turned * inverse)) for path in paths))
        step_im, step_re = zip(*(sincos(step * (turned * inverse)) for step in steps))
        for r2 in range(8):
            found = [[] for _ in range(4)]
            for h in range(2):
                r0 = 16 * r2 + 8 * h
                for side in range(2):
                    a = ref[MROWS * side + r0:MROWS * side + r0 + 8, :]
                    found[side].append(a * re[side])
                    found[2 + side].append(a * im[side])
                re, im = (
                    [a * p - b * q for a, b, p, q in zip(re, im, step_re, step_im)],
                    [a * q + b * p for a, b, p, q in zip(re, im, step_re, step_im)],
                )
            for k, values in enumerate(found):
                high, low = split2(jnp.concatenate(values, axis=0))
                r0, c0 = GROUP * (k >> 1) + 16 * r2, 128 * (k & 1)
                whi[m, r0:r0 + 16, c0:c0 + 128] = high
                wlo[m, r0:r0 + 16, c0:c0 + 128] = low
    for m in waves:
        table = utab[p, m]
        both = dot(table, whi[m])
        field = both[:2 * UROWS] + both[2 * UROWS:] + dot(table[:2 * UROWS], wlo[m])
        out = outs[m]
        if before is None:
            out[...] = field
        elif flipped:
            out[0:UROWS] = before[m, 0:UROWS] + field[:UROWS]
            out[UROWS:2 * UROWS] = before[m, UROWS:2 * UROWS] - field[UROWS:]
        else:
            out[...] = before[m] + field


def lens_kernel(keep, got, vtab, weight, border, smat, lenses, mine, other):
    parts = []
    w, s, y, z, x, core, sign, pair = place_of()
    theirs = jnp.concatenate([got[4 * UROWS + 16 * k:4 * UROWS + 16 * k + 16, :] for k in range(2)], axis=1)
    first = core == 0
    borders = jnp.where(first, border[...], theirs), jnp.where(first, theirs, border[...])
    for m in range(2):
        rows = slice(2 * UROWS * m, 2 * UROWS * (m + 1))
        left, right = (
            jnp.concatenate([ref[rows, 128 * q:128 * q + 128] for ref in (keep, got)], axis=1) for q in range(2)
        )
        odd_part = left - right
        sides = left + right, jnp.concatenate([odd_part[UROWS:], -odd_part[:UROWS]], axis=0)
        terms = []
        for q, side in enumerate(sides):
            high, low = split2(side)
            both = dot(jnp.concatenate([high, low], axis=0), vtab[m, q, 0])
            terms.append(both[:2 * UROWS] + both[2 * UROWS:] + dot(high, vtab[m, q, 1]))
        summed = []
        for q, value in enumerate((terms[0] + terms[1], terms[0] - terms[1])):
            re, im = value[:UROWS], value[UROWS:]
            power = re * re + im * im
            edges = power[FROWS:] * borders[q]
            power = power[:FROWS] * weight[:, FHALF * q:FHALF * (q + 1)]
            edges = edges[:8] + edges[8:]
            edges = edges + pltpu.roll(edges, 4, 0)
            edges = edges + pltpu.roll(edges, 2, 0)
            summed.append(jnp.concatenate([sum(power[8 * r:8 * r + 8] for r in range(8)), edges], axis=0))
        parts.extend(split2(jnp.concatenate(summed, axis=1)))
    lens = dot(jnp.concatenate(parts, axis=0), smat[...])
    for m in range(2):
        for k, out in enumerate((mine, other)):
            at = slice(128 * k, 128 * k + 128)
            out[16 * m:16 * m + 16, :] = lens[32 * m:32 * m + 16, at] + lens[32 * m + 16:32 * m + 32, at]
    row, lane = iota((128, 128), 0), iota((128, 128), 1) & 31
    spot = ((lane >= 18) & (lane < 21) & (row == 16 * (lane - 18) + 15)) | ((lane >= 21) & (lane < 24) & (row == 16 * (lane - 21)))
    sides = dot(lenses[...].astype(BF16), spot.astype(BF16))
    for out in (mine, other):
        out[0:16, :] += sides


def pack_kernel(mine, got, *outs):
    w, s, y, z, x, core, sign, pair = place_of()
    lane = iota((16, 128), 1) >> 5
    for k, out in enumerate(outs):
        at = (x + k) & 3
        packed = 0.0
        for c in range(2):
            rows = jnp.where(core == c, mine[...], got[...])
            for m in range(2):
                moved = pltpu.roll(rows[16 * m:16 * m + 16], (32 * (2 * c + m - at)) & 127, 1)
                packed = jnp.where(lane == 2 * c + m, moved, packed)
        out[...] = packed


def order(a):
    return a - 1 if 0 < a < 9 else 8 + a // 9


def detector_kernel(kernel, a0, a1, a2, a3, lenses, out, arrived, base, across, image, sems):
    w, s, y, z, x, core, sign, pair = place_of()
    for k, ref in enumerate((a0, a1, a2, a3)):
        for c in range(4):
            arrived[4 * ((x - k + 4) & 3) + c] = ref[...] if c == 0 else pltpu.roll(ref[...], 128 - 32 * c, 1)
    spot = (iota((128, 640), 0) == (iota((128, 640), 1) >> 5)) & (iota((128, 640), 1) < 18 * DPIX)
    spot = spot.astype(BF16)
    left, own, right = arrived[jnp.maximum(2 * w - 2, 0)], lenses[...], arrived[jnp.minimum(2 * w + 2, WAVES - 1)]
    lane = iota((16, 128), 1)
    tables = []
    for c in range(3):
        tables.append(
            jnp.where(
                lane == 0,
                pltpu.roll(left, 128 - 18 - c, 1),
                jnp.where(lane == 17, pltpu.roll(right, 128 - 4 - c, 1), pltpu.roll(own, 129 - 16 * c if c else 1, 1)),
            )
        )
    parts = list(split2(arrived[...].reshape(WAVES * 16, 128)))
    wide = dot(jnp.concatenate(parts + [jnp.concatenate(tables, axis=0).astype(BF16)], axis=0), spot)
    values, tables = wide[:16 * WAVES] + wide[16 * WAVES:32 * WAVES], wide[32 * WAVES:]
    row, column, count = tables[0:16] * 0.25, tables[16:32], tables[32:48]
    offset = 0.5 * ((iota((16, 640), 1) & 31).astype(F32) - column)
    falling, rising = jnp.exp(-offset), jnp.exp(offset)
    spread = 0.0
    for wave in range(WAVES):
        value = values[16 * wave:16 * wave + 16]
        along = jnp.minimum(falling * math.exp(0.5 * wave), rising * math.exp(-0.5 * wave))
        spread = spread + jnp.where(count > wave, value, 0.0) * along
    within = iota((16, 512), 1) & 31
    moved = [pltpu.roll(spread, 640 - (30 + q), 1)[:, 0:512] for q in range(5)]
    inside = [(within + q - 2 >= 0) & (within + q - 2 < DPIX) for q in range(5)]
    own = [jnp.where(i, v, 0.0) for i, v in zip(inside, moved)]
    beside = [jnp.where(i, 0.0, v) for i, v in zip(inside, moved)]
    for p in range(5):
        weights = [kernel[p:p + 1, q:q + 1] + (1.0 if p == q == 2 else 0.0) for q in range(5)]
        base[p] = sum(v * k for v, k in zip(own, weights))
        base[5 + p] = sum(v * k for q, (v, k) in enumerate(zip(beside, weights)) if q != 2)
    near = row[:, DPIX:DPIX + 512]
    far = jnp.where(within < 2, pltpu.roll(row, 640 - 30, 1)[:, 0:512], pltpu.roll(row, 640 - 34, 1)[:, 0:512])
    for k, value in enumerate((near, -near, far, -far)):
        across[k] = jnp.exp(value)
    sub = iota((8, 128), 0)
    depth = sub.astype(F32) * 0.25
    downs = [jnp.exp(-(depth + 2.0 * t)) for t in range(4)]
    ups = [jnp.exp(depth + 2.0 * t) for t in range(4)]
    copies = []
    for lt in range(4):
        at = slice(128 * lt, 128 * lt + 128)
        state = None
        for a in range(10):
            r = order(a)
            scale = [base[p, r:r + 1, at] for p in range(10)]
            fall, rise, fall_far, rise_far = (across[k, r:r + 1, at] for k in range(4))
            for t in (3,) if a == 0 else (0,) if a == 9 else range(4):
                one = jnp.minimum(downs[t] * fall, ups[t] * rise)
                two = jnp.minimum(downs[t] * fall_far, ups[t] * rise_far)
                h = [one * scale[p] + two * scale[5 + p] for p in range(5)]
                if state is not None:
                    part, h0, h1, h3, h4 = state
                    done = part + pltpu.roll(jnp.where(sub == 0, h[3], h3), 7, 0)
                    done = done + pltpu.roll(jnp.where(sub < 2, h[4], h4), 6, 0)
                    image[lt, 8 * (4 * a + t - 4):8 * (4 * a + t - 4) + 8, :] = done
                    part = h[2] + pltpu.roll(jnp.where(sub >= 6, h0, h[0]), 2, 0)
                    part = part + pltpu.roll(jnp.where(sub == 7, h1, h[1]), 1, 0)
                else:
                    part = h[2]
                state = part, h[0], h[1], h[3], h[4]
        copies.append(pltpu.make_async_copy(image.at[lt, 8:264, :], out.at[:, at], sems.at[lt]))
        copies[-1].start()
    for copy in copies:
        copy.wait()


def call(kernel, outs, in_smem, n_in, scratch=(), tail=(), limit=40, outside=False, aliases=None):
    specs = [pl.BlockSpec(memory_space=pltpu.SMEM)] * in_smem
    specs += [pl.BlockSpec(memory_space=pltpu.VMEM)] * (n_in - in_smem)
    specs[n_in - len(tail):] = tail
    single = not isinstance(outs, (list, tuple))
    vmem = pl.BlockSpec(memory_space=pltpu.VMEM)
    return pl.pallas_call(
        kernel,
        out_shape=outs,
        in_specs=specs,
        out_specs=pl.BlockSpec(memory_space=pl.ANY) if outside else vmem if single else [vmem] * len(outs),
        scratch_shapes=list(scratch),
        input_output_aliases=aliases or {},
        compiler_params=pltpu.CompilerParams(vmem_limit_bytes=limit * 2**20),
        name=getattr(kernel, "func", kernel).__name__,
    )


def shape(*dims, dtype=F32):
    return jax.ShapeDtypeStruct(dims, dtype)


def along_z(k):
    return [(4 * y + z, 4 * y + (z + k) % 4) for y in range(4) for z in range(4)]


def along_y(other):
    return [(4 * y + z, 4 * other[y] + z) for y in range(4) for z in range(4)]


def body(amplitude, seg_map, seg_table, focal_mask, trace_row, trace_col, block_count, crosstalk):
    anywhere = [pl.BlockSpec(memory_space=pl.ANY)]
    piece, up, down, trace = call(
        prepare_kernel,
        [shape(PIECE, 128), shape(PIECE + EDGE, 128), shape(PIECE + EDGE, 128), shape(8, 128)],
        0,
        7,
        [
            pltpu.VMEM((ROWS, NP), F32),
            pltpu.VMEM((16, NP), I32),
            pltpu.VMEM((3, SEGMENTS), I32),
            pltpu.VMEM((3, 8, 16), I32),
            pltpu.VMEM((2, 8, FHALF), F32),
            pltpu.SemaphoreType.DMA((9,)),
        ],
        tail=[pl.BlockSpec(memory_space=pltpu.HBM)] * 7,
    )(*(pltpu.with_memory_space_constraint(v, pltpu.HBM) for v in (amplitude, seg_map, seg_table.T, focal_mask, trace_row, trace_col, block_count)))
    utab, vtab, spot = call(
        table_kernel,
        [shape(2, 4, 4 * UROWS, 256, dtype=BF16), shape(2, 2, 2, HALF, FHALF, dtype=BF16), shape(128, 768, dtype=BF16)],
        0,
        1,
        tail=anywhere,
    )(piece)
    p1 = lax.ppermute(up, "slab", along_z(1))
    p3 = lax.ppermute(down, "slab", along_z(3))
    p2 = lax.ppermute(piece, "slab", along_z(2))
    begun = call(opposite_kernel, shape(2 * MROWS, 128), 0, 3, tail=anywhere)(piece, p2, utab)
    own, more = call(
        merge_kernel, [shape(2 * MROWS, 128), shape(2 * MROWS + 32, 128)], 0, 3, aliases={0: 0}
    )(begun, p1, p3)
    partner = lax.ppermute(more, "slab", along_y((3, 2, 1, 0)))
    beside = lax.ppermute(more, "slab", along_y((1, 0, 3, 2)))
    last = lax.ppermute(own, "slab", along_y((2, 3, 0, 1)))
    scratch = [pltpu.VMEM((4, 256, 256), BF16)] * 2

    def add(group, p, flipped, *before, outs=shape(4, 2 * UROWS, 256), tail=(), **options):
        kernel = functools.partial(group_kernel, p=p, flipped=flipped, **options)
        return call(kernel, outs, 0, 3 + len(before), scratch, tail=tail)(group, utab, spot, *before)

    field = add(own, 0, False)
    field = add(partner, 0, True, field)
    field = add(beside, 1, False, field)
    weight, border, lenses, smat = call(
        weight_kernel,
        [shape(FROWS, NF), shape(16, FHALF), shape(16, 128), shape(NF, 256, dtype=BF16)],
        0,
        6,
        [pltpu.VMEM((8, FROWS + 8, 128), F32), pltpu.VMEM((4, 24, 128), F32)],
    )(focal_mask, p1, p3, partner, beside, trace)
    give = add(last, 1, True, field, border, outs=shape(4 * UROWS + 32, 256), waves=(2, 3))
    keep = add(last, 1, True, field, give, outs=shape(4 * UROWS, 256), waves=(0, 1), tail=anywhere)
    sibling = [(i, i ^ 1) for i in range(NWAV)]
    crossed = lax.ppermute(give, "wav", sibling)
    mine, other = call(lens_kernel, [shape(32, 128)] * 2, 0, 7)(
        keep, crossed, vtab, weight, border, smat, lenses
    )
    got = lax.ppermute(other, "wav", sibling)
    def along_x(sent, k):
        return lax.ppermute(sent, "wav", [(i, (i + 2 * k) % NWAV) for i in range(NWAV)])

    kept, *sent = call(pack_kernel, [shape(16, 128)] * 4, 0, 2)(mine, got)
    arrived = [along_x(sent[k - 1], k) for k in (1, 2, 3)]
    return call(
        detector_kernel,
        shape(256, 512),
        0,
        6,
        [
            pltpu.VMEM((WAVES, 16, 128), F32),
            pltpu.VMEM((10, 16, 512), F32),
            pltpu.VMEM((4, 16, 512), F32),
            pltpu.VMEM((4, 264, 128), F32),
            pltpu.SemaphoreType.DMA((4,)),
        ],
        outside=True,
    )(crosstalk, kept, *arrived, lenses)


def solution(mesh):
    return jax.shard_map(
        body,
        mesh=mesh,
        in_specs=(
            P("slab", None),
            P("slab", None),
            P(),
            P("slab", None),
            P("slab", "wav"),
            P("slab", "wav"),
            P("slab", "wav"),
            P(),
        ),
        out_specs=P("slab", "wav"),
        check_vma=False,
    )
```

```python
import functools
import math

import jax
import jax.numpy as jnp
import numpy as np
from jax import lax
from jax.experimental import pallas as pl
from jax.experimental.pallas import tpu as pltpu
from jax.sharding import PartitionSpec as P

F32, BF16, I32 = jnp.float32, jnp.bfloat16, jnp.int32

NP, NF, NL, DPIX, SEGMENTS, WAVES = 512, 1024, 128, 32, 798, 16
NWAV, NSLAB = 8, 16
ROWS = NP // NSLAB
FROWS = NF // NSLAB
UROWS = FROWS + 16
GROUP = 128
PIECE, EDGE = 2 * (ROWS + 8), 40
MROWS = GROUP + 8
HALF, FHALF = NP // 2, NF // 2

SIN = (6.283184916495428, -41.34158923268831, 81.59994332977429, -76.61447253115396, 41.34288235413569, -12.471243534350362)
COS = (0.9999999890590228, -19.73920449945383, 64.93911745989081, -85.45013953079767,
       60.167630950263465, -25.967599245923743, 6.52865815775625)


def place_of():
    w, s = lax.axis_index("wav").astype(I32), lax.axis_index("slab").astype(I32)
    y = s >> 2
    return w, s, y, s & 3, w >> 1, w & 1, jnp.where(y < 2, 1.0, -1.0), jnp.where((y == 0) | (y == 3), 0, 1)


def iota(shape, dim):
    return lax.broadcasted_iota(I32, shape, dim)


def dot(a, b):
    return jnp.dot(a, b, preferred_element_type=F32)


def split2(x):
    high = x.astype(BF16)
    return high, (x - high.astype(F32)).astype(BF16)


def split3(x):
    high = x.astype(BF16)
    rest = x - high.astype(F32)
    middle = rest.astype(BF16)
    return high, middle, (rest - middle.astype(F32)).astype(BF16)


def sincos(turns):
    t = turns - jnp.round(turns)
    z = t * t
    s, c = SIN[-1], COS[-1]
    for a in SIN[-2::-1]:
        s = s * z + a
    for b in COS[-2::-1]:
        c = c * z + b
    return s * t, c


def focal_row(s, shape):
    a = iota(shape, 0)
    r = (a - FROWS) >> 1
    own = 8 * (a & 7) + (a >> 3)
    return FROWS * s + jnp.where(a < FROWS, own, jnp.where((a & 1) == 0, r - 8, FROWS + r))


def reversal(n):
    return (iota((n, n), 0) + iota((n, n), 1) == n - 1).astype(BF16)


def prepare_kernel(amp_in, seg_in, tab_in, mask, trow, tcol, count, out, up, down, trace, amp, seg, tab, tables, edges, sems):
    w, s, y, z, x, core, sign, pair = place_of()
    half = pl.ds(pl.multiple_of(FHALF * core, FHALF), FHALF)
    copies = [
        pltpu.make_async_copy(a, b, sems.at[k])
        for k, (a, b) in enumerate(
            (
                (tab_in, tab),
                (seg_in.at[0:8, :], seg.at[0:8, :]),
                (seg_in.at[16:24, :], seg.at[8:16, :]),
                (amp_in, amp),
                (trow, tables.at[0]),
                (tcol, tables.at[1]),
                (count, tables.at[2]),
                (mask.at[FROWS - 8:FROWS, half], edges.at[0]),
                (mask.at[0:8, half], edges.at[1]),
            )
        )
    ]
    for copy in copies:
        copy.start()
    lower = y >= 2
    rows, cols = iota((ROWS, ROWS), 0), iota((ROWS, ROWS), 1)
    turned = (cols == jnp.where(lower, ROWS - 1 - rows, rows)).astype(BF16)
    rev = reversal(128)
    lane = iota((NP, 128), 1)
    pick = ((iota((NP, 128), 0) == 16 * (lane & 31)) & (lane < 96)).astype(BF16)
    out[...] = jnp.zeros((PIECE, 128), F32)
    for ref in (up, down):
        ref[PIECE + 32:PIECE + EDGE, :] = jnp.zeros((8, 128), F32)
    trace[...] = jnp.zeros((8, 128), F32)
    for copy in copies:
        copy.wait()
    for c in range(3):
        table = tables[c].astype(F32)
        trace[:, 16 * c:16 * c + 16] = table
        up[PIECE + 32:PIECE + 33, 16 * c:16 * c + 16] = table[7:8]
        down[PIECE + 32:PIECE + 33, 16 * c:16 * c + 16] = table[0:1]
    ids = dot(jnp.concatenate(split2(seg[...].astype(F32)), axis=0), pick)
    ids = ids[0:16] + ids[16:32]
    upper_ids, lower_ids = ids[0:1], ids[8:9]
    ids = jnp.concatenate(
        [jnp.where(lower, lower_ids, upper_ids), jnp.where(lower, upper_ids, lower_ids)], axis=1
    )
    which = iota((SEGMENTS, 256), 0).astype(F32)
    table = jnp.concatenate([tab[...].astype(F32), jnp.zeros((5, SEGMENTS), F32)], axis=0)
    found = dot(jnp.concatenate(split2(table), axis=0), (which == ids).astype(BF16))
    found = found[0:3] + found[8:11]
    found = jnp.sum(jnp.where(iota((3, 256), 0) == (iota((3, 256), 1) & 127) >> 5, found, 0.0), axis=0, keepdims=True)
    for k in range(2):
        out[ROWS + k:ROWS + k + 1, :] = found[:, 128 * k:128 * k + 128]
    first = core == 0
    left = jnp.where(first, amp[:, 0:128], amp[:, 128:256])
    right = jnp.where(first, amp[:, 384:512], amp[:, 256:384])
    right = dot(jnp.concatenate(split3(right), axis=0), rev).astype(BF16)
    parts = list(split3(left)) + [right[ROWS * k:ROWS * k + ROWS] for k in range(3)]
    found = dot(turned, jnp.concatenate(parts, axis=1))
    for k in range(2):
        out[(ROWS + 8) * k:(ROWS + 8) * k + ROWS, :] = sum(found[:, 128 * q:128 * q + 128] for q in range(3 * k, 3 * k + 3))
    for k, ref in enumerate((up, down)):
        ref[0:PIECE, :] = out[...]
        for q in range(4):
            ref[PIECE + 8 * q:PIECE + 8 * q + 8, :] = edges[k, :, 128 * q:128 * q + 128]


def place_pieces(out, pieces):
    w, s, y, z, x, core, sign, pair = place_of()
    for k, piece in pieces:
        source = lax.rem(z - k + 4, 4)
        place = jnp.where(y >= 2, 3 - source, source)
        for at in range(4):

            @pl.when(place == at)
            def _(at=at, piece=piece):
                for t in range(2):
                    for b in range(2):
                        r0 = (ROWS + 8) * t + 16 * b
                        out[pl.ds(MROWS * t + 2 * at + b, 16, stride=8), :] = piece[r0:r0 + 16, :]
                out[GROUP + 2 * at:GROUP + 2 * at + 2, :] = piece[ROWS:ROWS + 2, :]


def merge_kernel(p0, p1, p2, p3, after, out, more):
    del after
    out[GROUP:MROWS, :] = jnp.zeros((8, 128), F32)
    out[MROWS + GROUP:2 * MROWS, :] = jnp.zeros((8, 128), F32)
    w, s, y, z, x, core, sign, pair = place_of()
    place_pieces(out, enumerate((p0, p1, p2, p3)))
    more[0:2 * MROWS, :] = out[...]
    wrap = jnp.where(z == 0, p1[PIECE:PIECE + EDGE, :], p3[PIECE:PIECE + EDGE, :])
    more[2 * MROWS:2 * MROWS + 32, :] = wrap[0:32]
    more[MROWS + GROUP:2 * MROWS, :] = wrap[32:EDGE]


def wavelength(w):
    return jnp.full((1, 1), 1000 + w, I32).astype(F32)


def slope(n, w):
    lam = wavelength(w)
    short = jnp.round(250.0 / lam * 2.0**14) * 2.0**-14
    rest = (250.0 - short * lam) / lam
    whole = n * (short * 2.0**-10)
    high = jnp.round(whole * 2.0**13) * 2.0**-13
    return high, (whole - high) + n * (rest * 2.0**-10)


def angle(m, step):
    t = m * step[0]
    t = t - jnp.round(t)
    return sincos(t + m * step[1])


def odd(index, count):
    return (2 * index + 1 - count).astype(F32)


def table_kernel(after, utab, vtab, spot):
    del after
    w, s, y, z, x, core, sign, pair = place_of()
    row, lane = iota((128, 768), 0), iota((128, 768), 1)
    block = 8 * core + ((lane & 127) >> 4)
    spot[...] = (row == 32 * (lane >> 8) + jnp.where((lane & 128) == 0, block, 31 - block)).astype(BF16)
    m = odd(focal_row(s, (UROWS, GROUP)), NF)
    rho = iota((1, GROUP), 1)
    for k in range(4):
        wave = 2 * (w if k < 2 else w ^ 1) + (k & 1)
        for p in range(2):
            g = pair if p == 0 else 1 - pair
            sin, cos = angle(m, slope(odd(128 * g + 16 * (rho & 7) + (rho >> 3), NP), wave))
            sin = sin * sign
            for r0, at, part in ((0, 0, cos), (0, GROUP, sin), (UROWS, 0, -sin), (UROWS, GROUP, cos)):
                high, low = split2(part)
                utab[p, k, r0:r0 + UROWS, at:at + GROUP] = high
                utab[p, k, r0 + 2 * UROWS:r0 + 3 * UROWS, at:at + GROUP] = low
    m = odd(iota((16, 128), 1), NF)
    for k in range(2):

        def chunk(c, carry, k=k):
            j0 = pl.multiple_of(16 * c, 16)
            step = slope(odd(((j0 + 128 * core) & 255) + iota((16, 128), 0), NP), 2 * w + k)
            sin, cos = angle(m, step)
            turn_im, turn_re = angle(jnp.full((16, 128), 256.0, F32), step)
            for t in range(4):
                for q, part in ((0, cos), (1, sin)):
                    high, low = split2(part)
                    vtab[k, q, 0, pl.ds(j0, 16), 128 * t:128 * t + 128] = high
                    vtab[k, q, 1, pl.ds(j0, 16), 128 * t:128 * t + 128] = low
                cos, sin = cos * turn_re - sin * turn_im, cos * turn_im + sin * turn_re
            return carry

        lax.fori_loop(0, HALF // 16, chunk, 0)


def flipped_columns(x):
    rev = reversal(256)
    n = x.shape[1] // 256
    parts = [jnp.concatenate(split3(x[:, 256 * q:256 * q + 256]), axis=0) for q in range(n)]
    rows, found = x.shape[0], [dot(part, rev) for part in reversed(parts)]
    return jnp.concatenate([f[:rows] + f[rows:2 * rows] + f[2 * rows:] for f in found], axis=1)


def fading(s):
    down, across = odd(focal_row(s, (UROWS, FHALF)), NF) * 0.5, odd(iota((UROWS, FHALF), 1), NF) * 0.5
    return 1.0 - jnp.exp((down * down + across * across) * (-1.0 / 1024.0))


def weight_kernel(mask, after, weight, smat, full):
    del after
    w, s, y, z, x, core, sign, pair = place_of()
    fade = fading(s)
    for q in range(8):
        for a in range(8):
            full[q, pl.ds(a, 8, stride=8), :] = mask[8 * a:8 * a + 8, 128 * q:128 * q + 128]
    left, right = (jnp.concatenate([full[4 * k + q, 0:FROWS, :] for q in range(4)], axis=1) for k in range(2))
    for k, part in enumerate((left, flipped_columns(right))):
        t = part * fade[:FROWS]
        weight[:, FHALF * k:FHALF * (k + 1)] = t * t * 2.0**-24
    row, lane = iota((FHALF, 256), 0), iota((FHALF, 256), 1)
    column = 2 * ((lane >> 5) & 3) + jnp.where(lane < 128, core, 1 - core)
    lens = jnp.where((lane & 31) < 18, 16 * column - 1 + (lane & 31), -1)
    smat[0:FHALF, :] = (lens == row >> 3).astype(BF16)
    smat[FHALF:NF, :] = (lens == NL - 1 - (row >> 3)).astype(BF16)


def border_kernel(p1, p3, beside, partner, trace, border, lenses, edges):
    w, s, y, z, x, core, sign, pair = place_of()
    rows, row = slice(2 * MROWS, 2 * MROWS + 32), slice(MROWS + GROUP, 2 * MROWS)
    inner, outer = jnp.where(z == 0, y == 2, y == 1), jnp.where(z == 0, y == 0, y == 3)
    crossing = [jnp.where(outer, 0.0, jnp.where(inner, partner[r, :], beside[r, :])) for r in (rows, row)]
    own_rows = slice(PIECE, PIECE + 32), slice(PIECE + 32, PIECE + EDGE)
    above = [jnp.where(z == 0, c, p1[r, :]) for c, r in zip(crossing, own_rows)]
    below = [jnp.where(z == 3, c, p3[r, :]) for c, r in zip(crossing, own_rows)]
    lenses[0:8, :] = trace[...]
    lenses[8:9, :] = above[1][0:1]
    lenses[9:10, :] = below[1][0:1]
    lenses[10:16, :] = jnp.zeros((6, 128), F32)
    for q in range(4):
        edges[q, pl.ds(0, 8, stride=2), :] = above[0][8 * q:8 * q + 8]
        edges[q, pl.ds(1, 8, stride=2), :] = below[0][8 * q:8 * q + 8]
    half = jnp.concatenate([edges[q, 0:16, :] for q in range(4)], axis=1)
    half = jnp.where(core == 0, half, flipped_columns(half))
    t = half * fading(s)[FROWS:]
    border[...] = t * t * 2.0**-24


def group_fields(ref, utab, spot, whi, wlo, p, flipped, waves=range(4)):
    w, s, y, z, x, core, sign, pair = place_of()
    g = pair if p == 0 else 1 - pair
    turned = -1.0 if flipped else 1.0
    coef = jnp.concatenate(split2(ref[GROUP:MROWS, :]), axis=0)
    both = dot(coef, spot[...])
    coef = both[0:8] + both[8:16]
    down = odd(16 * (8 * g + iota((8, 128), 0)), NP) * (1.0 / 1024.0)
    across = odd(128 * core + iota((8, 128), 1), NP) * (1.0 / 1024.0)
    paths, steps = [], []
    for side in range(2):
        piston, tip, tilt = (coef[:, 256 * c + 128 * side:256 * c + 128 * side + 128] for c in range(3))
        tilt = (sign * turned) * tilt
        paths.append(piston + (across if side == 0 else -across) * tip + tilt * down)
        steps.append(tilt * (1.0 / 512.0))
    for m in waves:
        inverse = 1.0 / wavelength(2 * (w if m < 2 else w ^ 1) + (m & 1))
        im, re = zip(*(sincos(path * (turned * inverse)) for path in paths))
        step_im, step_re = zip(*(sincos(step * (turned * inverse)) for step in steps))
        for r2 in range(8):
            found = [[] for _ in range(4)]
            for h in range(2):
                r0 = 16 * r2 + 8 * h
                for side in range(2):
                    a = ref[MROWS * side + r0:MROWS * side + r0 + 8, :]
                    found[side].append(a * re[side])
                    found[2 + side].append(a * im[side])
                re, im = (
                    [a * p - b * q for a, b, p, q in zip(re, im, step_re, step_im)],
                    [a * q + b * p for a, b, p, q in zip(re, im, step_re, step_im)],
                )
            for k, values in enumerate(found):
                high, low = split2(jnp.concatenate(values, axis=0))
                r0, c0 = GROUP * (k >> 1) + 16 * r2, 128 * (k & 1)
                whi[m, r0:r0 + 16, c0:c0 + 128] = high
                wlo[m, r0:r0 + 16, c0:c0 + 128] = low
    fields = {}
    for m in waves:
        table = utab[p, m]
        both = dot(table, whi[m])
        field = both[:2 * UROWS] + both[2 * UROWS:] + dot(table[:2 * UROWS], wlo[m])
        fields[m] = jnp.concatenate([field[:UROWS], -field[UROWS:]], axis=0) if flipped else field
    return fields


def own_kernel(ref, utab, spot, out, whi, wlo):
    for m, field in group_fields(ref, utab, spot, whi, wlo, 0, False).items():
        out[m] = field


def neighbour_kernel(ref, utab, spot, before, after, out, whi, wlo, *, p, flipped):
    del after
    for m, field in group_fields(ref, utab, spot, whi, wlo, p, flipped).items():
        out[m] = before[m] + field


def last_kernel(ref, utab, spot, before, border, out, whi, wlo, *, waves):
    for m, field in group_fields(ref, utab, spot, whi, wlo, 1, True, waves).items():
        out[2 * UROWS * (m & 1):2 * UROWS * ((m & 1) + 1), :] = before[m] + field
    if 2 in waves:
        for k in range(2):
            out[4 * UROWS + 16 * k:4 * UROWS + 16 * k + 16, :] = border[:, 256 * k:256 * k + 256]


def lens_kernel(keep, got, vtab, weight, border, smat, lenses, mine, other):
    parts = []
    w, s, y, z, x, core, sign, pair = place_of()
    theirs = jnp.concatenate([got[4 * UROWS + 16 * k:4 * UROWS + 16 * k + 16, :] for k in range(2)], axis=1)
    first = core == 0
    borders = jnp.where(first, border[...], theirs), jnp.where(first, theirs, border[...])
    for m in range(2):
        rows = slice(2 * UROWS * m, 2 * UROWS * (m + 1))
        left, right = (
            jnp.concatenate([ref[rows, 128 * q:128 * q + 128] for ref in (keep, got)], axis=1) for q in range(2)
        )
        odd_part = left - right
        sides = left + right, jnp.concatenate([odd_part[UROWS:], -odd_part[:UROWS]], axis=0)
        terms = []
        for q, side in enumerate(sides):
            high, low = split2(side)
            both = dot(jnp.concatenate([high, low], axis=0), vtab[m, q, 0])
            terms.append(both[:2 * UROWS] + both[2 * UROWS:] + dot(high, vtab[m, q, 1]))
        summed = []
        for q, value in enumerate((terms[0] + terms[1], terms[0] - terms[1])):
            re, im = value[:UROWS], value[UROWS:]
            power = re * re + im * im
            edges = power[FROWS:] * borders[q]
            power = power[:FROWS] * weight[:, FHALF * q:FHALF * (q + 1)]
            edges = edges[:8] + edges[8:]
            edges = edges + pltpu.roll(edges, 4, 0)
            edges = edges + pltpu.roll(edges, 2, 0)
            summed.append(jnp.concatenate([sum(power[8 * r:8 * r + 8] for r in range(8)), edges], axis=0))
        parts.extend(split2(jnp.concatenate(summed, axis=1)))
    lens = dot(jnp.concatenate(parts, axis=0), smat[...])
    for m in range(2):
        for k, out in enumerate((mine, other)):
            at = slice(128 * k, 128 * k + 128)
            out[16 * m:16 * m + 16, :] = lens[32 * m:32 * m + 16, at] + lens[32 * m + 16:32 * m + 32, at]
    row, lane = iota((128, 128), 0), iota((128, 128), 1) & 31
    spot = ((lane >= 18) & (lane < 21) & (row == 16 * (lane - 18) + 15)) | ((lane >= 21) & (lane < 24) & (row == 16 * (lane - 21)))
    sides = dot(lenses[...].astype(BF16), spot.astype(BF16))
    for out in (mine, other):
        out[0:16, :] += sides


def pack_kernel(mine, got, *outs):
    w, s, y, z, x, core, sign, pair = place_of()
    lane = iota((16, 128), 1) >> 5
    for k, out in enumerate(outs):
        at = (x + k) & 3
        packed = 0.0
        for c in range(2):
            rows = jnp.where(core == c, mine[...], got[...])
            for m in range(2):
                moved = pltpu.roll(rows[16 * m:16 * m + 16], (32 * (2 * c + m - at)) & 127, 1)
                packed = jnp.where(lane == 2 * c + m, moved, packed)
        out[...] = packed


def order(a):
    return a - 1 if 0 < a < 9 else 8 + a // 9


def detector_kernel(kernel, a0, a1, a2, a3, lenses, out, arrived, base, across, image, sems):
    w, s, y, z, x, core, sign, pair = place_of()
    for k, ref in enumerate((a0, a1, a2, a3)):
        for c in range(4):
            arrived[4 * ((x - k + 4) & 3) + c] = ref[...] if c == 0 else pltpu.roll(ref[...], 128 - 32 * c, 1)
    spot = (iota((128, 640), 0) == (iota((128, 640), 1) >> 5)) & (iota((128, 640), 1) < 18 * DPIX)
    spot = spot.astype(BF16)
    left, own, right = arrived[jnp.maximum(2 * w - 2, 0)], lenses[...], arrived[jnp.minimum(2 * w + 2, WAVES - 1)]
    lane = iota((16, 128), 1)
    tables = []
    for c in range(3):
        tables.append(
            jnp.where(
                lane == 0,
                pltpu.roll(left, 128 - 18 - c, 1),
                jnp.where(lane == 17, pltpu.roll(right, 128 - 4 - c, 1), pltpu.roll(own, 129 - 16 * c if c else 1, 1)),
            )
        )
    parts = list(split2(arrived[...].reshape(WAVES * 16, 128)))
    wide = dot(jnp.concatenate(parts + [jnp.concatenate(tables, axis=0).astype(BF16)], axis=0), spot)
    values, tables = wide[:16 * WAVES] + wide[16 * WAVES:32 * WAVES], wide[32 * WAVES:]
    row, column, count = tables[0:16] * 0.25, tables[16:32], tables[32:48]
    offset = 0.5 * ((iota((16, 640), 1) & 31).astype(F32) - column)
    falling, rising = jnp.exp(-offset), jnp.exp(offset)
    spread = 0.0
    for wave in range(WAVES):
        value = values[16 * wave:16 * wave + 16]
        along = jnp.minimum(falling * math.exp(0.5 * wave), rising * math.exp(-0.5 * wave))
        spread = spread + jnp.where(count > wave, value, 0.0) * along
    within = iota((16, 512), 1) & 31
    moved = [pltpu.roll(spread, 640 - (30 + q), 1)[:, 0:512] for q in range(5)]
    inside = [(within + q - 2 >= 0) & (within + q - 2 < DPIX) for q in range(5)]
    own = [jnp.where(i, v, 0.0) for i, v in zip(inside, moved)]
    beside = [jnp.where(i, 0.0, v) for i, v in zip(inside, moved)]
    for p in range(5):
        weights = [kernel[p:p + 1, q:q + 1] + (1.0 if p == q == 2 else 0.0) for q in range(5)]
        base[p] = sum(v * k for v, k in zip(own, weights))
        base[5 + p] = sum(v * k for q, (v, k) in enumerate(zip(beside, weights)) if q != 2)
    near = row[:, DPIX:DPIX + 512]
    far = jnp.where(within < 2, pltpu.roll(row, 640 - 30, 1)[:, 0:512], pltpu.roll(row, 640 - 34, 1)[:, 0:512])
    for k, value in enumerate((near, -near, far, -far)):
        across[k] = jnp.exp(value)
    sub = iota((8, 128), 0)
    depth = sub.astype(F32) * 0.25
    downs = [jnp.exp(-(depth + 2.0 * t)) for t in range(4)]
    ups = [jnp.exp(depth + 2.0 * t) for t in range(4)]
    copies = []
    for lt in range(4):
        at = slice(128 * lt, 128 * lt + 128)
        state = None
        for a in range(10):
            r = order(a)
            scale = [base[p, r:r + 1, at] for p in range(10)]
            fall, rise, fall_far, rise_far = (across[k, r:r + 1, at] for k in range(4))
            for t in (3,) if a == 0 else (0,) if a == 9 else range(4):
                one = jnp.minimum(downs[t] * fall, ups[t] * rise)
                two = jnp.minimum(downs[t] * fall_far, ups[t] * rise_far)
                h = [one * scale[p] + two * scale[5 + p] for p in range(5)]
                if state is not None:
                    part, h0, h1, h3, h4 = state
                    done = part + pltpu.roll(jnp.where(sub == 0, h[3], h3), 7, 0)
                    done = done + pltpu.roll(jnp.where(sub < 2, h[4], h4), 6, 0)
                    image[lt, 8 * (4 * a + t - 4):8 * (4 * a + t - 4) + 8, :] = done
                    part = h[2] + pltpu.roll(jnp.where(sub >= 6, h0, h[0]), 2, 0)
                    part = part + pltpu.roll(jnp.where(sub == 7, h1, h[1]), 1, 0)
                else:
                    part = h[2]
                state = part, h[0], h[1], h[3], h[4]
        copies.append(pltpu.make_async_copy(image.at[lt, 8:264, :], out.at[:, at], sems.at[lt]))
        copies[-1].start()
    for copy in copies:
        copy.wait()


def call(kernel, outs, in_smem, n_in, scratch=(), tail=(), limit=40, outside=False, aliases=None):
    specs = [pl.BlockSpec(memory_space=pltpu.SMEM)] * in_smem
    specs += [pl.BlockSpec(memory_space=pltpu.VMEM)] * (n_in - in_smem)
    specs[n_in - len(tail):] = tail
    single = not isinstance(outs, (list, tuple))
    vmem = pl.BlockSpec(memory_space=pltpu.VMEM)
    return pl.pallas_call(
        kernel,
        out_shape=outs,
        in_specs=specs,
        out_specs=pl.BlockSpec(memory_space=pl.ANY) if outside else vmem if single else [vmem] * len(outs),
        scratch_shapes=list(scratch),
        input_output_aliases=aliases or {},
        compiler_params=pltpu.CompilerParams(vmem_limit_bytes=limit * 2**20),
        name=getattr(kernel, "func", kernel).__name__,
    )


def shape(*dims, dtype=F32):
    return jax.ShapeDtypeStruct(dims, dtype)


def along_z(k):
    return [(4 * y + z, 4 * y + (z + k) % 4) for y in range(4) for z in range(4)]


def along_y(other):
    return [(4 * y + z, 4 * other[y] + z) for y in range(4) for z in range(4)]


def body(amplitude, seg_map, seg_table, focal_mask, trace_row, trace_col, block_count, crosstalk):
    anywhere = [pl.BlockSpec(memory_space=pl.ANY)]
    piece, up, down, trace = call(
        prepare_kernel,
        [shape(PIECE, 128), shape(PIECE + EDGE, 128), shape(PIECE + EDGE, 128), shape(8, 128)],
        0,
        7,
        [
            pltpu.VMEM((ROWS, NP), F32),
            pltpu.VMEM((16, NP), I32),
            pltpu.VMEM((3, SEGMENTS), I32),
            pltpu.VMEM((3, 8, 16), I32),
            pltpu.VMEM((2, 8, FHALF), F32),
            pltpu.SemaphoreType.DMA((9,)),
        ],
        tail=[pl.BlockSpec(memory_space=pltpu.HBM)] * 7,
    )(*(pltpu.with_memory_space_constraint(v, pltpu.HBM) for v in (amplitude, seg_map, seg_table.T, focal_mask, trace_row, trace_col, block_count)))
    utab, vtab, spot = call(
        table_kernel,
        [shape(2, 4, 4 * UROWS, 256, dtype=BF16), shape(2, 2, 2, HALF, FHALF, dtype=BF16), shape(128, 768, dtype=BF16)],
        0,
        1,
        tail=anywhere,
    )(piece)
    p1 = lax.ppermute(up, "slab", along_z(1))
    p3 = lax.ppermute(down, "slab", along_z(3))
    p2 = lax.ppermute(piece, "slab", along_z(2))
    own, more = call(
        merge_kernel, [shape(2 * MROWS, 128), shape(2 * MROWS + 32, 128)], 0, 5, tail=anywhere
    )(piece, p1, p2, p3, utab)
    partner = lax.ppermute(more, "slab", along_y((3, 2, 1, 0)))
    beside = lax.ppermute(more, "slab", along_y((1, 0, 3, 2)))
    last = lax.ppermute(own, "slab", along_y((2, 3, 0, 1)))
    scratch = [pltpu.VMEM((4, 256, 256), BF16)] * 2
    field = call(own_kernel, shape(4, 2 * UROWS, 256), 0, 3, scratch)(own, utab, spot)
    weight, smat = call(
        weight_kernel,
        [shape(FROWS, NF), shape(NF, 256, dtype=BF16)],
        0,
        2,
        [pltpu.VMEM((8, FROWS + 8, 128), F32)],
        tail=anywhere,
    )(focal_mask, field)
    for group, p, flipped in ((partner, 0, True), (beside, 1, False)):
        kernel = functools.partial(neighbour_kernel, p=p, flipped=flipped)
        field = call(kernel, shape(4, 2 * UROWS, 256), 0, 5, scratch, tail=anywhere)(group, utab, spot, field, smat)
    border, lenses = call(
        border_kernel, [shape(16, FHALF), shape(16, 128)], 0, 5, [pltpu.VMEM((4, 24, 128), F32)]
    )(p1, p3, beside, partner, trace)
    give = call(functools.partial(last_kernel, waves=(2, 3)), shape(4 * UROWS + 32, 256), 0, 5, scratch)(
        last, utab, spot, field, border
    )
    keep = call(functools.partial(last_kernel, waves=(0, 1)), shape(4 * UROWS, 256), 0, 5, scratch, tail=anywhere)(
        last, utab, spot, field, give
    )
    sibling = [(i, i ^ 1) for i in range(NWAV)]
    crossed = lax.ppermute(give, "wav", sibling)
    mine, other = call(lens_kernel, [shape(32, 128)] * 2, 0, 7)(
        keep, crossed, vtab, weight, border, smat, lenses
    )
    got = lax.ppermute(other, "wav", sibling)
    def along_x(sent, k):
        return lax.ppermute(sent, "wav", [(i, (i + 2 * k) % NWAV) for i in range(NWAV)])

    kept, *sent = call(pack_kernel, [shape(16, 128)] * 4, 0, 2)(mine, got)
    arrived = [along_x(sent[k - 1], k) for k in (1, 2, 3)]
    return call(
        detector_kernel,
        shape(256, 512),
        0,
        6,
        [
            pltpu.VMEM((WAVES, 16, 128), F32),
            pltpu.VMEM((10, 16, 512), F32),
            pltpu.VMEM((4, 16, 512), F32),
            pltpu.VMEM((4, 264, 128), F32),
            pltpu.SemaphoreType.DMA((4,)),
        ],
        outside=True,
    )(crosstalk, kept, *arrived, lenses)


def solution(mesh):
    return jax.shard_map(
        body,
        mesh=mesh,
        in_specs=(
            P("slab", None),
            P("slab", None),
            P(),
            P("slab", None),
            P("slab", "wav"),
            P("slab", "wav"),
            P("slab", "wav"),
            P(),
        ),
        out_specs=P("slab", "wav"),
        check_vma=False,
    )
```

```python
import functools
import math

import jax
import jax.numpy as jnp
import numpy as np
from jax import lax
from jax.experimental import pallas as pl
from jax.experimental.pallas import tpu as pltpu
from jax.sharding import PartitionSpec as P

F32, BF16, I32 = jnp.float32, jnp.bfloat16, jnp.int32

NP, NF, NL, DPIX, SEGMENTS, WAVES = 512, 1024, 128, 32, 798, 16
NWAV, NSLAB = 8, 16
ROWS = NP // NSLAB
FROWS = NF // NSLAB
UROWS = FROWS + 16
GROUP = 128
PIECE, EDGE = 2 * (ROWS + 8), 40
MROWS = GROUP + 8
HALF, FHALF = NP // 2, NF // 2

SIN = (6.283184916495428, -41.34158923268831, 81.59994332977429, -76.61447253115396, 41.34288235413569, -12.471243534350362)
COS = (0.9999999890590228, -19.73920449945383, 64.93911745989081, -85.45013953079767,
       60.167630950263465, -25.967599245923743, 6.52865815775625)


def place_of():
    w, s = lax.axis_index("wav").astype(I32), lax.axis_index("slab").astype(I32)
    y = s >> 2
    return w, s, y, s & 3, w >> 1, w & 1, jnp.where(y < 2, 1.0, -1.0), jnp.where((y == 0) | (y == 3), 0, 1)


def iota(shape, dim):
    return lax.broadcasted_iota(I32, shape, dim)


def dot(a, b):
    return jnp.dot(a, b, preferred_element_type=F32)


def split2(x):
    high = x.astype(BF16)
    return high, (x - high.astype(F32)).astype(BF16)


def split3(x):
    high = x.astype(BF16)
    rest = x - high.astype(F32)
    middle = rest.astype(BF16)
    return high, middle, (rest - middle.astype(F32)).astype(BF16)


def sincos(turns):
    t = turns - jnp.round(turns)
    z = t * t
    s, c = SIN[-1], COS[-1]
    for a in SIN[-2::-1]:
        s = s * z + a
    for b in COS[-2::-1]:
        c = c * z + b
    return s * t, c


def focal_row(s, shape):
    a = iota(shape, 0)
    r = (a - FROWS) >> 1
    own = 8 * (a & 7) + (a >> 3)
    return FROWS * s + jnp.where(a < FROWS, own, jnp.where((a & 1) == 0, r - 8, FROWS + r))


def reversal(n):
    return (iota((n, n), 0) + iota((n, n), 1) == n - 1).astype(BF16)


def prepare_kernel(amp_in, seg_in, tab_in, mask, trow, tcol, count, out, up, down, trace, amp, seg, tab, tables, edges, sems):
    w, s, y, z, x, core, sign, pair = place_of()
    half = pl.ds(pl.multiple_of(FHALF * core, FHALF), FHALF)
    copies = [
        pltpu.make_async_copy(a, b, sems.at[k])
        for k, (a, b) in enumerate(
            (
                (tab_in, tab),
                (seg_in.at[0:8, :], seg.at[0:8, :]),
                (seg_in.at[16:24, :], seg.at[8:16, :]),
                (amp_in, amp),
                (trow, tables.at[0]),
                (tcol, tables.at[1]),
                (count, tables.at[2]),
                (mask.at[FROWS - 8:FROWS, half], edges.at[0]),
                (mask.at[0:8, half], edges.at[1]),
            )
        )
    ]
    for copy in copies:
        copy.start()
    lower = y >= 2
    rows, cols = iota((ROWS, ROWS), 0), iota((ROWS, ROWS), 1)
    turned = (cols == jnp.where(lower, ROWS - 1 - rows, rows)).astype(BF16)
    rev = reversal(128)
    lane = iota((NP, 128), 1)
    pick = ((iota((NP, 128), 0) == 16 * (lane & 31)) & (lane < 96)).astype(BF16)
    out[...] = jnp.zeros((PIECE, 128), F32)
    for ref in (up, down):
        ref[PIECE + 32:PIECE + EDGE, :] = jnp.zeros((8, 128), F32)
    trace[...] = jnp.zeros((8, 128), F32)
    for copy in copies:
        copy.wait()
    for c in range(3):
        table = tables[c].astype(F32)
        trace[:, 16 * c:16 * c + 16] = table
        up[PIECE + 32:PIECE + 33, 16 * c:16 * c + 16] = table[7:8]
        down[PIECE + 32:PIECE + 33, 16 * c:16 * c + 16] = table[0:1]
    ids = dot(jnp.concatenate(split2(seg[...].astype(F32)), axis=0), pick)
    ids = ids[0:16] + ids[16:32]
    upper_ids, lower_ids = ids[0:1], ids[8:9]
    ids = jnp.concatenate(
        [jnp.where(lower, lower_ids, upper_ids), jnp.where(lower, upper_ids, lower_ids)], axis=1
    )
    which = iota((SEGMENTS, 256), 0).astype(F32)
    table = jnp.concatenate([tab[...].astype(F32), jnp.zeros((5, SEGMENTS), F32)], axis=0)
    found = dot(jnp.concatenate(split2(table), axis=0), (which == ids).astype(BF16))
    found = found[0:3] + found[8:11]
    found = jnp.sum(jnp.where(iota((3, 256), 0) == (iota((3, 256), 1) & 127) >> 5, found, 0.0), axis=0, keepdims=True)
    for k in range(2):
        out[ROWS + k:ROWS + k + 1, :] = found[:, 128 * k:128 * k + 128]
    first = core == 0
    left = jnp.where(first, amp[:, 0:128], amp[:, 128:256])
    right = jnp.where(first, amp[:, 384:512], amp[:, 256:384])
    right = dot(jnp.concatenate(split3(right), axis=0), rev).astype(BF16)
    parts = list(split3(left)) + [right[ROWS * k:ROWS * k + ROWS] for k in range(3)]
    found = dot(turned, jnp.concatenate(parts, axis=1))
    for k in range(2):
        out[(ROWS + 8) * k:(ROWS + 8) * k + ROWS, :] = sum(found[:, 128 * q:128 * q + 128] for q in range(3 * k, 3 * k + 3))
    for k, ref in enumerate((up, down)):
        ref[0:PIECE, :] = out[...]
        for q in range(4):
            ref[PIECE + 8 * q:PIECE + 8 * q + 8, :] = edges[k, :, 128 * q:128 * q + 128]


def place_pieces(out, pieces):
    w, s, y, z, x, core, sign, pair = place_of()
    for k, piece in pieces:
        source = lax.rem(z - k + 4, 4)
        place = jnp.where(y >= 2, 3 - source, source)
        for at in range(4):

            @pl.when(place == at)
            def _(at=at, piece=piece):
                for t in range(2):
                    for b in range(2):
                        r0 = (ROWS + 8) * t + 16 * b
                        out[pl.ds(MROWS * t + 2 * at + b, 16, stride=8), :] = piece[r0:r0 + 16, :]
                out[GROUP + 2 * at:GROUP + 2 * at + 2, :] = piece[ROWS:ROWS + 2, :]


def merge_kernel(p0, p1, p2, p3, after, out, more):
    del after
    out[GROUP:MROWS, :] = jnp.zeros((8, 128), F32)
    out[MROWS + GROUP:2 * MROWS, :] = jnp.zeros((8, 128), F32)
    w, s, y, z, x, core, sign, pair = place_of()
    place_pieces(out, enumerate((p0, p1, p2, p3)))
    more[0:2 * MROWS, :] = out[...]
    wrap = jnp.where(z == 0, p1[PIECE:PIECE + EDGE, :], p3[PIECE:PIECE + EDGE, :])
    more[2 * MROWS:2 * MROWS + 32, :] = wrap[0:32]
    more[MROWS + GROUP:2 * MROWS, :] = wrap[32:EDGE]


def wavelength(w):
    return jnp.full((1, 1), 1000 + w, I32).astype(F32)


def slope(n, w):
    lam = wavelength(w)
    short = jnp.round(250.0 / lam * 2.0**14) * 2.0**-14
    rest = (250.0 - short * lam) / lam
    whole = n * (short * 2.0**-10)
    high = jnp.round(whole * 2.0**13) * 2.0**-13
    return high, (whole - high) + n * (rest * 2.0**-10)


def angle(m, step):
    t = m * step[0]
    t = t - jnp.round(t)
    return sincos(t + m * step[1])


def odd(index, count):
    return (2 * index + 1 - count).astype(F32)


def table_kernel(after, utab, vtab, spot):
    del after
    w, s, y, z, x, core, sign, pair = place_of()
    row, lane = iota((128, 768), 0), iota((128, 768), 1)
    block = 8 * core + ((lane & 127) >> 4)
    spot[...] = (row == 32 * (lane >> 8) + jnp.where((lane & 128) == 0, block, 31 - block)).astype(BF16)
    m = odd(focal_row(s, (UROWS, GROUP)), NF)
    rho = iota((1, GROUP), 1)
    for k in range(4):
        wave = 2 * (w if k < 2 else w ^ 1) + (k & 1)
        for p in range(2):
            g = pair if p == 0 else 1 - pair
            sin, cos = angle(m, slope(odd(128 * g + 16 * (rho & 7) + (rho >> 3), NP), wave))
            sin = sin * sign
            for r0, at, part in ((0, 0, cos), (0, GROUP, sin), (UROWS, 0, -sin), (UROWS, GROUP, cos)):
                high, low = split2(part)
                utab[p, k, r0:r0 + UROWS, at:at + GROUP] = high
                utab[p, k, r0 + 2 * UROWS:r0 + 3 * UROWS, at:at + GROUP] = low
    m = odd(iota((16, 128), 1), NF)
    for k in range(2):

        def chunk(c, carry, k=k):
            j0 = pl.multiple_of(16 * c, 16)
            step = slope(odd(((j0 + 128 * core) & 255) + iota((16, 128), 0), NP), 2 * w + k)
            sin, cos = angle(m, step)
            turn_im, turn_re = angle(jnp.full((16, 128), 256.0, F32), step)
            for t in range(4):
                for q, part in ((0, cos), (1, sin)):
                    high, low = split2(part)
                    vtab[k, q, 0, pl.ds(j0, 16), 128 * t:128 * t + 128] = high
                    vtab[k, q, 1, pl.ds(j0, 16), 128 * t:128 * t + 128] = low
                cos, sin = cos * turn_re - sin * turn_im, cos * turn_im + sin * turn_re
            return carry

        lax.fori_loop(0, HALF // 16, chunk, 0)


def flipped_columns(x):
    rev = reversal(256)
    n = x.shape[1] // 256
    parts = [jnp.concatenate(split3(x[:, 256 * q:256 * q + 256]), axis=0) for q in range(n)]
    rows, found = x.shape[0], [dot(part, rev) for part in reversed(parts)]
    return jnp.concatenate([f[:rows] + f[rows:2 * rows] + f[2 * rows:] for f in found], axis=1)


def fading(s):
    down, across = odd(focal_row(s, (UROWS, FHALF)), NF) * 0.5, odd(iota((UROWS, FHALF), 1), NF) * 0.5
    return 1.0 - jnp.exp((down * down + across * across) * (-1.0 / 1024.0))


def weight_kernel(mask, after, weight, smat, full):
    del after
    w, s, y, z, x, core, sign, pair = place_of()
    fade = fading(s)
    for q in range(8):
        for a in range(8):
            full[q, pl.ds(a, 8, stride=8), :] = mask[8 * a:8 * a + 8, 128 * q:128 * q + 128]
    left, right = (jnp.concatenate([full[4 * k + q, 0:FROWS, :] for q in range(4)], axis=1) for k in range(2))
    for k, part in enumerate((left, flipped_columns(right))):
        t = part * fade[:FROWS]
        weight[:, FHALF * k:FHALF * (k + 1)] = t * t * 2.0**-24
    row, lane = iota((FHALF, 256), 0), iota((FHALF, 256), 1)
    column = 2 * ((lane >> 5) & 3) + jnp.where(lane < 128, core, 1 - core)
    lens = jnp.where((lane & 31) < 18, 16 * column - 1 + (lane & 31), -1)
    smat[0:FHALF, :] = (lens == row >> 3).astype(BF16)
    smat[FHALF:NF, :] = (lens == NL - 1 - (row >> 3)).astype(BF16)


def border_kernel(p1, p3, beside, partner, trace, border, lenses, edges):
    w, s, y, z, x, core, sign, pair = place_of()
    rows, row = slice(2 * MROWS, 2 * MROWS + 32), slice(MROWS + GROUP, 2 * MROWS)
    inner, outer = jnp.where(z == 0, y == 2, y == 1), jnp.where(z == 0, y == 0, y == 3)
    crossing = [jnp.where(outer, 0.0, jnp.where(inner, partner[r, :], beside[r, :])) for r in (rows, row)]
    own_rows = slice(PIECE, PIECE + 32), slice(PIECE + 32, PIECE + EDGE)
    above = [jnp.where(z == 0, c, p1[r, :]) for c, r in zip(crossing, own_rows)]
    below = [jnp.where(z == 3, c, p3[r, :]) for c, r in zip(crossing, own_rows)]
    lenses[0:8, :] = trace[...]
    lenses[8:9, :] = above[1][0:1]
    lenses[9:10, :] = below[1][0:1]
    lenses[10:16, :] = jnp.zeros((6, 128), F32)
    for q in range(4):
        edges[q, pl.ds(0, 8, stride=2), :] = above[0][8 * q:8 * q + 8]
        edges[q, pl.ds(1, 8, stride=2), :] = below[0][8 * q:8 * q + 8]
    half = jnp.concatenate([edges[q, 0:16, :] for q in range(4)], axis=1)
    half = jnp.where(core == 0, half, flipped_columns(half))
    t = half * fading(s)[FROWS:]
    border[...] = t * t * 2.0**-24


def group_fields(ref, utab, spot, whi, wlo, p, flipped, waves=range(4)):
    w, s, y, z, x, core, sign, pair = place_of()
    g = pair if p == 0 else 1 - pair
    turned = -1.0 if flipped else 1.0
    coef = jnp.concatenate(split2(ref[GROUP:MROWS, :]), axis=0)
    both = dot(coef, spot[...])
    coef = both[0:8] + both[8:16]
    down = odd(16 * (8 * g + iota((8, 128), 0)), NP) * (1.0 / 1024.0)
    across = odd(128 * core + iota((8, 128), 1), NP) * (1.0 / 1024.0)
    paths, steps = [], []
    for side in range(2):
        piston, tip, tilt = (coef[:, 256 * c + 128 * side:256 * c + 128 * side + 128] for c in range(3))
        tilt = (sign * turned) * tilt
        paths.append(piston + (across if side == 0 else -across) * tip + tilt * down)
        steps.append(tilt * (1.0 / 512.0))
    for m in waves:
        inverse = 1.0 / wavelength(2 * (w if m < 2 else w ^ 1) + (m & 1))
        im, re = zip(*(sincos(path * (turned * inverse)) for path in paths))
        step_im, step_re = zip(*(sincos(step * (turned * inverse)) for step in steps))
        for r2 in range(8):
            found = [[] for _ in range(4)]
            for h in range(2):
                r0 = 16 * r2 + 8 * h
                for side in range(2):
                    a = ref[MROWS * side + r0:MROWS * side + r0 + 8, :]
                    found[side].append(a * re[side])
                    found[2 + side].append(a * im[side])
                re, im = (
                    [a * p - b * q for a, b, p, q in zip(re, im, step_re, step_im)],
                    [a * q + b * p for a, b, p, q in zip(re, im, step_re, step_im)],
                )
            for k, values in enumerate(found):
                high, low = split2(jnp.concatenate(values, axis=0))
                r0, c0 = GROUP * (k >> 1) + 16 * r2, 128 * (k & 1)
                whi[m, r0:r0 + 16, c0:c0 + 128] = high
                wlo[m, r0:r0 + 16, c0:c0 + 128] = low
    fields = {}
    for m in waves:
        table = utab[p, m]
        both = dot(table, whi[m])
        field = both[:2 * UROWS] + both[2 * UROWS:] + dot(table[:2 * UROWS], wlo[m])
        fields[m] = jnp.concatenate([field[:UROWS], -field[UROWS:]], axis=0) if flipped else field
    return fields


def own_kernel(ref, utab, spot, out, whi, wlo):
    for m, field in group_fields(ref, utab, spot, whi, wlo, 0, False).items():
        out[m] = field


def neighbour_kernel(ref, utab, spot, before, after, out, whi, wlo, *, p, flipped):
    del after
    for m, field in group_fields(ref, utab, spot, whi, wlo, p, flipped).items():
        out[m] = before[m] + field


def last_kernel(ref, utab, spot, before, border, out, whi, wlo, *, waves):
    for m, field in group_fields(ref, utab, spot, whi, wlo, 1, True, waves).items():
        out[2 * UROWS * (m & 1):2 * UROWS * ((m & 1) + 1), :] = before[m] + field
    if 2 in waves:
        for k in range(2):
            out[4 * UROWS + 16 * k:4 * UROWS + 16 * k + 16, :] = border[:, 256 * k:256 * k + 256]


def lens_kernel(keep, got, vtab, weight, border, smat, lenses, mine, other):
    parts = []
    w, s, y, z, x, core, sign, pair = place_of()
    theirs = jnp.concatenate([got[4 * UROWS + 16 * k:4 * UROWS + 16 * k + 16, :] for k in range(2)], axis=1)
    first = core == 0
    borders = jnp.where(first, border[...], theirs), jnp.where(first, theirs, border[...])
    for m in range(2):
        rows = slice(2 * UROWS * m, 2 * UROWS * (m + 1))
        left, right = (
            jnp.concatenate([ref[rows, 128 * q:128 * q + 128] for ref in (keep, got)], axis=1) for q in range(2)
        )
        odd_part = left - right
        sides = left + right, jnp.concatenate([odd_part[UROWS:], -odd_part[:UROWS]], axis=0)
        terms = []
        for q, side in enumerate(sides):
            high, low = split2(side)
            both = dot(jnp.concatenate([high, low], axis=0), vtab[m, q, 0])
            terms.append(both[:2 * UROWS] + both[2 * UROWS:] + dot(high, vtab[m, q, 1]))
        summed = []
        for q, value in enumerate((terms[0] + terms[1], terms[0] - terms[1])):
            re, im = value[:UROWS], value[UROWS:]
            power = re * re + im * im
            edges = power[FROWS:] * borders[q]
            power = power[:FROWS] * weight[:, FHALF * q:FHALF * (q + 1)]
            edges = edges[:8] + edges[8:]
            edges = edges + pltpu.roll(edges, 4, 0)
            edges = edges + pltpu.roll(edges, 2, 0)
            summed.append(jnp.concatenate([sum(power[8 * r:8 * r + 8] for r in range(8)), edges], axis=0))
        parts.extend(split2(jnp.concatenate(summed, axis=1)))
    lens = dot(jnp.concatenate(parts, axis=0), smat[...])
    for m in range(2):
        for k, out in enumerate((mine, other)):
            at = slice(128 * k, 128 * k + 128)
            out[16 * m:16 * m + 16, :] = lens[32 * m:32 * m + 16, at] + lens[32 * m + 16:32 * m + 32, at]
    row, lane = iota((128, 128), 0), iota((128, 128), 1) & 31
    spot = ((lane >= 18) & (lane < 21) & (row == 16 * (lane - 18) + 15)) | ((lane >= 21) & (lane < 24) & (row == 16 * (lane - 21)))
    sides = dot(lenses[...].astype(BF16), spot.astype(BF16))
    for out in (mine, other):
        out[0:16, :] += sides


def pack_kernel(mine, got, *outs):
    w, s, y, z, x, core, sign, pair = place_of()
    lane = iota((16, 128), 1) >> 5
    for k, out in enumerate(outs):
        at = (x + k) & 3
        packed = 0.0
        for c in range(2):
            rows = jnp.where(core == c, mine[...], got[...])
            for m in range(2):
                moved = pltpu.roll(rows[16 * m:16 * m + 16], (32 * (2 * c + m - at)) & 127, 1)
                packed = jnp.where(lane == 2 * c + m, moved, packed)
        out[...] = packed


def order(a):
    return a - 1 if 0 < a < 9 else 8 + a // 9


def detector_kernel(kernel, a0, a1, a2, a3, lenses, out, arrived, base, across, image, sems):
    w, s, y, z, x, core, sign, pair = place_of()
    for k, ref in enumerate((a0, a1, a2, a3)):
        for c in range(4):
            arrived[4 * ((x - k + 4) & 3) + c] = ref[...] if c == 0 else pltpu.roll(ref[...], 128 - 32 * c, 1)
    spot = (iota((128, 640), 0) == (iota((128, 640), 1) >> 5)) & (iota((128, 640), 1) < 18 * DPIX)
    spot = spot.astype(BF16)
    left, own, right = arrived[jnp.maximum(2 * w - 2, 0)], lenses[...], arrived[jnp.minimum(2 * w + 2, WAVES - 1)]
    lane = iota((16, 128), 1)
    tables = []
    for c in range(3):
        tables.append(
            jnp.where(
                lane == 0,
                pltpu.roll(left, 128 - 18 - c, 1),
                jnp.where(lane == 17, pltpu.roll(right, 128 - 4 - c, 1), pltpu.roll(own, 129 - 16 * c if c else 1, 1)),
            )
        )
    parts = list(split2(arrived[...].reshape(WAVES * 16, 128)))
    wide = dot(jnp.concatenate(parts + [jnp.concatenate(tables, axis=0).astype(BF16)], axis=0), spot)
    values, tables = wide[:16 * WAVES] + wide[16 * WAVES:32 * WAVES], wide[32 * WAVES:]
    row, column, count = tables[0:16] * 0.25, tables[16:32], tables[32:48]
    offset = 0.5 * ((iota((16, 640), 1) & 31).astype(F32) - column)
    falling, rising = jnp.exp(-offset), jnp.exp(offset)
    spread = 0.0
    for wave in range(WAVES):
        value = values[16 * wave:16 * wave + 16]
        along = jnp.minimum(falling * math.exp(0.5 * wave), rising * math.exp(-0.5 * wave))
        spread = spread + jnp.where(count > wave, value, 0.0) * along
    within = iota((16, 512), 1) & 31
    moved = [pltpu.roll(spread, 640 - (30 + q), 1)[:, 0:512] for q in range(5)]
    inside = [(within + q - 2 >= 0) & (within + q - 2 < DPIX) for q in range(5)]
    own = [jnp.where(i, v, 0.0) for i, v in zip(inside, moved)]
    beside = [jnp.where(i, 0.0, v) for i, v in zip(inside, moved)]
    for p in range(5):
        weights = [kernel[p:p + 1, q:q + 1] + (1.0 if p == q == 2 else 0.0) for q in range(5)]
        base[p] = sum(v * k for v, k in zip(own, weights))
        base[5 + p] = sum(v * k for q, (v, k) in enumerate(zip(beside, weights)) if q != 2)
    near = row[:, DPIX:DPIX + 512]
    far = jnp.where(within < 2, pltpu.roll(row, 640 - 30, 1)[:, 0:512], pltpu.roll(row, 640 - 34, 1)[:, 0:512])
    for k, value in enumerate((near, -near, far, -far)):
        across[k] = jnp.exp(value)
    sub = iota((8, 128), 0)
    depth = sub.astype(F32) * 0.25
    downs = [jnp.exp(-(depth + 2.0 * t)) for t in range(4)]
    ups = [jnp.exp(depth + 2.0 * t) for t in range(4)]
    copies = []
    for lt in range(4):
        at = slice(128 * lt, 128 * lt + 128)
        state = None
        for a in range(10):
            r = order(a)
            scale = [base[p, r:r + 1, at] for p in range(10)]
            fall, rise, fall_far, rise_far = (across[k, r:r + 1, at] for k in range(4))
            for t in (3,) if a == 0 else (0,) if a == 9 else range(4):
                one = jnp.minimum(downs[t] * fall, ups[t] * rise)
                two = jnp.minimum(downs[t] * fall_far, ups[t] * rise_far)
                h = [one * scale[p] + two * scale[5 + p] for p in range(5)]
                if state is not None:
                    part, h0, h1, h3, h4 = state
                    done = part + pltpu.roll(jnp.where(sub == 0, h[3], h3), 7, 0)
                    done = done + pltpu.roll(jnp.where(sub < 2, h[4], h4), 6, 0)
                    image[lt, 8 * (4 * a + t - 4):8 * (4 * a + t - 4) + 8, :] = done
                    part = h[2] + pltpu.roll(jnp.where(sub >= 6, h0, h[0]), 2, 0)
                    part = part + pltpu.roll(jnp.where(sub == 7, h1, h[1]), 1, 0)
                else:
                    part = h[2]
                state = part, h[0], h[1], h[3], h[4]
            if a in (5, 9):
                rows = (0, 152) if a == 5 else (152, 256)
                source, place = image.at[lt, rows[0] + 8:rows[1] + 8, :], out.at[rows[0]:rows[1], at]
                copies.append(pltpu.make_async_copy(source, place, sems.at[len(copies)]))
                copies[-1].start()
    for copy in copies:
        copy.wait()


def call(kernel, outs, in_smem, n_in, scratch=(), tail=(), limit=40, outside=False, aliases=None):
    specs = [pl.BlockSpec(memory_space=pltpu.SMEM)] * in_smem
    specs += [pl.BlockSpec(memory_space=pltpu.VMEM)] * (n_in - in_smem)
    specs[n_in - len(tail):] = tail
    single = not isinstance(outs, (list, tuple))
    vmem = pl.BlockSpec(memory_space=pltpu.VMEM)
    return pl.pallas_call(
        kernel,
        out_shape=outs,
        in_specs=specs,
        out_specs=pl.BlockSpec(memory_space=pl.ANY) if outside else vmem if single else [vmem] * len(outs),
        scratch_shapes=list(scratch),
        input_output_aliases=aliases or {},
        compiler_params=pltpu.CompilerParams(vmem_limit_bytes=limit * 2**20),
        name=getattr(kernel, "func", kernel).__name__,
    )


def shape(*dims, dtype=F32):
    return jax.ShapeDtypeStruct(dims, dtype)


def along_z(k):
    return [(4 * y + z, 4 * y + (z + k) % 4) for y in range(4) for z in range(4)]


def along_y(other):
    return [(4 * y + z, 4 * other[y] + z) for y in range(4) for z in range(4)]


def body(amplitude, seg_map, seg_table, focal_mask, trace_row, trace_col, block_count, crosstalk):
    anywhere = [pl.BlockSpec(memory_space=pl.ANY)]
    piece, up, down, trace = call(
        prepare_kernel,
        [shape(PIECE, 128), shape(PIECE + EDGE, 128), shape(PIECE + EDGE, 128), shape(8, 128)],
        0,
        7,
        [
            pltpu.VMEM((ROWS, NP), F32),
            pltpu.VMEM((16, NP), I32),
            pltpu.VMEM((3, SEGMENTS), I32),
            pltpu.VMEM((3, 8, 16), I32),
            pltpu.VMEM((2, 8, FHALF), F32),
            pltpu.SemaphoreType.DMA((9,)),
        ],
        tail=[pl.BlockSpec(memory_space=pltpu.HBM)] * 7,
    )(*(pltpu.with_memory_space_constraint(v, pltpu.HBM) for v in (amplitude, seg_map, seg_table.T, focal_mask, trace_row, trace_col, block_count)))
    utab, vtab, spot = call(
        table_kernel,
        [shape(2, 4, 4 * UROWS, 256, dtype=BF16), shape(2, 2, 2, HALF, FHALF, dtype=BF16), shape(128, 768, dtype=BF16)],
        0,
        1,
        tail=anywhere,
    )(piece)
    p1 = lax.ppermute(up, "slab", along_z(1))
    p3 = lax.ppermute(down, "slab", along_z(3))
    p2 = lax.ppermute(piece, "slab", along_z(2))
    own, more = call(
        merge_kernel, [shape(2 * MROWS, 128), shape(2 * MROWS + 32, 128)], 0, 5, tail=anywhere
    )(piece, p1, p2, p3, utab)
    partner = lax.ppermute(more, "slab", along_y((3, 2, 1, 0)))
    beside = lax.ppermute(more, "slab", along_y((1, 0, 3, 2)))
    last = lax.ppermute(own, "slab", along_y((2, 3, 0, 1)))
    scratch = [pltpu.VMEM((4, 256, 256), BF16)] * 2
    field = call(own_kernel, shape(4, 2 * UROWS, 256), 0, 3, scratch)(own, utab, spot)
    weight, smat = call(
        weight_kernel,
        [shape(FROWS, NF), shape(NF, 256, dtype=BF16)],
        0,
        2,
        [pltpu.VMEM((8, FROWS + 8, 128), F32)],
        tail=anywhere,
    )(focal_mask, field)
    for group, p, flipped in ((partner, 0, True), (beside, 1, False)):
        kernel = functools.partial(neighbour_kernel, p=p, flipped=flipped)
        field = call(kernel, shape(4, 2 * UROWS, 256), 0, 5, scratch, tail=anywhere)(group, utab, spot, field, smat)
    border, lenses = call(
        border_kernel, [shape(16, FHALF), shape(16, 128)], 0, 5, [pltpu.VMEM((4, 24, 128), F32)]
    )(p1, p3, beside, partner, trace)
    give = call(functools.partial(last_kernel, waves=(2, 3)), shape(4 * UROWS + 32, 256), 0, 5, scratch)(
        last, utab, spot, field, border
    )
    keep = call(functools.partial(last_kernel, waves=(0, 1)), shape(4 * UROWS, 256), 0, 5, scratch, tail=anywhere)(
        last, utab, spot, field, give
    )
    sibling = [(i, i ^ 1) for i in range(NWAV)]
    crossed = lax.ppermute(give, "wav", sibling)
    mine, other = call(lens_kernel, [shape(32, 128)] * 2, 0, 7)(
        keep, crossed, vtab, weight, border, smat, lenses
    )
    got = lax.ppermute(other, "wav", sibling)
    def along_x(sent, k):
        return lax.ppermute(sent, "wav", [(i, (i + 2 * k) % NWAV) for i in range(NWAV)])

    kept, *sent = call(pack_kernel, [shape(16, 128)] * 4, 0, 2)(mine, got)
    arrived = [along_x(sent[k - 1], k) for k in (1, 2, 3)]
    return call(
        detector_kernel,
        shape(256, 512),
        0,
        6,
        [
            pltpu.VMEM((WAVES, 16, 128), F32),
            pltpu.VMEM((10, 16, 512), F32),
            pltpu.VMEM((4, 16, 512), F32),
            pltpu.VMEM((4, 264, 128), F32),
            pltpu.SemaphoreType.DMA((8,)),
        ],
        outside=True,
    )(crosstalk, kept, *arrived, lenses)


def solution(mesh):
    return jax.shard_map(
        body,
        mesh=mesh,
        in_specs=(
            P("slab", None),
            P("slab", None),
            P(),
            P("slab", None),
            P("slab", "wav"),
            P("slab", "wav"),
            P("slab", "wav"),
            P(),
        ),
        out_specs=P("slab", "wav"),
        check_vma=False,
    )
```
